32 devices in a mesh: dp: 8 (over y, x, core), mp: 4 (over z).
Axes of the slice: x: 2, y: 2, z: 4, core: 2. Of those that a mesh axis runs over, the one named last changes fastest.
Arguments:
- inputs: float32 [8192, 768], P(('dp', 'mp')), may hold values from -6 to 6
- cotangent: float32 [8192, 768], P(('dp', 'mp')), may hold values from -6 to 6
- mask_bits: int32 [8192], P(('dp', 'mp')), may hold values from 0 to 1, as said below
- frame_pregain: float32 [768], P(('dp', 'mp')), may hold values from 0.5 to 1.5
- frame_prebias: float32 [768], P(('dp', 'mp')), may hold values from -1.75 to 1.75
- frame_inweight: float32 [768, 3, 768], P('dp', None, 'mp'), may hold values from -0.21875 to 0.21875
- frame_inbias: float32 [2, 768], P(None, ('mp', 'dp')), may hold values from -1.75 to 1.75
- frame_outweight: float32 [768, 768], P('mp', 'dp'), may hold values from -0.875 to 0.875
- frame_outbias: float32 [768], P(('dp', 'mp')), may hold values from -1.75 to 1.75
- frame_midgain: float32 [768], P(('dp', 'mp')), may hold values from 0.5 to 1.5
- frame_midbias: float32 [768], P(('dp', 'mp')), may hold values from -1.75 to 1.75
- frame_upweight: float32 [768, 3072], P('dp', 'mp'), may hold values from -0.21875 to 0.21875
- frame_upbias: float32 [3072], P(('mp', 'dp')), may hold values from -1.75 to 1.75
- frame_downweight: float32 [3072, 768], P('mp', 'dp'), may hold values from -0.109375 to 0.109375
- frame_downbias: float32 [768], P(('dp', 'mp')), may hold values from -1.75 to 1.75
- tube_pregain: float32 [768], P(('dp', 'mp')), may hold values from 0.5 to 1.5
- tube_prebias: float32 [768], P(('dp', 'mp')), may hold values from -1.75 to 1.75
- tube_inweight: float32 [768, 3, 768], P('dp', None, 'mp'), may hold values from -0.21875 to 0.21875
- tube_inbias: float32 [2, 768], P(None, ('mp', 'dp')), may hold values from -1.75 to 1.75
- tube_outweight: float32 [768, 768], P('mp', 'dp'), may hold values from -0.875 to 0.875
- tube_outbias: float32 [768], P(('dp', 'mp')), may hold values from -1.75 to 1.75
- tube_midgain: float32 [768], P(('dp', 'mp')), may hold values from 0.5 to 1.5
- tube_midbias: float32 [768], P(('dp', 'mp')), may hold values from -1.75 to 1.75
- tube_upweight: float32 [768, 3072], P('dp', 'mp'), may hold values from -0.21875 to 0.21875
- tube_upbias: float32 [3072], P(('mp', 'dp')), may hold values from -1.75 to 1.75
- tube_downweight: float32 [3072, 768], P('mp', 'dp'), may hold values from -0.109375 to 0.109375
- tube_downbias: float32 [768], P(('dp', 'mp')), may hold values from -1.75 to 1.75
Outputs:
- outputs: float32 [8192, 768], P(('dp', 'mp'))
- input_grad: float32 [8192, 768], P(('dp', 'mp'))
- frame_pregain_grad: float32 [768], P(('dp', 'mp'))
- frame_prebias_grad: float32 [768], P(('dp', 'mp'))
- frame_inweight_grad: float32 [768, 3, 768], P('dp', None, 'mp')
- frame_inbias_grad: float32 [2, 768], P(None, ('mp', 'dp'))
- frame_outweight_grad: float32 [768, 768], P('mp', 'dp')
- frame_outbias_grad: float32 [768], P(('dp', 'mp'))
- frame_midgain_grad: float32 [768], P(('dp', 'mp'))
- frame_midbias_grad: float32 [768], P(('dp', 'mp'))
- frame_upweight_grad: float32 [768, 3072], P('dp', 'mp')
- frame_upbias_grad: float32 [3072], P(('mp', 'dp'))
- frame_downweight_grad: float32 [3072, 768], P('mp', 'dp')
- frame_downbias_grad: float32 [768], P(('dp', 'mp'))
- tube_pregain_grad: float32 [768], P(('dp', 'mp'))
- tube_prebias_grad: float32 [768], P(('dp', 'mp'))
- tube_inweight_grad: float32 [768, 3, 768], P('dp', None, 'mp')
- tube_inbias_grad: float32 [2, 768], P(None, ('mp', 'dp'))
- tube_outweight_grad: float32 [768, 768], P('mp', 'dp')
- tube_outbias_grad: float32 [768], P(('dp', 'mp'))
- tube_midgain_grad: float32 [768], P(('dp', 'mp'))
- tube_midbias_grad: float32 [768], P(('dp', 'mp'))
- tube_upweight_grad: float32 [768, 3072], P('dp', 'mp')
- tube_upbias_grad: float32 [3072], P(('mp', 'dp'))
- tube_downweight_grad: float32 [3072, 768], P('mp', 'dp')
- tube_downbias_grad: float32 [768], P(('dp', 'mp'))
The draws below stay inside these ranges and needn't reach their ends.
Inputs may be any that keep to these rules, and one draw needn't show every extreme that they name: mask_bits is 0 or 1; each clip of 4096 tokens has its own masking probability, between one half and one.
All inputs are finite; a program needn't handle non-finite values.
Results may differ from the reference program's by a relative error of at most 0.02.
Values may be sent and summed in bfloat16 or wider, within the bound.
A program may use at most 192 MiB of HBM per device.

```python
import jax
import jax.numpy as jnp
from jax import lax

D = 768
HEADS = 12
HEAD = 64
FF = 3072
SIDE = 16
TUBE = 4
CLIP = 4096
TOKENS = 8192


def draw_mask_bits(key, part):
    key = jax.random.fold_in(key, 7)
    first, second = jax.random.split(key)
    clips = TOKENS // CLIP
    ratio = jax.random.randint(first, (clips, 1), 50, 101)
    level = jax.random.randint(second, (clips, CLIP), 0, 100)
    return (level < ratio).astype(jnp.int32).reshape(TOKENS)


def shard_levels(stream_key, shape, cuts, smallest, high):
    level = 1.0
    for axis_at, parts in cuts:
        steps = jax.random.uniform(jax.random.fold_in(jax.random.fold_in(stream_key, 6), axis_at), (parts,), jnp.float32, smallest / len(cuts), high / len(cuts))
        level = level * jnp.repeat(jnp.exp(steps), shape[axis_at] // parts).reshape((-1,) + (1,) * (len(shape) - 1 - axis_at))
    return level


def bell_draw(rng, dims, scale, bound, cuts=(), held_as=jnp.bfloat16):
    drawn = scale * jax.random.normal(rng, dims, jnp.float32)
    if cuts:
        drawn = drawn * shard_levels(rng, dims, cuts, -0.22, 0.18)
    return jnp.clip(drawn, -bound, bound).astype(held_as)


def setup_inputs(seed: int = 0) -> dict:
    key_of = jax.random.split(jax.random.key(seed), 28)
    inputs = bell_draw(key_of[0], (TOKENS, D), 1.0, 6.0, ((0, 32),), jnp.float32)
    cotangent = bell_draw(key_of[1], (TOKENS, D), 1.0, 6.0, ((0, 32),), jnp.float32)
    mask_bits = draw_mask_bits(jax.random.fold_in(key_of[27], 71), 0)
    frame_pregain = jnp.clip(1.0 + 0.1 * jax.random.normal(key_of[3], (D,), jnp.float32), 0.5, 1.5)
    frame_prebias = bell_draw(key_of[4], (D,), 0.3, 1.75, ((0, 32),), jnp.float32)
    frame_inweight = bell_draw(key_of[5], (D, 3, D), D ** -0.5, 0.21875, ((0, 8), (2, 4)), jnp.float32)
    frame_inbias = bell_draw(key_of[6], (2, D), 0.3, 1.75, ((1, 32),), jnp.float32)
    frame_outweight = bell_draw(key_of[7], (D, D), (D // 16) ** -0.5, 0.875, ((0, 4), (1, 8)), jnp.float32)
    frame_outbias = bell_draw(key_of[8], (D,), 0.3, 1.75, ((0, 32),), jnp.float32)
    frame_midgain = jnp.clip(1.0 + 0.1 * jax.random.normal(key_of[9], (D,), jnp.float32), 0.5, 1.5)
    frame_midbias = bell_draw(key_of[10], (D,), 0.3, 1.75, ((0, 32),), jnp.float32)
    frame_upweight = bell_draw(key_of[11], (D, FF), D ** -0.5, 0.21875, ((0, 8), (1, 4)), jnp.float32)
    frame_upbias = bell_draw(key_of[12], (FF,), 0.3, 1.75, ((0, 32),), jnp.float32)
    frame_downweight = bell_draw(key_of[13], (FF, D), FF ** -0.5, 0.109375, ((0, 4), (1, 8)), jnp.float32)
    frame_downbias = bell_draw(key_of[14], (D,), 0.3, 1.75, ((0, 32),), jnp.float32)
    tube_pregain = jnp.clip(1.0 + 0.1 * jax.random.normal(key_of[15], (D,), jnp.float32), 0.5, 1.5)
    tube_prebias = bell_draw(key_of[16], (D,), 0.3, 1.75, ((0, 32),), jnp.float32)
    tube_inweight = bell_draw(key_of[17], (D, 3, D), D ** -0.5, 0.21875, ((0, 8), (2, 4)), jnp.float32)
    tube_inbias = bell_draw(key_of[18], (2, D), 0.3, 1.75, ((1, 32),), jnp.float32)
    tube_outweight = bell_draw(key_of[19], (D, D), (D // 16) ** -0.5, 0.875, ((0, 4), (1, 8)), jnp.float32)
    tube_outbias = bell_draw(key_of[20], (D,), 0.3, 1.75, ((0, 32),), jnp.float32)
    tube_midgain = jnp.clip(1.0 + 0.1 * jax.random.normal(key_of[21], (D,), jnp.float32), 0.5, 1.5)
    tube_midbias = bell_draw(key_of[22], (D,), 0.3, 1.75, ((0, 32),), jnp.float32)
    tube_upweight = bell_draw(key_of[23], (D, FF), D ** -0.5, 0.21875, ((0, 8), (1, 4)), jnp.float32)
    tube_upbias = bell_draw(key_of[24], (FF,), 0.3, 1.75, ((0, 32),), jnp.float32)
    tube_downweight = bell_draw(key_of[25], (FF, D), FF ** -0.5, 0.109375, ((0, 4), (1, 8)), jnp.float32)
    tube_downbias = bell_draw(key_of[26], (D,), 0.3, 1.75, ((0, 32),), jnp.float32)
    return dict(inputs=inputs, cotangent=cotangent, mask_bits=mask_bits, frame_pregain=frame_pregain, frame_prebias=frame_prebias, frame_inweight=frame_inweight, frame_inbias=frame_inbias, frame_outweight=frame_outweight, frame_outbias=frame_outbias, frame_midgain=frame_midgain, frame_midbias=frame_midbias, frame_upweight=frame_upweight, frame_upbias=frame_upbias, frame_downweight=frame_downweight, frame_downbias=frame_downbias, tube_pregain=tube_pregain, tube_prebias=tube_prebias, tube_inweight=tube_inweight, tube_inbias=tube_inbias, tube_outweight=tube_outweight, tube_outbias=tube_outbias, tube_midgain=tube_midgain, tube_midbias=tube_midbias, tube_upweight=tube_upweight, tube_upbias=tube_upbias, tube_downweight=tube_downweight, tube_downbias=tube_downbias)


@jax.custom_vjp
def low(v):
    return lax.optimization_barrier(v.astype(jnp.bfloat16)).astype(jnp.float32)

@jax.custom_vjp
def low_back(v):
    return v

def low_keep(v):
    return (low(v), None)

def low_pass(kept, grad):
    return (grad,)

def back_keep(v):
    return (v, None)

def back_low(kept, grad):
    return (low(grad),)
low.defvjp(low_keep, low_pass)
low_back.defvjp(back_keep, back_low)
EPS = 1e-06

def norm_rows(values, gain, shift):
    center = values - lax.optimization_barrier(jnp.mean(values, axis=-1, keepdims=True))
    spread = lax.optimization_barrier(jnp.mean(center * center, axis=-1, keepdims=True))
    return center * lax.rsqrt(spread + EPS) * gain + shift

def spatial_split(rows):
    return rows.reshape(rows.shape[0] // (SIDE * SIDE), SIDE * SIDE, rows.shape[-1])

def spatial_join(windows):
    return windows.reshape(-1, windows.shape[-1])

def tube_split(rows):
    frames = rows.shape[0] // (SIDE * SIDE)
    across = SIDE // TUBE
    width = rows.shape[-1]
    shaped = rows.reshape(frames, across, TUBE, across, TUBE, width).transpose(1, 3, 0, 2, 4, 5)
    return shaped.reshape(across * across, frames * TUBE * TUBE, width)

def tube_join(windows):
    across = SIDE // TUBE
    frames = windows.shape[1] // (TUBE * TUBE)
    width = windows.shape[-1]
    shaped = windows.reshape(across, across, frames, TUBE, TUBE, width).transpose(2, 0, 3, 1, 4, 5)
    return shaped.reshape(-1, width)

def matmul(left, right):
    return jnp.dot(left, right, precision=lax.Precision.HIGHEST, preferred_element_type=jnp.float32)

def block(inputs, params, split, join):
    pregain, prebias, inweight, inbias, outweight, outbias, midgain, midbias, upweight, upbias, downweight, downbias = params
    normed = low(norm_rows(inputs, low(pregain), low(prebias)))
    pre = matmul(normed, low(inweight).reshape(D, 3 * D)).reshape(-1, 3, D)
    offset = jnp.stack([low(inbias[0]), jnp.zeros_like(inbias[0]), low(inbias[1])])
    packed = low(low_back(pre + offset))
    queries = split(packed[:, 0])
    keys = split(packed[:, 1])
    values = split(packed[:, 2])
    count = queries.shape[0]
    length = queries.shape[1]
    queries = queries.reshape(count, length, HEADS, HEAD)
    keys = keys.reshape(count, length, HEADS, HEAD)
    values = values.reshape(count, length, HEADS, HEAD)
    scores = low_back(jnp.einsum('wqhd,wkhd->whqk', queries, keys, precision=lax.Precision.HIGHEST) * HEAD ** (-0.5))
    shifted = scores - lax.optimization_barrier(jnp.max(scores, axis=-1, keepdims=True))
    expo = jnp.exp(shifted)
    probs = expo / lax.optimization_barrier(jnp.sum(expo, axis=-1, keepdims=True))
    mixed = jnp.einsum('whqk,wkhd->wqhd', low(probs), values, precision=lax.Precision.HIGHEST)
    context = low(low_back(join(mixed.reshape(count, length, D))))
    middle = inputs + low_back(matmul(context, low(outweight))) + low(outbias)
    normed_next = low(norm_rows(middle, low(midgain), low(midbias)))
    upper = low_back(matmul(normed_next, low(upweight)) + low(upbias))
    hidden = low(jax.nn.gelu(upper, approximate=False))
    return middle + low_back(matmul(hidden, low(downweight))) + low(downbias)

def two_blocks(inputs, frame, tube):
    middle = block(inputs, frame, spatial_split, spatial_join)
    return block(middle, tube, tube_split, tube_join)

def reference(inputs, cotangent, mask_bits, frame_pregain, frame_prebias, frame_inweight, frame_inbias, frame_outweight, frame_outbias, frame_midgain, frame_midbias, frame_upweight, frame_upbias, frame_downweight, frame_downbias, tube_pregain, tube_prebias, tube_inweight, tube_inbias, tube_outweight, tube_outbias, tube_midgain, tube_midbias, tube_upweight, tube_upbias, tube_downweight, tube_downbias):
    frame = (frame_pregain, frame_prebias, frame_inweight, frame_inbias, frame_outweight, frame_outbias, frame_midgain, frame_midbias, frame_upweight, frame_upbias, frame_downweight, frame_downbias)
    tube = (tube_pregain, tube_prebias, tube_inweight, tube_inbias, tube_outweight, tube_outbias, tube_midgain, tube_midbias, tube_upweight, tube_upbias, tube_downweight, tube_downbias)
    clips = inputs.shape[0] // CLIP

    def clip_pass(carry, slab):
        rows, grads, bits = slab
        result, pullback = jax.vjp(two_blocks, rows, frame, tube)
        row_grad, frame_grads, tube_grads = pullback(grads * bits.astype(grads.dtype)[:, None])
        carry = jax.tree.map(lambda total, part: total + part, carry, (frame_grads, tube_grads))
        return (carry, (result, row_grad))
    zeros = jax.tree.map(jnp.zeros_like, (frame, tube))
    totals, (results, row_grads) = lax.scan(clip_pass, zeros, (inputs.reshape(clips, CLIP, D), cotangent.reshape(clips, CLIP, D), mask_bits.reshape(clips, CLIP)))
    fgrad, tgrad = totals
    return (results.reshape(-1, D), row_grads.reshape(-1, D), fgrad[0], fgrad[1], fgrad[2], fgrad[3], fgrad[4], fgrad[5], fgrad[6], fgrad[7], fgrad[8], fgrad[9], fgrad[10], fgrad[11], tgrad[0], tgrad[1], tgrad[2], tgrad[3], tgrad[4], tgrad[5], tgrad[6], tgrad[7], tgrad[8], tgrad[9], tgrad[10], tgrad[11])
```

```python
import functools

import jax
import jax.numpy as jnp
import numpy as np
from jax import lax
from jax.experimental import pallas as pl
from jax.experimental.pallas import tpu as pltpu
from jax.sharding import PartitionSpec as P

MESH = pl.DeviceIdType.MESH
HEAD = 64
SIDE = 16
TUBE = 4
FRAME = SIDE * SIDE
CLIP = 4096
EPS = 1e-06
INNER = 8
F32 = jnp.float32
BF16 = jnp.bfloat16


def mm(left, right):
    return lax.dot_general(left, right, (((1,), (0,)), ((), ())), preferred_element_type=F32)


def mm_t(left, right):
    return lax.dot_general(left, right, (((1,), (1,)), ((), ())), preferred_element_type=F32)


def t_mm(left, right):
    return lax.dot_general(left, right, (((0,), (0,)), ((), ())), preferred_element_type=F32)


def exact(left, right, dims):
    return lax.dot_general(
        left, right, (dims, ((), ())), precision=lax.Precision.HIGHEST, preferred_element_type=F32
    )


def flip(value, weight):
    bit = (value // weight) % 2
    return value + weight * (1 - 2 * bit)


def flip_by(value, key):
    weight = 1
    while key:
        if key & 1:
            value = flip(value, weight)
        key >>= 1
        weight *= 2
    return value


def unit_rows(values):
    center = values - jnp.mean(values, axis=-1, keepdims=True)
    spread = jnp.mean(center * center, axis=-1, keepdims=True)
    scale = lax.rsqrt(spread + EPS)
    return center * scale, scale


def kernel(
    sizes,
    x_ref,
    g_ref,
    ws_ref,
    small_ref,
    swap_ref,
    tiles_ref,
    mask_ref,
    out_ref,
    ig_ref,
    wg_ref,
    sg_ref,
    W,
    SG,
    SV,
    BI,
    BU,
    H,
    M,
    NB,
    NT,
    GT,
    PK,
    CT,
    HID,
    GP,
    PR,
    ACC,
    GR,
    SGR,
    RES,
    SB,
    RB,
    HS,
    CS,
    US,
    PS,
    LS,
    AR,
    zs,
    zr,
    a1s,
    a1r,
    b1s,
    b1r,
    a2s,
    a2r,
    b2s,
    b2r,
    cs,
    cr,
    vs,
    vr,
    ts,
    tr,
    ss,
    sr,
    rs,
    rr,
    free_x,
    free_y,
    free_z,
    free_c,
    WG,
    ls,
):
    outer, nmp, d, rows = sizes
    per = INNER
    half = d // 2
    dp = lax.axis_index("dp")
    z = lax.axis_index("mp")
    low = dp % outer
    q = dp // outer
    c = q % 2
    x = (q // 2) % 2
    y = q // 4
    oc, ox, oy = 1 - c, 1 - x, 1 - y
    members = CLIP // FRAME
    dpc = members // nmp
    me = (dp % dpc) * nmp + z

    def place(cc, xx, yy):
        return (yy * 4 + xx * 2 + cc) * outer + low

    to_c = (place(oc, x, y), z)
    to_x = (place(c, ox, y), z)
    to_y = (place(c, x, oy), z)

    def to_z(zz):
        return (dp, zz)

    def to_member(f):
        return ((dp // dpc) * dpc + f // nmp, f % nmp)

    def send(src, dst, s_sem, r_sem, device):
        pltpu.make_async_remote_copy(
            src_ref=src, dst_ref=dst, send_sem=s_sem, recv_sem=r_sem, device_id=device, device_id_type=MESH
        ).start()

    def sent(src, s_sem):
        pltpu.make_async_remote_copy(
            src_ref=src, dst_ref=src, send_sem=s_sem, recv_sem=s_sem, device_id=to_c, device_id_type=MESH
        ).wait_send()

    def got(dst, r_sem):
        pltpu.make_async_remote_copy(
            src_ref=dst, dst_ref=dst, send_sem=r_sem, recv_sem=r_sem, device_id=to_c, device_id_type=MESH
        ).wait_recv()

    def keep(src, dst, n):
        return pltpu.make_async_copy(src, dst, ls.at[n])

    for m in range(6):
        keep(ws_ref.at[m], W.at[m, z, y, x, c], m).start()
    keep(x_ref, ACC, 6).start()

    barrier = pltpu.get_barrier_semaphore()
    for key in range(1, members):
        pl.semaphore_signal(barrier, inc=1, device_id=to_member(flip_by(me, key)), device_id_type=MESH)
    for device in (to_c, to_x, to_y):
        pl.semaphore_signal(barrier, inc=1, device_id=device, device_id_type=MESH)
    pl.semaphore_wait(barrier, members - 1 + 3)

    def z_start(m):
        for key in range(1, nmp):
            zz = flip_by(z, key)
            ref = W.at[m, z, y, x, c]
            send(ref, ref, zs.at[m, zz], zr.at[m, z], to_z(zz))

    def g1(m, k):
        zz = flip_by(z, k)
        if k:
            got(W.at[m, zz, y, x, c], zr.at[m, zz])
        t = m * nmp + k
        left = W.at[m, zz, y, x, c, :, pl.ds(0, half)]
        right = W.at[m, zz, y, x, c, :, pl.ds(half, half)]
        send(left, left, a1s.at[t], a1r.at[t], to_x)
        send(right, right, b1s.at[t], b1r.at[t], to_y)

    def g2(m, k):
        zz = flip_by(z, k)
        t = m * nmp + k
        got(W.at[m, zz, y, ox, c, :, pl.ds(0, half)], a1r.at[t])
        left = W.at[m, zz, y, :, c, :, pl.ds(0, half)]
        send(left, left, a2s.at[t], a2r.at[t], to_y)
        got(W.at[m, zz, oy, x, c, :, pl.ds(half, half)], b1r.at[t])
        right = W.at[m, zz, :, x, c, :, pl.ds(half, half)]
        send(right, right, b2s.at[t], b2r.at[t], to_x)

    def g3(m, k):
        zz = flip_by(z, k)
        t = m * nmp + k
        got(W.at[m, zz, oy, :, c, :, pl.ds(0, half)], a2r.at[t])
        got(W.at[m, zz, :, ox, c, :, pl.ds(half, half)], b2r.at[t])
        whole = W.at[m, zz, :, :, c]
        send(whole, whole, cs.at[t], cr.at[t], to_c)

    def g4(m, k):
        zz = flip_by(z, k)
        t = m * nmp + k
        got(W.at[m, zz, :, :, oc], cr.at[t])

    def g_done(m):
        for key in range(1, nmp):
            zz = flip_by(z, key)
            sent(W.at[m, z, y, x, c], zs.at[m, zz])
        for k in range(nmp):
            zz = flip_by(z, k)
            t = m * nmp + k
            sent(W.at[m, zz, y, x, c, :, pl.ds(0, half)], a1s.at[t])
            sent(W.at[m, zz, y, x, c, :, pl.ds(half, half)], b1s.at[t])
            sent(W.at[m, zz, y, :, c, :, pl.ds(0, half)], a2s.at[t])
            sent(W.at[m, zz, :, x, c, :, pl.ds(half, half)], b2s.at[t])
            sent(W.at[m, zz, :, :, c], cs.at[t])

    total = 6 * nmp

    def advance(t, base=0, last=total):
        def at(s):
            return base + s // nmp, s % nmp

        def ranged(s, stage):
            if isinstance(base, int) or s < 3 * nmp:
                if s < total:
                    stage(*at(s))
            else:
                pl.when(base == 0)(lambda: stage(*at(s)))

        def first(m, k):
            if k == 0:
                if isinstance(m, int):
                    if m + 1 < 6:
                        z_start(m + 1)
                else:
                    pl.when(m + 1 < 6)(lambda: z_start(m + 1))
            g1(m, k)

        ranged(t, first)
        if t >= 1:
            ranged(t - 1, g2)
        if t >= 2:
            ranged(t - 2, g3)
        if t >= 3:
            ranged(t - 3, g4)

    def release(m):
        g_done(m)
        pl.semaphore_signal(free_x.at[m], inc=1, device_id=to_x, device_id_type=MESH)
        pl.semaphore_signal(free_y.at[m], inc=1, device_id=to_y, device_id_type=MESH)
        for key in range(1, nmp):
            pl.semaphore_signal(free_z.at[m, z], inc=1, device_id=to_z(flip_by(z, key)), device_id_type=MESH)

    def may_send(m):
        pl.semaphore_wait(free_x.at[m], 1)
        pl.semaphore_wait(free_y.at[m], 1)

    def r1(m, k):
        t = m * nmp + k
        send(
            W.at[m, k, :, ox, c, :, pl.ds(0, half)],
            W.at[m, k, :, ox, oc, :, pl.ds(0, half)],
            a1s.at[t],
            a1r.at[t],
            to_x,
        )
        send(
            W.at[m, k, oy, :, c, :, pl.ds(half, half)],
            W.at[m, k, oy, :, oc, :, pl.ds(half, half)],
            b1s.at[t],
            b1r.at[t],
            to_y,
        )

    def add_to(dst, src):
        dst[...] = (dst[...].astype(F32) + src[...].astype(F32)).astype(BF16)

    def r2(m, k):
        t = m * nmp + k
        src = W.at[m, k, :, x, oc, :, pl.ds(0, half)]
        got(src, a1r.at[t])
        add_to(W.at[m, k, :, x, c, :, pl.ds(0, half)], src)
        send(
            W.at[m, k, oy, x, c, :, pl.ds(0, half)],
            W.at[m, k, oy, ox, oc, :, pl.ds(0, half)],
            a2s.at[t],
            a2r.at[t],
            to_y,
        )
        src = W.at[m, k, y, :, oc, :, pl.ds(half, half)]
        got(src, b1r.at[t])
        add_to(W.at[m, k, y, :, c, :, pl.ds(half, half)], src)
        send(
            W.at[m, k, y, ox, c, :, pl.ds(half, half)],
            W.at[m, k, oy, ox, oc, :, pl.ds(half, half)],
            b2s.at[t],
            b2r.at[t],
            to_x,
        )

    def r3(m, k):
        t = m * nmp + k
        src = W.at[m, k, y, ox, oc, :, pl.ds(0, half)]
        got(src, a2r.at[t])
        add_to(W.at[m, k, y, x, c, :, pl.ds(0, half)], src)
        src = W.at[m, k, oy, x, oc, :, pl.ds(half, half)]
        got(src, b2r.at[t])
        add_to(W.at[m, k, y, x, c, :, pl.ds(half, half)], src)

        @pl.when(k != z)
        def _():
            pl.semaphore_wait(free_z.at[m, k], 1)
            send(W.at[m, k, y, x, c], W.at[m, z, oy, ox, oc], zs.at[m, k], zr.at[m, z], to_z(k))

    def r4(m):
        sum_ = W[m, z, y, x, c].astype(F32)
        for key in range(1, nmp):
            zz = flip_by(z, key)
            src = W.at[m, zz, oy, ox, oc]
            got(src, zr.at[m, zz])
            sum_ = sum_ + src[...].astype(F32)
        if m < 3:
            keep(WG.at[m], wg_ref.at[m + 3], m + 3).wait()
        WG[m % 3] = sum_
        keep(WG.at[m % 3], wg_ref.at[m], m).start()

    def r_done(m):
        for key in range(1, nmp):
            zz = flip_by(z, key)
            sent(W.at[m, zz, y, x, c], zs.at[m, zz])
        for k in range(nmp):
            t = m * nmp + k
            sent(W.at[m, k, :, ox, c, :, pl.ds(0, half)], a1s.at[t])
            sent(W.at[m, k, oy, :, c, :, pl.ds(half, half)], b1s.at[t])
            sent(W.at[m, k, oy, x, c, :, pl.ds(0, half)], a2s.at[t])
            sent(W.at[m, k, y, ox, c, :, pl.ds(half, half)], b2s.at[t])

    def each(stage):
        def step(k, _):
            stage(k)
            return 0
        lax.fori_loop(0, nmp, step, 0)

    def swap_start(i):
        RB[i, pl.ds(me, 1)] = SB[i, pl.ds(me, 1)]
        for key in range(1, members):
            f = flip_by(me, key)
            send(SB.at[i, f], RB.at[i, me], ts.at[i, key], tr.at[i, key], to_member(f))

    def swap_wait(i):
        for key in range(1, members):
            got(RB.at[i, flip_by(me, key)], tr.at[i, key])

    def swap_done(i):
        for key in range(1, members):
            sent(SB.at[i, flip_by(me, key)], ts.at[i, key])

    def rows_of(ref, i):
        return ref[i].reshape(rows, d)

    for m in range(6):
        keep(ws_ref.at[m], W.at[m, z, y, x, c], m).wait()
    z_start(0)
    SG[z, y, x, c] = small_ref[...]
    for key in range(1, nmp):
        zz = flip_by(z, key)
        ref = SG.at[z, y, x, c]
        send(ref, ref, vs.at[zz], vr.at[z], to_z(zz))
    advance(0)
    swap = swap_ref[...]
    SB[0] = mm(swap, g_ref[...]).astype(BF16).reshape(members, rows // members, d)
    swap_start(0)
    keep(x_ref, ACC, 6).wait()
    H[0] = exact(swap.astype(F32), ACC[...], ((1,), (0,)))
    for key in range(1, nmp):
        zz = flip_by(z, key)
        got(SG.at[zz, y, x, c], vr.at[zz])
    ref = SG.at[:, y, x, c]
    send(ref, ref, vs.at[nmp], vr.at[nmp], to_x)
    advance(1)
    got(SG.at[:, y, ox, c], vr.at[nmp])
    ref = SG.at[:, y, :, c]
    send(ref, ref, vs.at[nmp + 1], vr.at[nmp + 1], to_y)
    advance(2)
    got(SG.at[:, oy, :, c], vr.at[nmp + 1])
    ref = SG.at[:, :, :, c]
    send(ref, ref, vs.at[nmp + 2], vr.at[nmp + 2], to_c)
    advance(3)
    got(SG.at[:, :, :, oc], vr.at[nmp + 2])

    lane = lax.broadcasted_iota(jnp.int32, (1, d), 1)
    third = d // nmp
    tall = SG[...].reshape(nmp * per * 16, 128)
    spread = mm(tall, tiles_ref[0]).reshape(nmp * per, 16, d)
    spread = jnp.sum(spread * mask_ref[0:nmp * per].reshape(nmp * per, 1, d), axis=0)
    SV[0, 0:6] = spread[0:6]
    SV[1, 0:6] = spread[6:12]
    is_q = (lane < third).astype(F32)
    is_v = jnp.logical_and(lane >= third, lane < 2 * third).astype(F32)
    spread_in = mm(tall, tiles_ref[1]).reshape(nmp, per, 16, d)
    spread_up = mm(tall, tiles_ref[2]).reshape(nmp, per, 16, d)
    mask_in = mask_ref[nmp * per:nmp * per + per].reshape(per, 1, d)
    mask_up = mask_ref[nmp * per + per:nmp * per + 2 * per].reshape(per, 1, d)
    for k in range(nmp):
        one = jnp.sum(spread_in[k] * mask_in, axis=0)
        two = jnp.sum(spread_up[k] * mask_up, axis=0)
        for b in range(2):
            BI[b, k] = one[12 + 2 * b:13 + 2 * b] * is_q + one[13 + 2 * b:14 + 2 * b] * is_v
            BU[b, k] = two[b:b + 1]
    advance(4)
    advance(5)
    advance(6)

    lane2 = lax.broadcasted_iota(jnp.int32, (1, 256), 1)
    heads = third // HEAD

    def head_mask(lead):
        return jnp.logical_and(lane2 >= lead * HEAD, lane2 < lead * HEAD + HEAD).astype(F32).astype(BF16)

    q_masks = [head_mask(h) for h in range(heads)]
    v_masks = [head_mask(h + 1) for h in range(heads)]
    scale = HEAD ** (-0.5)
    wide = 5 * 128

    def flat(values):
        return values.reshape(d, values.shape[-1])

    def lower(values):
        return values.reshape(half, values.shape[-1])

    def tall_view(values):
        return values.T.astype(BF16).reshape(2, 2, 2, d // per, rows)

    def forward(b, _):
        m = 3 * b
        h = H[b]
        unit, _s = unit_rows(h)
        normed = unit * SV[b, 0:1] + SV[b, 1:2]
        NB[...] = normed.astype(BF16)
        NT[b, 0] = tall_view(normed)
        ACC[...] = h + SV[b, 2:3]

        def attend(k, _):
            packed = (mm(NB[...], flat(W[m, k, :, :, :, :, 0:wide])) + BI[b, k, :, 0:wide]).astype(BF16)
            PK[b, k] = packed
            qs = packed[:, 0:256] * BF16(scale)
            vv = packed[:, 128:384]
            kk = packed[:, 384:640]
            mixed = jnp.zeros((rows, 256), F32)
            for h in range(heads):
                scores = mm_t(qs * q_masks[h], kk)
                expo = jnp.exp(scores - jnp.max(scores, axis=-1, keepdims=True))
                probs = (expo * (1.0 / jnp.sum(expo, axis=-1, keepdims=True))).astype(BF16)
                PR[b, k, h] = probs
                mixed += mm(probs, vv * v_masks[h])
            mixed = mixed.astype(BF16)
            CT[b, k] = mixed
            ACC[...] += mm_t(mixed, flat(W[m, k, :, :, :, :, d - 256:d]))
            return 0

        lax.fori_loop(0, nmp, attend, 0)
        for t in range(7, 11):
            advance(t, m)
        middle = ACC[...]
        M[b] = middle
        unit, _s = unit_rows(middle)
        normed = unit * SV[b, 3:4] + SV[b, 4:5]
        NB[...] = normed.astype(BF16)
        NT[b, 1] = tall_view(normed)
        ACC[...] = middle + SV[b, 5:6]

        def expand(k, _):
            upper = mm(NB[...], flat(W[m + 1, k])) + BU[b, k]
            cdf = 0.5 + 0.5 * lax.erf(upper * (0.5 ** 0.5))
            HID[b, k] = (upper * cdf).astype(BF16)
            density = jnp.exp(-0.5 * upper * upper) * ((2 * np.pi) ** -0.5)
            GP[b, k] = (cdf + upper * density).astype(BF16)
            return 0

        lax.fori_loop(0, nmp, expand, 0)
        for t in range(11, 15):
            advance(t, m)

        def contract(k, _):
            ACC[...] += mm_t(HID[b, k], flat(W[m + 2, k]))
            return 0

        lax.fori_loop(0, nmp, contract, 0)
        SB[1 + b] = ACC[...].astype(BF16).reshape(members, rows // members, d)
        swap_start(1 + b)
        for t in range(15, 19):
            advance(t, m)

        @pl.when(b == 0)
        def _():
            swap_wait(1)
            H[1] = rows_of(RB, 1).astype(F32)
        return 0

    lax.fori_loop(0, 2, forward, 0)

    swap_wait(0)
    GR[...] = rows_of(RB, 0).astype(F32)

    def norm_back(grad, start, gain):
        unit, scale = unit_rows(start)
        lifted = grad * gain
        back = scale * (
            lifted
            - jnp.mean(lifted, axis=-1, keepdims=True)
            - unit * jnp.mean(lifted * unit, axis=-1, keepdims=True)
        )
        return back, jnp.sum(grad * unit, axis=0, keepdims=True), jnp.sum(grad, axis=0, keepdims=True)

    def to_sibling(src, dst, n):
        send(src, dst, ss.at[n], sr.at[n], to_c)

    def backward(step, _):
        b = 1 - step
        m = 3 * b
        row = 16 * b

        @pl.when(step == 1)
        def _():
            pl.semaphore_wait(free_c, 1)

        to_sibling(HID.at[b], HS, 0)
        to_sibling(NT.at[b, 0, :, :, oc], LS.at[0], 1)
        to_sibling(NT.at[b, 1, :, :, oc], LS.at[1], 2)
        to_sibling(CT.at[b], CS, 3)
        grad = GR[...]
        SGR[pl.ds(row + 5, 1)] = jnp.sum(grad, axis=0, keepdims=True)
        NB[...] = grad.astype(BF16)
        GT[0] = tall_view(grad)
        to_sibling(GT.at[0, :, :, oc], LS.at[2], 4)

        def shrink(k, _):
            hidden_grad = mm(NB[...], flat(W[m + 2, k]))
            upper_grad = (GP[b, k].astype(F32) * hidden_grad).astype(BF16)
            GP[b, k] = upper_grad
            to_sibling(GP.at[b, k], US.at[k], 6 + k)
            SGR[pl.ds(row + 10 + k, 1)] = jnp.sum(upper_grad.astype(F32), axis=0, keepdims=True)
            return 0

        lax.fori_loop(0, nmp, shrink, 0)
        release(m + 2)
        got(HS, sr.at[0])
        got(LS.at[2], sr.at[4])
        may_send(m + 2)

        def down_grad(k, _):
            own = mm(lower(GT[0, :, :, c]), HID[b, k]) + mm(lower(LS[2]), HS[k])
            W[m + 2, k, :, :, c] = own.astype(BF16).reshape(2, 2, d // per, d)
            r1(m + 2, k)
            return 0

        lax.fori_loop(0, nmp, down_grad, 0)
        ACC[...] = jnp.zeros_like(ACC)

        def spread_up(k, _):
            ACC[...] += mm_t(GP[b, k], flat(W[m + 1, k]))
            return 0

        lax.fori_loop(0, nmp, spread_up, 0)
        release(m + 1)
        for k in range(nmp):
            got(US.at[k], sr.at[6 + k])
        got(LS.at[1], sr.at[2])
        may_send(m + 1)

        @pl.when(step == 1)
        def _():
            each(functools.partial(r2, 3))
            each(functools.partial(r3, 4))
            r4(5)

        def up_grad(k, _):
            own = mm(lower(NT[b, 1, :, :, c]), GP[b, k]) + mm(lower(LS[1]), US[k])
            W[m + 1, k, :, :, c] = own.astype(BF16).reshape(2, 2, d // per, d)
            r1(m + 1, k)
            return 0

        lax.fori_loop(0, nmp, up_grad, 0)
        back, gain_grad, bias_grad = norm_back(ACC[...], M[b], SV[b, 3:4])
        SGR[pl.ds(row + 3, 1)] = gain_grad
        SGR[pl.ds(row + 4, 1)] = bias_grad
        middle_grad = GR[...] + back
        GR[...] = middle_grad
        SGR[pl.ds(row + 2, 1)] = jnp.sum(middle_grad, axis=0, keepdims=True)
        NB[...] = middle_grad.astype(BF16)
        GT[1] = tall_view(middle_grad)
        to_sibling(GT.at[1, :, :, oc], LS.at[3], 5)
        ACC[...] = jnp.zeros_like(ACC)
        each(functools.partial(r2, m + 2))

        @pl.when(step == 1)
        def _():
            each(functools.partial(r3, 3))
            r4(4)

        def attend_back(k, _):
            mixed_grad = mm(NB[...], flat(W[m, k, :, :, :, :, d - 256:d])).astype(BF16)
            packed = PK[b, k]
            qs = packed[:, 0:256] * BF16(scale)
            vv = packed[:, 128:384]
            kk = packed[:, 384:640]
            q_grad = jnp.zeros((rows, 256), F32)
            k_grad = jnp.zeros((rows, 256), F32)
            v_grad = jnp.zeros((rows, 256), F32)
            for h in range(heads):
                part = mixed_grad * v_masks[h]
                probs_low = PR[b, k, h]
                probs = probs_low.astype(F32)
                weighted = probs * mm_t(part, vv)
                score_grad = (weighted - probs * jnp.sum(weighted, axis=-1, keepdims=True)).astype(BF16)
                q_grad += mm(score_grad, kk * q_masks[h])
                k_grad += t_mm(score_grad, qs * q_masks[h])
                v_grad += t_mm(probs_low, part)
            q_grad = q_grad * scale
            packed_grad = jnp.concatenate(
                [q_grad[:, 0:128], q_grad[:, 128:256] + v_grad[:, 0:128], v_grad[:, 128:256], k_grad], axis=1
            ).astype(BF16)
            PK[b, k] = packed_grad
            to_sibling(PK.at[b, k], PS.at[k], 10 + k)
            SGR[pl.ds(row + 6 + k, 1), 0:wide] = jnp.sum(packed_grad.astype(F32), axis=0, keepdims=True)
            ACC[...] += mm_t(packed_grad, flat(W[m, k, :, :, :, :, 0:wide]))
            return 0

        lax.fori_loop(0, nmp, attend_back, 0)
        release(m)
        back, gain_grad, bias_grad = norm_back(ACC[...], H[b], SV[b, 0:1])
        SGR[pl.ds(row, 1)] = gain_grad
        SGR[pl.ds(row + 1, 1)] = bias_grad
        GR[...] = GR[...] + back

        @pl.when(step == 0)
        def _():
            SB[3] = GR[...].astype(BF16).reshape(members, rows // members, d)
            swap_start(3)

        for k in range(nmp):
            got(PS.at[k], sr.at[10 + k])
        got(LS.at[0], sr.at[1])
        got(LS.at[3], sr.at[5])
        got(CS, sr.at[3])
        may_send(m)

        def in_grad(k, _):
            one = mm(lower(NT[b, 0, :, :, c]), PK[b, k]) + mm(lower(LS[0]), PS[k])
            two = mm(lower(GT[1, :, :, c]), CT[b, k]) + mm(lower(LS[3]), CS[k])
            own = jnp.concatenate(
                [one[:, 0:512], one[:, 512:640] + two[:, 0:128], two[:, 128:256]], axis=1
            ).astype(BF16)
            W[m, k, :, :, c] = own.reshape(2, 2, d // per, d)
            r1(m, k)
            return 0

        lax.fori_loop(0, nmp, in_grad, 0)

        sent(HID.at[b], ss.at[0])
        sent(NT.at[b, 0, :, :, oc], ss.at[1])
        sent(NT.at[b, 1, :, :, oc], ss.at[2])
        sent(CT.at[b], ss.at[3])
        sent(GT.at[0, :, :, oc], ss.at[4])
        sent(GT.at[1, :, :, oc], ss.at[5])
        for k in range(nmp):
            sent(GP.at[b, k], ss.at[6 + k])
            sent(PK.at[b, k], ss.at[10 + k])

        @pl.when(step == 0)
        def _():
            pl.semaphore_signal(free_c, inc=1, device_id=to_c, device_id_type=MESH)

        each(functools.partial(r2, m + 1))
        each(functools.partial(r3, m + 2))

        @pl.when(step == 1)
        def _():
            r4(3)

        @pl.when(step == 0)
        def _():
            swap_wait(3)
            GR[...] = rows_of(RB, 3).astype(F32)
        return 0

    lax.fori_loop(0, 2, backward, 0)

    peers = [to_c, to_x, to_y]
    key = 1
    while key < nmp:
        peers.append(to_z(flip_by(z, key)))
        key *= 2
    for i, device in enumerate(peers):
        send(SGR, AR.at[i], rs.at[i], rr.at[i], device)
        if i == 0:
            each(functools.partial(r2, 0))
        if i == 1:
            each(functools.partial(r3, 1))
        if i == 2:
            r4(2)
        if i == 3:
            swap_wait(2)
            M[0] = mm(swap, rows_of(RB, 2))
            keep(M.at[0], out_ref, 6).start()
            ACC[...] = exact(swap.astype(F32), GR[...], ((1,), (0,)))
            keep(ACC, ig_ref, 7).start()
        sent(SGR, rs.at[i])
        got(AR.at[i], rr.at[i])
        SGR[...] += AR[i]
    each(functools.partial(r3, 0))
    grads = SGR[...]
    own = mask_ref[pl.ds(z * per + q, 1)]
    own_in = mask_ref[pl.ds(nmp * per + q, 1)]
    own_up = mask_ref[pl.ds(nmp * per + per + q, 1)]
    turned = ((1,), (1,))
    RES[0] = exact(grads * own, tiles_ref[0].astype(F32), turned)
    RES[1] = exact(grads * own_in * is_q, tiles_ref[1].astype(F32), turned)
    RES[2] = exact(grads * own_in * is_v, tiles_ref[1].astype(F32), turned)
    RES[3] = exact(grads * own_up, tiles_ref[2].astype(F32), turned)
    sg_ref[...] = jnp.zeros_like(sg_ref)
    for b in range(2):
        sg_ref[b, 0:6] = RES[0, 16 * b:16 * b + 6]
        sg_ref[b, 6:7] = RES[1, pl.ds(16 * b + 6 + z, 1)]
        sg_ref[b, 7:8] = RES[2, pl.ds(16 * b + 6 + z, 1)]
        sg_ref[b, 8:9] = RES[3, pl.ds(16 * b + 10 + z, 1)]
    r4(1)
    r4(0)
    for m in range(3):
        keep(WG.at[m], wg_ref.at[m], m).wait()
    keep(M.at[0], out_ref, 6).wait()
    keep(ACC, ig_ref, 7).wait()
    for m in range(6):
        r_done(m)
    for i in range(4):
        swap_done(i)
    for key in range(1, nmp):
        sent(SG.at[z, y, x, c], vs.at[flip_by(z, key)])
    sent(SG.at[:, y, x, c], vs.at[nmp])
    sent(SG.at[:, y, :, c], vs.at[nmp + 1])
    sent(SG.at[:, :, :, c], vs.at[nmp + 2])


def tables(outer, ndp, nmp, d):
    n = d // (ndp * nmp)
    tiles = np.zeros((3, 128, d), np.float32)
    masks = np.zeros((nmp * INNER + 2 * INNER, d), np.float32)
    for at in range(d):
        i = at % n
        zz = (at // n) % nmp
        pp = at // (n * nmp)
        qq, lo = pp // outer, pp % outer
        tiles[0, lo * n + i, at] = 1
        masks[zz * INNER + qq, at] = 1
    third = d // nmp
    step = third // INNER
    for at in range(2 * third):
        tiles[1, at % step, at] = 1
        masks[nmp * INNER + (at % third) // step, at] = 1
    step = d // INNER
    for at in range(d):
        tiles[2, 32 + at % step, at] = 1
        masks[nmp * INNER + INNER + at // step, at] = 1
    return tiles, masks


def turn_table():
    swap = np.zeros((FRAME, FRAME), np.float32)
    across = SIDE // TUBE
    for wr in range(across):
        for i in range(TUBE):
            for wc in range(across):
                for j in range(TUBE):
                    natural = ((wr * TUBE + i) * across + wc) * TUBE + j
                    turned = ((wr * across + wc) * TUBE + i) * TUBE + j
                    swap[turned, natural] = 1
    return swap


def fused(sizes, x, grad, shards, small, ndp):
    outer, nmp, d, rows = sizes
    tiles, masks = tables(outer, ndp, nmp, d)
    members = CLIP // FRAME
    vmem = pltpu.VMEM
    dma = pltpu.SemaphoreType.DMA
    regular = pltpu.SemaphoreType.REGULAR
    block = d // INNER
    steps = 6 * nmp
    scratch = [
        vmem((6, nmp, 2, 2, 2, block, d), BF16),
        vmem((nmp, 2, 2, 2, 16, 128), BF16),
        vmem((2, 8, d), F32),
        vmem((2, nmp, 1, d), F32),
        vmem((2, nmp, 1, d), F32),
        vmem((2, rows, d), F32),
        vmem((2, rows, d), F32),
        vmem((rows, d), BF16),
        vmem((2, 2, 2, 2, 2, block, rows), BF16),
        vmem((2, 2, 2, 2, block, rows), BF16),
        vmem((2, nmp, rows, 640), BF16),
        vmem((2, nmp, rows, 256), BF16),
        vmem((2, nmp, rows, d), BF16),
        vmem((2, nmp, rows, d), BF16),
        vmem((2, nmp, d // nmp // HEAD, rows, rows), BF16),
        vmem((rows, d), F32),
        vmem((rows, d), F32),
        vmem((32, d), F32),
        vmem((4, 32, 128), F32),
        vmem((4, members, rows // members, d), BF16),
        vmem((4, members, rows // members, d), BF16),
        vmem((nmp, rows, d), BF16),
        vmem((nmp, rows, 256), BF16),
        vmem((nmp, rows, d), BF16),
        vmem((nmp, rows, 640), BF16),
        vmem((4, 2, 2, block, rows), BF16),
        vmem((3 + nmp.bit_length() - 1, 32, d), F32),
        dma((6, nmp)),
        dma((6, nmp)),
    ]
    scratch += [dma((steps,)) for _ in range(10)]
    scratch += [
        dma((nmp + 3,)),
        dma((nmp + 3,)),
        dma((4, members)),
        dma((4, members)),
        dma((14,)),
        dma((14,)),
        dma((3 + nmp.bit_length() - 1,)),
        dma((3 + nmp.bit_length() - 1,)),
        regular((6,)),
        regular((6,)),
        regular((6, nmp)),
        regular,
        vmem((3, block, d), F32),
        dma((8,)),
    ]
    return pl.pallas_call(
        functools.partial(kernel, sizes),
        out_shape=(
            jax.ShapeDtypeStruct((rows, d), F32),
            jax.ShapeDtypeStruct((rows, d), F32),
            jax.ShapeDtypeStruct((6, block, d), F32),
            jax.ShapeDtypeStruct((2, 16, 128), F32),
        ),
        in_specs=[pl.BlockSpec(memory_space=s) for s in (pl.ANY, vmem, pl.ANY, vmem, vmem, vmem, vmem)],
        out_specs=tuple(pl.BlockSpec(memory_space=s) for s in (pl.ANY, pl.ANY, pl.ANY, vmem)),
        scratch_shapes=scratch,
        compiler_params=pltpu.CompilerParams(
            collective_id=0, has_side_effects=True, vmem_limit_bytes=64 << 20
        ),
        name="two_blocks",
    )(
        x,
        grad,
        shards,
        small,
        jnp.asarray(turn_table(), BF16),
        jnp.asarray(tiles, BF16),
        jnp.asarray(masks, F32),
    )


def pack_weights(params):
    inweight, outweight, upweight, downweight = params[2], params[4], params[8], params[10]
    attention = jnp.concatenate([inweight[:, 0], inweight[:, 2], inweight[:, 1], outweight.T], axis=1)
    return [attention.astype(BF16), upweight.astype(BF16), downweight.T.astype(BF16)]


def shards_of(ndp, nmp, inputs, cotangent, mask_bits, *params):
    frame, tube = params[:12], params[12:]
    d = inputs.shape[1]
    rows = inputs.shape[0]
    outer = ndp // INNER
    groups = [[qq * outer + lo for lo in range(outer)] for qq in range(INNER)]
    weights = jnp.stack(pack_weights(frame) + pack_weights(tube))
    vectors = []
    for block in (frame, tube):
        vectors += [block[0], block[1], block[5], block[6], block[7], block[11]]
    for block in (frame, tube):
        vectors += [block[3][0], block[3][1]]
    vectors = jnp.stack(vectors).astype(BF16)
    ups = jnp.stack([frame[9], tube[9]]).astype(BF16)
    if outer > 1:
        weights = lax.all_gather(weights, "dp", axis=1, tiled=True, axis_index_groups=groups)
        vectors = lax.all_gather(vectors, "dp", axis=1, tiled=True, axis_index_groups=groups)
        ups = lax.all_gather(ups, "dp", axis=1, tiled=True, axis_index_groups=groups)
    wide = vectors.shape[1]
    small = jnp.concatenate(
        [jnp.pad(vectors, ((0, 0), (0, 32 - wide))), jnp.pad(ups, ((0, 14), (0, 0)))], axis=1
    )
    grad = (cotangent * mask_bits.astype(F32)[:, None]).astype(BF16)
    out, input_grad, wg, sg = fused((outer, nmp, d, rows), inputs, grad, weights, small, ndp)
    if outer > 1:
        wg = lax.psum_scatter(wg, "dp", scatter_dimension=1, tiled=True, axis_index_groups=groups)
        sg = lax.psum(sg, "dp", axis_index_groups=groups)
    low = lax.axis_index("dp") % outer

    def piece(values, start, size):
        size = size // outer
        if outer == 1:
            return values[start:start + size]
        return lax.dynamic_slice_in_dim(values, start + low * size, size)

    n = wide
    third = d // nmp
    results = []
    for b in range(2):
        attention, up, down = wg[3 * b], wg[3 * b + 1], wg[3 * b + 2]
        rows_ = sg[b]
        results += [
            piece(rows_[0], 0, n),
            piece(rows_[1], 0, n),
            jnp.stack([attention[:, 0:third], attention[:, 2 * third:3 * third], attention[:, third:2 * third]], axis=1),
            jnp.stack([piece(rows_[6], 0, n), piece(rows_[7], 0, n)]),
            attention[:, 3 * third:].T,
            piece(rows_[2], 0, n),
            piece(rows_[3], 0, n),
            piece(rows_[4], 0, n),
            up,
            piece(rows_[8], 32, 4 * n),
            down.T,
            piece(rows_[5], 0, n),
        ]
    return (out, input_grad) + tuple(results)


def solution(mesh):
    rows = P(("dp", "mp"), None)
    small = P(("dp", "mp"))
    block = (
        small,
        small,
        P("dp", None, "mp"),
        P(None, ("mp", "dp")),
        P("mp", "dp"),
        small,
        small,
        small,
        P("dp", "mp"),
        P(("mp", "dp")),
        P("mp", "dp"),
        small,
    )
    return jax.shard_map(
        functools.partial(shards_of, mesh.shape["dp"], mesh.shape["mp"]),
        mesh=mesh,
        in_specs=(rows, rows, small) + block + block,
        out_specs=(rows, rows) + block + block,
        check_vma=False,
    )
```

```python
import functools

import jax
import jax.numpy as jnp
import numpy as np
from jax import lax
from jax.experimental import pallas as pl
from jax.experimental.pallas import tpu as pltpu
from jax.sharding import PartitionSpec as P

MESH = pl.DeviceIdType.MESH
HEAD = 64
SIDE = 16
TUBE = 4
FRAME = SIDE * SIDE
CLIP = 4096
EPS = 1e-06
INNER = 8
LEAD = 3
LAG = 3
DEPTH = 3
LAG_TWO = 4
LAG_THREE = 7
F32 = jnp.float32
BF16 = jnp.bfloat16


def mm(left, right):
    return lax.dot_general(left, right, (((1,), (0,)), ((), ())), preferred_element_type=F32)


def mm_t(left, right):
    return lax.dot_general(left, right, (((1,), (1,)), ((), ())), preferred_element_type=F32)


def t_mm(left, right):
    return lax.dot_general(left, right, (((0,), (0,)), ((), ())), preferred_element_type=F32)


def exact(left, right, dims):
    return lax.dot_general(
        left, right, (dims, ((), ())), precision=lax.Precision.HIGHEST, preferred_element_type=F32
    )


def flip(value, weight):
    bit = (value // weight) % 2
    return value + weight * (1 - 2 * bit)


def flip_by(value, key):
    weight = 1
    while key:
        if key & 1:
            value = flip(value, weight)
        key >>= 1
        weight *= 2
    return value


def unit_rows(values):
    center = values - jnp.mean(values, axis=-1, keepdims=True)
    spread = jnp.mean(center * center, axis=-1, keepdims=True)
    scale = lax.rsqrt(spread + EPS)
    return center * scale, scale


def kernel(
    sizes,
    count,
    *refs,
):
    x_ref, ct_ref, bits_ref = refs[:3]
    matrices = (refs[3:7], refs[7:11])
    vectors = refs[11:11 + count]
    swap_ref, tiles_ref, mask_ref, out_ref, ig_ref = refs[11 + count:16 + count]
    grads_out = (refs[16 + count:20 + count], refs[20 + count:24 + count])
    sg_ref = refs[24 + count]
    body(
        sizes, x_ref, ct_ref, bits_ref, matrices, vectors, swap_ref, tiles_ref, mask_ref, out_ref, ig_ref,
        grads_out, sg_ref, *refs[25 + count:]
    )


def body(
    sizes,
    x_ref,
    ct_ref,
    bits_ref,
    matrices,
    vectors,
    swap_ref,
    tiles_ref,
    mask_ref,
    out_ref,
    ig_ref,
    grads_out,
    sg_ref,
    W,
    SG,
    SV,
    BI,
    BU,
    H,
    M,
    NB,
    NT,
    GT,
    PK,
    CT,
    HID,
    GP,
    PR,
    ACC,
    GR,
    SGR,
    XS,
    XR,
    SB,
    RB,
    HS,
    CS,
    US,
    PS,
    LS,
    zs,
    zr,
    h1s,
    h1r,
    h2s,
    h2r,
    cs,
    cr,
    vs,
    vr,
    ts,
    tr,
    ss,
    sr,
    rs,
    rr,
    free,
    free_c,
    WI,
    WO,
    SM,
    ls,
):
    outer, nmp, d, rows = sizes
    per = INNER
    half = d // 2
    dp = lax.axis_index("dp")
    z = lax.axis_index("mp")
    low = dp % outer
    q = dp // outer
    c = q % 2
    x = (q // 2) % 2
    y = q // 4
    oc, ox, oy = 1 - c, 1 - x, 1 - y
    members = CLIP // FRAME
    dpc = members // nmp
    me = (dp % dpc) * nmp + z

    def place(cc, xx, yy):
        return (yy * 4 + xx * 2 + cc) * outer + low

    to_c = (place(oc, x, y), z)
    to_x = (place(c, ox, y), z)
    to_y = (place(c, x, oy), z)

    def to_z(zz):
        return (dp, zz)

    def peer(key):
        return flip_by(q, key // nmp), flip_by(z, key % nmp)

    def to_peer(key):
        qq, zz = peer(key)
        return (qq * outer + low, zz)

    def to_member(f):
        return ((dp // dpc) * dpc + f // nmp, f % nmp)

    def send(src, dst, s_sem, r_sem, device):
        pltpu.make_async_remote_copy(
            src_ref=src, dst_ref=dst, send_sem=s_sem, recv_sem=r_sem, device_id=device, device_id_type=MESH
        ).start()

    def sent(src, s_sem):
        pltpu.make_async_remote_copy(
            src_ref=src, dst_ref=src, send_sem=s_sem, recv_sem=s_sem, device_id=to_c, device_id_type=MESH
        ).wait_send()

    def got(dst, r_sem):
        pltpu.make_async_remote_copy(
            src_ref=dst, dst_ref=dst, send_sem=r_sem, recv_sem=r_sem, device_id=to_c, device_id_type=MESH
        ).wait_recv()

    def keep(src, dst, n):
        return pltpu.make_async_copy(src, dst, ls.at[n])

    block = d // per
    third = d // nmp

    def matrix_copies(b):
        inw, outw, up, down = matrices[b]
        return (
            keep(inw, WI.at[b], 4 * b),
            keep(outw, WO.at[b], 4 * b + 1),
            keep(up, M.at[b, pl.ds(0, block)], 4 * b + 2),
            keep(down, M.at[b, pl.ds(block, block)], 4 * b + 3),
        )

    for b in range(2):
        for copy in matrix_copies(b):
            copy.start()
    keep(x_ref, ACC, 8).start()
    keep(ct_ref, GR, 9).start()

    barrier = pltpu.get_barrier_semaphore()
    greeted = [to_peer(key) for key in range(1, nmp * per)]
    if outer > 1:
        greeted += [to_member(flip_by(me, key)) for key in range(1, members)]
    for device in greeted:
        pl.semaphore_signal(barrier, inc=1, device_id=device, device_id_type=MESH)
    SM[...] = jnp.zeros_like(SM)
    narrow = 0
    for i, ref in enumerate(vectors[:12]):
        narrow = ref.shape[1]
        SM[i:i + 1, 0:narrow] = ref[...]
    for i, ref in enumerate(vectors[12:14]):
        SM[12 + 2 * i:14 + 2 * i, 0:narrow] = ref[...]
    for i, ref in enumerate(vectors[14:16]):
        SM[i:i + 1, 32:32 + ref.shape[1]] = ref[...]
    SG[z, y, x, c] = SM[...].astype(BF16)

    def own_shards(b):
        copies = matrix_copies(b)
        copies[0].wait()
        copies[1].wait()
        parts = [WI[b, 0], WI[b, 2], WI[b, 1], WO[b].T]
        W[3 * b, z, y, x, c] = jnp.concatenate(parts, axis=1).astype(BF16)
        copies[2].wait()
        W[3 * b + 1, z, y, x, c] = M[b, 0:block].astype(BF16)
        copies[3].wait()
        W[3 * b + 2, z, y, x, c] = M[b, block:2 * block].astype(BF16)

    own_shards(0)
    pl.semaphore_wait(barrier, len(greeted))

    def z_start(m):
        for key in range(1, nmp):
            ref = W.at[m, z, y, x, c]
            send(ref, ref, zs.at[m], zr.at[m, z], to_z(flip_by(z, key)))

    def g1(m, k):
        zz = flip_by(z, k)
        if k:
            got(W.at[m, zz, y, x, c], zr.at[m, zz])
        t = m * nmp + k
        left = W.at[m, zz, y, x, c, :, pl.ds(0, half)]
        right = W.at[m, zz, y, x, c, :, pl.ds(half, half)]
        send(left, left, h1s.at[m], h1r.at[t], to_x)
        send(right, right, h1s.at[m], h1r.at[t], to_y)

    def g2(m, k):
        zz = flip_by(z, k)
        t = m * nmp + k
        got(W.at[m, zz, oy, ox, c], h1r.at[t])
        left = W.at[m, zz, y, :, c, :, pl.ds(0, half)]
        right = W.at[m, zz, :, x, c, :, pl.ds(half, half)]
        send(left, left, h2s.at[m], h2r.at[t], to_y)
        send(right, right, h2s.at[m], h2r.at[t], to_x)

    def g3(m, k):
        zz = flip_by(z, k)
        t = m * nmp + k
        got(W.at[m, zz, oy, :, c], h2r.at[t])
        whole = W.at[m, zz, :, :, c]
        send(whole, whole, cs.at[m], cr.at[t], to_c)

    def g4(m, k):
        zz = flip_by(z, k)
        t = m * nmp + k
        got(W.at[m, zz, :, :, oc], cr.at[t])

    def g_done(m):
        sent(W.at[m, pl.ds(0, nmp - 1), y, x, c], zs.at[m])
        sent(W.at[m, :, y, x, c], h1s.at[m])
        sent(W.at[m, :, y, :, c], h2s.at[m])
        sent(W.at[m, :, :, :, c], cs.at[m])

    total = 6 * nmp

    def advance(t, base=0):
        def ranged(s, stage):
            if s < 0:
                return
            m, k = s, 0
            if s >= LEAD:
                m, k = (s - LEAD) // nmp, (s - LEAD) % nmp
                if k == 0:
                    m += LEAD
            if m < 3 or (m < 6 and isinstance(base, int)):
                stage(base + m, k)
            elif m < 6:
                pl.when(base == 0)(lambda: stage(m, k))

        def first(m, k):
            if k == 1:
                if isinstance(m, int):
                    if m + 1 < 6:
                        z_start(m + 1)
                else:
                    pl.when(m + 1 < 6)(lambda: z_start(m + 1))
            g1(m, k)

        ranged(t - LAG, g2)
        ranged(t, first)
        ranged(t - LAG - DEPTH, g3)
        ranged(t - LAG - DEPTH - 1, g4)

    def complete(j):
        return nmp * (j + 1) + LEAD + LAG + DEPTH

    def release(m):
        g_done(m)
        for device in [to_x, to_y] + [to_z(flip_by(z, key)) for key in range(1, nmp)]:
            pl.semaphore_signal(free.at[m], inc=1, device_id=device, device_id_type=MESH)

    def may_send(m):
        pl.semaphore_wait(free.at[m], nmp + 1)

    def r1(m, k):
        t = m * nmp + k
        send(
            W.at[m, k, :, ox, c, :, pl.ds(0, half)],
            W.at[m, k, :, ox, oc, :, pl.ds(0, half)],
            h2s.at[m],
            h2r.at[t],
            to_x,
        )
        send(
            W.at[m, k, oy, :, c, :, pl.ds(half, half)],
            W.at[m, k, oy, :, oc, :, pl.ds(half, half)],
            h2s.at[m],
            h2r.at[t],
            to_y,
        )

    def add_to(dst, src):
        dst[...] = (dst[...].astype(F32) + src[...].astype(F32)).astype(BF16)

    def r2(m, k):
        t = m * nmp + k
        got(W.at[m, k, y, :, oc], h2r.at[t])
        add_to(W.at[m, k, :, x, c, :, pl.ds(0, half)], W.at[m, k, :, x, oc, :, pl.ds(0, half)])
        send(
            W.at[m, k, oy, x, c, :, pl.ds(0, half)],
            W.at[m, k, oy, ox, oc, :, pl.ds(0, half)],
            h1s.at[m],
            h1r.at[t],
            to_y,
        )
        add_to(W.at[m, k, y, :, c, :, pl.ds(half, half)], W.at[m, k, y, :, oc, :, pl.ds(half, half)])
        send(
            W.at[m, k, y, ox, c, :, pl.ds(half, half)],
            W.at[m, k, oy, ox, oc, :, pl.ds(half, half)],
            h1s.at[m],
            h1r.at[t],
            to_x,
        )

    def r3(m, k):
        t = m * nmp + k
        got(W.at[m, k, y, x, oc], h1r.at[t])
        add_to(W.at[m, k, y, x, c, :, pl.ds(0, half)], W.at[m, k, y, ox, oc, :, pl.ds(0, half)])
        add_to(W.at[m, k, y, x, c, :, pl.ds(half, half)], W.at[m, k, oy, x, oc, :, pl.ds(half, half)])

        @pl.when(k != z)
        def _():
            send(W.at[m, k, y, x, c], W.at[m, z, oy, ox, oc], zs.at[m], zr.at[m, z], to_z(k))

    def r4(m):
        sum_ = W[m, z, y, x, c].astype(F32)
        for key in range(1, nmp):
            zz = flip_by(z, key)
            src = W.at[m, zz, oy, ox, oc]
            got(src, zr.at[m, zz])
            sum_ = sum_ + src[...].astype(F32)
        b, j = m // 3, m % 3
        if j == 0:
            WI[b, 0] = sum_[:, 0:third]
            WI[b, 2] = sum_[:, third:2 * third]
            WI[b, 1] = sum_[:, 2 * third:3 * third]
            WO[b] = sum_[:, 3 * third:].T
            result_copy(b, 0).start()
            result_copy(b, 1).start()
        else:
            M[b, (j - 1) * block:j * block] = sum_
            result_copy(b, j + 1).start()

    def result_copy(b, i):
        src = (WI.at[b], WO.at[b], M.at[b, pl.ds(0, block)], M.at[b, pl.ds(block, block)])[i]
        return keep(src, grads_out[b][i], 4 * b + i)

    def r_done(m):
        sent(W.at[m, pl.ds(0, nmp - 1), y, x, c], zs.at[m])
        sent(W.at[m, :, y, x, c], h1s.at[m])
        sent(W.at[m, :, y, :, c], h2s.at[m])

    def chunk(k):
        key, out, weight = nmp - 1 - k, 0, 1
        while weight < nmp:
            out = out + weight * ((z // weight + key // weight) % 2)
            weight *= 2
        return out

    def retreat(u):
        def at(s, stage):
            stage(5 - s // nmp, chunk(s % nmp))

        if isinstance(u, int):
            if u < total:
                at(u, r1)
            if u - LAG_TWO < total:
                at(u - LAG_TWO, r2)
            if u - LAG_THREE < total:
                at(u - LAG_THREE, r3)
            return
        at(u, r1)
        pl.when(u >= LAG_TWO)(lambda: at(u - LAG_TWO, r2))
        pl.when(u >= LAG_THREE)(lambda: at(u - LAG_THREE, r3))

    def swap_start(i):
        RB[i, pl.ds(me, 1)] = SB[i, pl.ds(me, 1)]
        for key in range(1, members):
            f = flip_by(me, key)
            send(SB.at[i, f], RB.at[i, me], ts.at[i], tr.at[i], to_member(f))

    def swap_wait(i):
        got(RB.at[i, pl.ds(0, members - 1)], tr.at[i])

    def swap_done(i):
        sent(SB.at[i, pl.ds(0, members - 1)], ts.at[i])

    def rows_of(ref, i):
        return ref[i].reshape(rows, d)

    for key in range(1, nmp):
        ref = SG.at[z, y, x, c]
        send(ref, ref, vs.at[0], vr.at[0], to_z(flip_by(z, key)))
    z_start(0)
    advance(0)
    advance(1)
    own_shards(1)
    got(SG.at[pl.ds(0, nmp - 1), y, x, c], vr.at[0])
    ref = SG.at[:, y, x, c]
    send(ref, ref, vs.at[1], vr.at[1], to_x)
    swap = swap_ref[...]
    keep(x_ref, ACC, 8).wait()
    H[0] = exact(swap.astype(F32), ACC[...], ((1,), (0,)))
    advance(2)
    got(SG.at[:, y, ox, c], vr.at[1])
    ref = SG.at[:, y, :, c]
    send(ref, ref, vs.at[2], vr.at[2], to_y)
    advance(3)
    got(SG.at[:, oy, :, c], vr.at[2])
    ref = SG.at[:, :, :, c]
    send(ref, ref, vs.at[3], vr.at[3], to_c)
    advance(4)
    got(SG.at[:, :, :, oc], vr.at[3])

    lane = lax.broadcasted_iota(jnp.int32, (1, d), 1)
    tall = SG[...].reshape(nmp * per * 16, 128)
    spread = mm(tall, tiles_ref[0]).reshape(nmp * per, 16, d)
    spread = jnp.sum(spread * mask_ref[0:nmp * per].reshape(nmp * per, 1, d), axis=0)
    SV[0, 0:6] = spread[0:6]
    SV[1, 0:6] = spread[6:12]
    is_q = (lane < third).astype(F32)
    is_v = jnp.logical_and(lane >= third, lane < 2 * third).astype(F32)
    spread_in = mm(tall, tiles_ref[1]).reshape(nmp, per, 16, d)
    spread_up = mm(tall, tiles_ref[2]).reshape(nmp, per, 16, d)
    mask_in = mask_ref[nmp * per:nmp * per + per].reshape(per, 1, d)
    mask_up = mask_ref[nmp * per + per:nmp * per + 2 * per].reshape(per, 1, d)
    for k in range(nmp):
        one = jnp.sum(spread_in[k] * mask_in, axis=0)
        two = jnp.sum(spread_up[k] * mask_up, axis=0)
        for b in range(2):
            BI[b, k] = one[12 + 2 * b:13 + 2 * b] * is_q + one[13 + 2 * b:14 + 2 * b] * is_v
            BU[b, k] = two[b:b + 1]
    for t in range(5, complete(0) + 1):
        advance(t)

    lane2 = lax.broadcasted_iota(jnp.int32, (1, 256), 1)
    heads = third // HEAD

    def head_mask(lead):
        return jnp.logical_and(lane2 >= lead * HEAD, lane2 < lead * HEAD + HEAD).astype(F32).astype(BF16)

    q_masks = [head_mask(h) for h in range(heads)]
    v_masks = [head_mask(h + 1) for h in range(heads)]
    scale = HEAD ** (-0.5)
    wide = 5 * 128

    def flat(values):
        return values.reshape(d, values.shape[-1])

    def lower(values):
        return values.reshape(half, values.shape[-1])

    def tall_view(values):
        return values.T.astype(BF16).reshape(2, 2, 2, d // per, rows)

    def to_sibling(src, dst, n):
        send(src, dst, ss.at[n], sr.at[n], to_c)

    def early_to_sibling(b):
        to_sibling(HID.at[b], HS, 0)
        to_sibling(NT.at[b, 0, :, :, oc], LS.at[0], 1)
        to_sibling(NT.at[b, 1, :, :, oc], LS.at[1], 2)
        to_sibling(CT.at[b], CS, 3)

    def take_grad(b):
        grad = GR[...]
        SGR[pl.ds(16 * b + 5, 1)] = jnp.sum(grad, axis=0, keepdims=True)
        NB[...] = grad.astype(BF16)
        GT[0] = tall_view(grad)
        to_sibling(GT.at[0, :, :, oc], LS.at[2], 4)

    def shrink(b, k):
        hidden_grad = mm(NB[...], flat(W[3 * b + 2, k]))
        upper_grad = (GP[b, k].astype(F32) * hidden_grad).astype(BF16)
        GP[b, k] = upper_grad
        to_sibling(GP.at[b, k], US.at[k], 6)
        SGR[pl.ds(16 * b + 10 + k, 1)] = jnp.sum(upper_grad.astype(F32), axis=0, keepdims=True)

    def forward(b, _):
        m = 3 * b
        h = H[b]
        unit, _s = unit_rows(h)
        normed = unit * SV[b, 0:1] + SV[b, 1:2]
        NB[...] = normed.astype(BF16)
        NT[b, 0] = tall_view(normed)
        ACC[...] = h + SV[b, 2:3]

        def attend(k, _):
            packed = (mm(NB[...], flat(W[m, k, :, :, :, :, 0:wide])) + BI[b, k, :, 0:wide]).astype(BF16)
            PK[b, k] = packed
            qs = packed[:, 0:256] * BF16(scale)
            vv = packed[:, 128:384]
            kk = packed[:, 384:640]
            mixed = jnp.zeros((rows, 256), F32)
            for h in range(heads):
                scores = mm_t(qs * q_masks[h], kk)
                expo = jnp.exp(scores - jnp.max(scores, axis=-1, keepdims=True))
                probs = (expo * (1.0 / jnp.sum(expo, axis=-1, keepdims=True))).astype(BF16)
                PR[b, k, h] = probs
                mixed += mm(probs, vv * v_masks[h])
            mixed = mixed.astype(BF16)
            CT[b, k] = mixed
            ACC[...] += mm_t(mixed, flat(W[m, k, :, :, :, :, d - 256:d]))
            return 0

        lax.fori_loop(0, nmp, attend, 0)
        for t in range(complete(0) + 1, complete(1) + 1):
            advance(t, m)
        middle = ACC[...]
        M[b] = middle
        unit, _s = unit_rows(middle)
        normed = unit * SV[b, 3:4] + SV[b, 4:5]
        NB[...] = normed.astype(BF16)
        NT[b, 1] = tall_view(normed)
        ACC[...] = middle + SV[b, 5:6]

        def expand(k, _):
            upper = mm(NB[...], flat(W[m + 1, k])) + BU[b, k]
            cdf = 0.5 + 0.5 * lax.erf(upper * (0.5 ** 0.5))
            HID[b, k] = (upper * cdf).astype(BF16)
            density = jnp.exp(-0.5 * upper * upper) * ((2 * np.pi) ** -0.5)
            GP[b, k] = (cdf + upper * density).astype(BF16)
            return 0

        lax.fori_loop(0, nmp, expand, 0)

        @pl.when(b == 0)
        def _():
            keep(ct_ref, GR, 9).wait()
            picked = (swap.astype(F32) * bits_ref[...].astype(F32)).astype(BF16)
            SB[0] = mm(picked, GR[...].astype(BF16)).astype(BF16).reshape(members, rows // members, d)
            swap_start(0)

        @pl.when(b == 1)
        def _():
            early_to_sibling(1)
            swap_wait(0)
            GR[...] = rows_of(RB, 0).astype(F32)
            take_grad(1)

        def contract(k):
            pl.when(b == 1)(lambda: shrink(1, k))
            ACC[...] += mm_t(HID[b, k], flat(W[m + 2, k]))

        contract(z)
        for t in range(complete(1) + 1, complete(2) + 1):
            advance(t, m)
            if t > complete(2) - nmp + 1:
                contract(flip_by(z, t - complete(2) + nmp - 1))
        SB[1 + b] = ACC[...].astype(BF16).reshape(members, rows // members, d)
        swap_start(1 + b)
        for t in range(complete(2) + 1, complete(3) + 1):
            advance(t, m)

        @pl.when(b == 0)
        def _():
            swap_wait(1)
            H[1] = rows_of(RB, 1).astype(F32)
        return 0

    lax.fori_loop(0, 2, forward, 0)

    def norm_back(grad, start, gain):
        unit, scale = unit_rows(start)
        lifted = grad * gain
        back = scale * (
            lifted
            - jnp.mean(lifted, axis=-1, keepdims=True)
            - unit * jnp.mean(lifted * unit, axis=-1, keepdims=True)
        )
        return back, jnp.sum(grad * unit, axis=0, keepdims=True), jnp.sum(grad, axis=0, keepdims=True)

    def deal():
        rows_ = []
        for zz in range(nmp):
            own = mask_ref[zz * per:zz * per + per].reshape(per, 1, d)
            plain = jnp.concatenate([SGR[0:6], SGR[16:22]], axis=0).reshape(1, 12, d) * own
            pair = jnp.concatenate([SGR[6 + zz:7 + zz], SGR[22 + zz:23 + zz]], axis=0).reshape(1, 2, d) * mask_in
            up = jnp.concatenate([SGR[10 + zz:11 + zz], SGR[26 + zz:27 + zz]], axis=0).reshape(1, 2, d) * mask_up
            rows_ = jnp.concatenate([plain, pair, up], axis=1).reshape(per * 16, d)
            high = rows_.astype(BF16)
            rest = (rows_ - high.astype(F32)).astype(BF16)
            line = lax.broadcasted_iota(jnp.int32, (per, 16, 128), 1)
            parts = [
                (mm_t(high, tiles_ref[i]) + mm_t(rest, tiles_ref[i])).reshape(per, 16, 128) for i in (0, 3, 2)
            ]
            XS[zz] = jnp.where(line < 12, parts[0], jnp.where(line < 14, parts[1], parts[2]))
        for key in range(1, nmp * per):
            qq, zz = peer(key)
            send(XS.at[zz, qq], XR.at[key], rs.at[0], rr.at[0], to_peer(key))

    def backward(step, _):
        b = 1 - step
        m = 3 * b
        row = 16 * b

        @pl.when(step == 1)
        def _():
            pl.semaphore_wait(free_c, 1)
            early_to_sibling(b)
            take_grad(b)

            def shrink_all(k, _):
                shrink(b, k)
                return 0

            lax.fori_loop(0, nmp, shrink_all, 0)

        release(m + 2)
        got(HS, sr.at[0])
        got(LS.at[2], sr.at[4])
        may_send(m + 2)

        def down_grad(step_k, _):
            k = chunk(step_k)
            own = mm(lower(GT[0, :, :, c]), HID[b, k]) + mm(lower(LS[2]), HS[k])
            W[m + 2, k, :, :, c] = own.astype(BF16).reshape(2, 2, d // per, d)
            retreat(3 * nmp * step + step_k)
            return 0

        lax.fori_loop(0, nmp, down_grad, 0)
        pl.when(step == 1)(lambda: r4(5))
        ACC[...] = jnp.zeros_like(ACC)

        def spread_up(k, _):
            ACC[...] += mm_t(GP[b, k], flat(W[m + 1, k]))
            return 0

        lax.fori_loop(0, nmp, spread_up, 0)
        release(m + 1)
        got(US, sr.at[6])
        got(LS.at[1], sr.at[2])
        may_send(m + 1)

        def up_grad(step_k, _):
            k = chunk(step_k)
            own = mm(lower(NT[b, 1, :, :, c]), GP[b, k]) + mm(lower(LS[1]), US[k])
            W[m + 1, k, :, :, c] = own.astype(BF16).reshape(2, 2, d // per, d)
            retreat(3 * nmp * step + nmp + step_k)
            return 0

        lax.fori_loop(0, nmp, up_grad, 0)
        pl.when(step == 1)(lambda: r4(4))
        back, gain_grad, bias_grad = norm_back(ACC[...], M[b], SV[b, 3:4])
        SGR[pl.ds(row + 3, 1)] = gain_grad
        SGR[pl.ds(row + 4, 1)] = bias_grad
        middle_grad = GR[...] + back
        GR[...] = middle_grad
        SGR[pl.ds(row + 2, 1)] = jnp.sum(middle_grad, axis=0, keepdims=True)
        NB[...] = middle_grad.astype(BF16)
        GT[1] = tall_view(middle_grad)
        to_sibling(GT.at[1, :, :, oc], LS.at[3], 5)
        ACC[...] = jnp.zeros_like(ACC)
        def attend_back(k, _):
            mixed_grad = mm(NB[...], flat(W[m, k, :, :, :, :, d - 256:d])).astype(BF16)
            packed = PK[b, k]
            qs = packed[:, 0:256] * BF16(scale)
            vv = packed[:, 128:384]
            kk = packed[:, 384:640]
            q_grad = jnp.zeros((rows, 256), F32)
            k_grad = jnp.zeros((rows, 256), F32)
            v_grad = jnp.zeros((rows, 256), F32)
            for h in range(heads):
                part = mixed_grad * v_masks[h]
                probs_low = PR[b, k, h]
                probs = probs_low.astype(F32)
                weighted = probs * mm_t(part, vv)
                score_grad = (weighted - probs * jnp.sum(weighted, axis=-1, keepdims=True)).astype(BF16)
                q_grad += mm(score_grad, kk * q_masks[h])
                k_grad += t_mm(score_grad, qs * q_masks[h])
                v_grad += t_mm(probs_low, part)
            q_grad = q_grad * scale
            packed_grad = jnp.concatenate(
                [q_grad[:, 0:128], q_grad[:, 128:256] + v_grad[:, 0:128], v_grad[:, 128:256], k_grad], axis=1
            ).astype(BF16)
            PK[b, k] = packed_grad
            to_sibling(PK.at[b, k], PS.at[k], 7)
            SGR[pl.ds(row + 6 + k, 1), 0:wide] = jnp.sum(packed_grad.astype(F32), axis=0, keepdims=True)
            ACC[...] += mm_t(packed_grad, flat(W[m, k, :, :, :, :, 0:wide]))
            return 0

        lax.fori_loop(0, nmp, attend_back, 0)
        release(m)
        back, gain_grad, bias_grad = norm_back(ACC[...], H[b], SV[b, 0:1])
        SGR[pl.ds(row, 1)] = gain_grad
        SGR[pl.ds(row + 1, 1)] = bias_grad
        GR[...] = GR[...] + back

        @pl.when(step == 0)
        def _():
            SB[3] = GR[...].astype(BF16).reshape(members, rows // members, d)
            swap_start(3)

        pl.when(step == 1)(deal)
        got(PS, sr.at[7])
        got(LS.at[0], sr.at[1])
        got(LS.at[3], sr.at[5])
        got(CS, sr.at[3])
        may_send(m)

        def in_grad(step_k, _):
            k = chunk(step_k)
            one = mm(lower(NT[b, 0, :, :, c]), PK[b, k]) + mm(lower(LS[0]), PS[k])
            two = mm(lower(GT[1, :, :, c]), CT[b, k]) + mm(lower(LS[3]), CS[k])
            own = jnp.concatenate(
                [one[:, 0:512], one[:, 512:640] + two[:, 0:128], two[:, 128:256]], axis=1
            ).astype(BF16)
            W[m, k, :, :, c] = own.reshape(2, 2, d // per, d)
            retreat(3 * nmp * step + 2 * nmp + step_k)
            return 0

        lax.fori_loop(0, nmp, in_grad, 0)

        sent(HID.at[b], ss.at[0])
        sent(NT.at[b, 0, :, :, oc], ss.at[1])
        sent(NT.at[b, 1, :, :, oc], ss.at[2])
        sent(CT.at[b], ss.at[3])
        sent(GT.at[0, :, :, oc], ss.at[4])
        sent(GT.at[1, :, :, oc], ss.at[5])
        sent(GP.at[b], ss.at[6])
        sent(PK.at[b], ss.at[7])

        @pl.when(step == 0)
        def _():
            pl.semaphore_signal(free_c, inc=1, device_id=to_c, device_id_type=MESH)

        pl.when(step == 1)(lambda: r4(3))

        @pl.when(step == 0)
        def _():
            swap_wait(3)
            GR[...] = rows_of(RB, 3).astype(F32)
        return 0

    lax.fori_loop(0, 2, backward, 0)

    swap_wait(2)
    H[1] = mm(swap, rows_of(RB, 2))
    keep(H.at[1], out_ref, 8).start()
    ACC[...] = exact(swap.astype(F32), GR[...], ((1,), (0,)))
    keep(ACC, ig_ref, 9).start()
    for u in range(total, total + LAG_THREE):
        retreat(u)
    r4(2)
    got(XR.at[pl.ds(1, nmp * per - 1)], rr.at[0])
    sg_ref[...] = XS[z, q] + jnp.sum(XR[1:nmp * per], axis=0)
    r4(1)
    r4(0)
    sent(XR.at[pl.ds(1, nmp * per - 1)], rs.at[0])
    for b in range(2):
        for i in range(4):
            result_copy(b, i).wait()
    keep(H.at[1], out_ref, 8).wait()
    keep(ACC, ig_ref, 9).wait()
    for m in range(6):
        r_done(m)
    for i in range(4):
        swap_done(i)
    sent(SG.at[pl.ds(0, nmp - 1), y, x, c], vs.at[0])
    sent(SG.at[:, y, x, c], vs.at[1])
    sent(SG.at[:, y, :, c], vs.at[2])
    sent(SG.at[:, :, :, c], vs.at[3])


def tables(outer, ndp, nmp, d):
    n = d // (ndp * nmp)
    tiles = np.zeros((4, 128, d), np.float32)
    masks = np.zeros((nmp * INNER + 2 * INNER, d), np.float32)
    for at in range(d):
        i = at % n
        zz = (at // n) % nmp
        pp = at // (n * nmp)
        qq, lo = pp // outer, pp % outer
        tiles[0, lo * n + i, at] = 1
        masks[zz * INNER + qq, at] = 1
    third = d // nmp
    step = third // INNER
    for at in range(2 * third):
        tiles[1, at % step, at] = 1
        tiles[3, at % step + 32 * (at // third), at] = 1
        masks[nmp * INNER + (at % third) // step, at] = 1
    step = d // INNER
    for at in range(d):
        tiles[2, 32 + at % step, at] = 1
        masks[nmp * INNER + INNER + at // step, at] = 1
    return tiles, masks


def turn_table():
    swap = np.zeros((FRAME, FRAME), np.float32)
    across = SIDE // TUBE
    for wr in range(across):
        for i in range(TUBE):
            for wc in range(across):
                for j in range(TUBE):
                    natural = ((wr * TUBE + i) * across + wc) * TUBE + j
                    turned = ((wr * across + wc) * TUBE + i) * TUBE + j
                    swap[turned, natural] = 1
    return swap


def fused(sizes, x, cotangent, bits, matrices, vectors, ndp):
    outer, nmp, d, rows = sizes
    tiles, masks = tables(outer, ndp, nmp, d)
    members = CLIP // FRAME
    vmem = pltpu.VMEM
    dma = pltpu.SemaphoreType.DMA
    regular = pltpu.SemaphoreType.REGULAR
    block = d // INNER
    steps = 6 * nmp
    scratch = [
        vmem((6, nmp, 2, 2, 2, block, d), BF16),
        vmem((nmp, 2, 2, 2, 16, 128), BF16),
        vmem((2, 8, d), F32),
        vmem((2, nmp, 1, d), F32),
        vmem((2, nmp, 1, d), F32),
        vmem((2, rows, d), F32),
        vmem((2, rows, d), F32),
        vmem((rows, d), BF16),
        vmem((2, 2, 2, 2, 2, block, rows), BF16),
        vmem((2, 2, 2, 2, block, rows), BF16),
        vmem((2, nmp, rows, 640), BF16),
        vmem((2, nmp, rows, 256), BF16),
        vmem((2, nmp, rows, d), BF16),
        vmem((2, nmp, rows, d), BF16),
        vmem((2, nmp, d // nmp // HEAD, rows, rows), BF16),
        vmem((rows, d), F32),
        vmem((rows, d), F32),
        vmem((32, d), F32),
        vmem((nmp, INNER, 16, 128), F32),
        vmem((nmp * INNER, 16, 128), F32),
        vmem((4, members, rows // members, d), BF16),
        vmem((4, members, rows // members, d), BF16),
        vmem((nmp, rows, d), BF16),
        vmem((nmp, rows, 256), BF16),
        vmem((nmp, rows, d), BF16),
        vmem((nmp, rows, 640), BF16),
        vmem((4, 2, 2, block, rows), BF16),
        dma((6,)),
        dma((6, nmp)),
        dma((6,)),
        dma((steps,)),
        dma((6,)),
        dma((steps,)),
        dma((6,)),
        dma((steps,)),
        dma((4,)),
        dma((4,)),
        dma((4,)),
        dma((4,)),
        dma((8,)),
        dma((8,)),
        dma((1,)),
        dma((1,)),
        regular((6,)),
        regular,
        vmem((2, 3, block, d // nmp), F32),
        vmem((2, d // nmp, block), F32),
        vmem((16, 128), F32),
        dma((10,)),
    ]
    grads = [
        jax.ShapeDtypeStruct((3, block, d // nmp), F32),
        jax.ShapeDtypeStruct((d // nmp, block), F32),
        jax.ShapeDtypeStruct((block, d), F32),
        jax.ShapeDtypeStruct((block, d), F32),
    ]
    whole = jax.ShapeDtypeStruct((rows, d), F32)
    anywhere = pl.BlockSpec(memory_space=pl.ANY)
    inside = pl.BlockSpec(memory_space=vmem)
    return pl.pallas_call(
        functools.partial(kernel, sizes, len(vectors)),
        out_shape=[whole, whole] + grads + grads + [jax.ShapeDtypeStruct((16, 128), F32)],
        in_specs=[anywhere] * 2 + [inside] + [anywhere] * 8 + [inside] * (len(vectors) + 3),
        out_specs=[anywhere] * 10 + [inside],
        scratch_shapes=scratch,
        compiler_params=pltpu.CompilerParams(
            collective_id=0, has_side_effects=True, vmem_limit_bytes=64 << 20
        ),
        name="two_blocks",
    )(
        x,
        cotangent,
        bits,
        *matrices,
        *vectors,
        jnp.asarray(turn_table(), BF16),
        jnp.asarray(tiles, BF16),
        jnp.asarray(masks, F32),
    )


def settle_kernel(wide, *refs):
    big, sg_ref, outs = refs[:10], refs[10], refs[11:37]
    held, sems = refs[37:47], refs[47]
    copies = []
    for i in range(10):
        copies.append(
            (
                pltpu.make_async_copy(big[i], held[i], sems.at[0, i]),
                pltpu.make_async_copy(held[i], outs[i], sems.at[1, i]),
            )
        )
        copies[i][0].start()
    for b in range(2):
        small = outs[10 + 8 * b:18 + 8 * b]
        for i in range(6):
            small[i][...] = sg_ref[6 * b + i:6 * b + i + 1, 0:wide]
        small[6][0:1] = sg_ref[12 + b:13 + b, 0:wide]
        small[6][1:2] = sg_ref[12 + b:13 + b, 32:32 + wide]
        small[7][...] = sg_ref[14 + b:15 + b, 32:32 + 4 * wide]
    for arrive, leave in copies:
        arrive.wait()
        leave.start()
    for _, leave in copies:
        leave.wait()


def settle(big, sg, wide, ups):
    anywhere = pl.BlockSpec(memory_space=pl.ANY)
    inside = pl.BlockSpec(memory_space=pltpu.VMEM)
    row = jax.ShapeDtypeStruct((1, wide), F32)
    small = [row] * 6 + [jax.ShapeDtypeStruct((2, wide), F32), jax.ShapeDtypeStruct((1, ups), F32)]
    outs = pl.pallas_call(
        functools.partial(settle_kernel, wide),
        out_shape=[jax.ShapeDtypeStruct(v.shape, v.dtype) for v in big] + small + small,
        in_specs=[anywhere] * 10 + [inside],
        out_specs=[anywhere] * 10 + [inside] * 16,
        scratch_shapes=[pltpu.VMEM(v.shape, v.dtype) for v in big] + [pltpu.SemaphoreType.DMA((2, 10))],
        name="settle",
    )(*big, sg)
    return outs[:10], (outs[10:18], outs[18:26])


def shards_of(ndp, nmp, inputs, cotangent, mask_bits, *params):
    frame, tube = params[:12], params[12:]
    d = inputs.shape[1]
    rows = inputs.shape[0]
    outer = ndp // INNER
    groups = [[qq * outer + lo for lo in range(outer)] for qq in range(INNER)]

    def joined(values, axis):
        if outer == 1:
            return values
        return lax.all_gather(values, "dp", axis=axis, tiled=True, axis_index_groups=groups)

    matrices = []
    vectors = []
    for block in (frame, tube):
        matrices += [
            joined(block[2].transpose(1, 0, 2), 1),
            joined(block[4], 1),
            joined(block[8], 0),
            joined(block[10].T, 0),
        ]
        vectors += [joined(block[i][None], 1) for i in (0, 1, 5, 6, 7, 11)]
    vectors += [joined(block[3], 1) for block in (frame, tube)]
    vectors += [joined(block[9][None], 1) for block in (frame, tube)]
    wide, ups = vectors[0].shape[1], vectors[-1].shape[1]
    outs = fused((outer, nmp, d, rows), inputs, cotangent, mask_bits[None], matrices, vectors, ndp)
    big, sg = list(outs[:10]), outs[10]
    if outer == 1:
        big, small = settle(big, sg, wide, ups)
    else:
        low = lax.axis_index("dp") % outer
        sg = lax.psum(sg, "dp", axis_index_groups=groups)

        def piece(values, start, size):
            size = size // outer
            return lax.dynamic_slice_in_dim(values, start + low * size, size, 1)

        small = []
        for b in range(2):
            parts = [piece(sg[6 * b + i:6 * b + i + 1], 0, wide) for i in range(6)]
            pair = sg[12 + b, 0:64].reshape(2, 32)
            small.append(parts + [piece(pair, 0, wide), piece(sg[14 + b:15 + b], 32, ups)])
            for i, axis in enumerate((1, 1, 0, 0)):
                at = 2 + 4 * b + i
                big[at] = lax.psum_scatter(
                    big[at], "dp", scatter_dimension=axis, tiled=True, axis_index_groups=groups
                )
    results = []
    for b in range(2):
        inw, outw, up, down = big[2 + 4 * b:6 + 4 * b]
        rows_ = small[b]
        results += [
            rows_[0].reshape(-1),
            rows_[1].reshape(-1),
            inw.transpose(1, 0, 2),
            rows_[6],
            outw,
            rows_[2].reshape(-1),
            rows_[3].reshape(-1),
            rows_[4].reshape(-1),
            up,
            rows_[7].reshape(-1),
            down.T,
            rows_[5].reshape(-1),
        ]
    return (big[0], big[1]) + tuple(results)


def solution(mesh):
    rows = P(("dp", "mp"), None)
    small = P(("dp", "mp"))
    block = (
        small,
        small,
        P("dp", None, "mp"),
        P(None, ("mp", "dp")),
        P("mp", "dp"),
        small,
        small,
        small,
        P("dp", "mp"),
        P(("mp", "dp")),
        P("mp", "dp"),
        small,
    )
    return jax.shard_map(
        functools.partial(shards_of, mesh.shape["dp"], mesh.shape["mp"]),
        mesh=mesh,
        in_specs=(rows, rows, small) + block + block,
        out_specs=(rows, rows) + block + block,
        check_vma=False,
    )
```

```python
import functools

import jax
import jax.numpy as jnp
import numpy as np
from jax import lax
from jax.experimental import pallas as pl
from jax.experimental.pallas import tpu as pltpu
from jax.sharding import PartitionSpec as P

MESH = pl.DeviceIdType.MESH
HEAD = 64
SIDE = 16
TUBE = 4
FRAME = SIDE * SIDE
CLIP = 4096
EPS = 1e-06
INNER = 8
CUT_LOW = 256
CUT_HIGH = 640
BACK_LOW = 128
BACK_HIGH = 512
LAG = 2
DEPTH = 3
ORDER = (
    [(0, 0), (1, 0), (2, 0), (3, 0)]
    + [(0, 1), (0, 2), (0, 3), (4, 0)]
    + [(1, 1), (1, 2), (1, 3), (5, 0)]
    + [(m, k) for m in (2, 3, 4, 5) for k in (1, 2, 3)]
)
Z_AT = {3: (1,), 5: (2,), 8: (3,), 12: (4,), 16: (5,)}
REST_AT = {3: (0,), 4: (1,), 6: (2,), 9: (3,), 13: (4,), 17: (5,)}
PASS_AT = {3: (0,), 7: (1,), 11: (2,), 14: (3,), 17: (4,), 20: (5,)}
PASS_REST_AT = {5: (0,), 8: (1,), 12: (2,), 15: (3,), 18: (4,), 21: (5,)}
NO_THIRD = (0, 1)
LAG_TWO = 4
LAG_THREE = 7
LAG_FOUR = 9
LAG_JOIN = 12
TAIL_TWO = {20: (16, 17), 21: (18, 19), 22: (20,), 23: (21,), 24: (22,), 25: (23,), 26: ()}
TAIL_THREE = {20: (13, 14), 21: (15, 16), 22: (17, 18), 23: (19, 20), 24: (21,), 25: (22,), 26: (23,)}
TAIL_FOUR = {20: (11, 12), 21: (13, 14), 22: (15, 16), 23: (17, 18), 24: (19, 20), 25: (21,), 26: (22, 23)}
TAIL_JOIN = {20: (), 21: (11,), 22: (), 23: (15,), 24: (), 25: (), 26: ()}
F32 = jnp.float32
BF16 = jnp.bfloat16


def mm(left, right):
    return lax.dot_general(left, right, (((1,), (0,)), ((), ())), preferred_element_type=F32)


def mm_t(left, right):
    return lax.dot_general(left, right, (((1,), (1,)), ((), ())), preferred_element_type=F32)


def t_mm(left, right):
    return lax.dot_general(left, right, (((0,), (0,)), ((), ())), preferred_element_type=F32)


def exact(left, right, dims):
    return lax.dot_general(
        left, right, (dims, ((), ())), precision=lax.Precision.HIGHEST, preferred_element_type=F32
    )


def flip(value, weight):
    bit = (value // weight) % 2
    return value + weight * (1 - 2 * bit)


def flip_by(value, key):
    weight = 1
    while key:
        if key & 1:
            value = flip(value, weight)
        key >>= 1
        weight *= 2
    return value


def unit_rows(values):
    center = values - jnp.mean(values, axis=-1, keepdims=True)
    spread = jnp.mean(center * center, axis=-1, keepdims=True)
    scale = lax.rsqrt(spread + EPS)
    return center * scale, scale


def kernel(
    sizes,
    count,
    *refs,
):
    x_ref, ct_ref, bits_ref = refs[:3]
    matrices = (refs[3:7], refs[7:11])
    vectors = refs[11:11 + count]
    swap_ref, tiles_ref, mask_ref, out_ref, ig_ref = refs[11 + count:16 + count]
    grads_out = (refs[16 + count:20 + count], refs[20 + count:24 + count])
    sg_ref = refs[24 + count]
    body(
        sizes, x_ref, ct_ref, bits_ref, matrices, vectors, swap_ref, tiles_ref, mask_ref, out_ref, ig_ref,
        grads_out, sg_ref, *refs[25 + count:]
    )


def body(
    sizes,
    x_ref,
    ct_ref,
    bits_ref,
    matrices,
    vectors,
    swap_ref,
    tiles_ref,
    mask_ref,
    out_ref,
    ig_ref,
    grads_out,
    sg_ref,
    W,
    SG,
    SV,
    BI,
    BU,
    H,
    M,
    NB,
    NT,
    GT,
    PK,
    CT,
    HID,
    GP,
    PR,
    ACC,
    GR,
    SGR,
    XS,
    XR,
    SB,
    RB,
    HS,
    CS,
    US,
    PS,
    LS,
    zs,
    zr,
    zcs,
    zcr,
    zds,
    zdr,
    hcs,
    hcr,
    h1s,
    h1r,
    h2s,
    h2r,
    cs,
    cr,
    vs,
    vr,
    ts,
    tr,
    ss,
    sr,
    rs,
    rr,
    free,
    free_c,
    WI,
    WO,
    SM,
    XC,
    ls,
):
    outer, nmp, d, rows = sizes
    per = INNER
    half = d // 2
    dp = lax.axis_index("dp")
    z = lax.axis_index("mp")
    low = dp % outer
    q = dp // outer
    c = q % 2
    x = (q // 2) % 2
    y = q // 4
    oc, ox, oy = 1 - c, 1 - x, 1 - y
    members = CLIP // FRAME
    dpc = members // nmp
    me = (dp % dpc) * nmp + z

    def place(cc, xx, yy):
        return (yy * 4 + xx * 2 + cc) * outer + low

    assert nmp == 4
    z1, z2, z3 = flip_by(z, 1), flip_by(z, 2), flip_by(z, 3)
    across = 2 - z // 2
    inner = jnp.logical_or(z == 1, z == 2)
    outermost = jnp.logical_not(inner)

    to_c = (place(oc, x, y), z)
    to_x = (place(c, ox, y), z)
    to_y = (place(c, x, oy), z)

    def to_z(zz):
        return (dp, zz)

    def peer(key):
        return flip_by(q, key // nmp), flip_by(z, key % nmp)

    def to_peer(key):
        qq, zz = peer(key)
        return (qq * outer + low, zz)

    def to_member(f):
        return ((dp // dpc) * dpc + f // nmp, f % nmp)

    def send(src, dst, s_sem, r_sem, device):
        pltpu.make_async_remote_copy(
            src_ref=src, dst_ref=dst, send_sem=s_sem, recv_sem=r_sem, device_id=device, device_id_type=MESH
        ).start()

    def sent(src, s_sem):
        pltpu.make_async_remote_copy(
            src_ref=src, dst_ref=src, send_sem=s_sem, recv_sem=s_sem, device_id=to_c, device_id_type=MESH
        ).wait_send()

    def got(dst, r_sem):
        pltpu.make_async_remote_copy(
            src_ref=dst, dst_ref=dst, send_sem=r_sem, recv_sem=r_sem, device_id=to_c, device_id_type=MESH
        ).wait_recv()

    def keep(src, dst, n):
        return pltpu.make_async_copy(src, dst, ls.at[n])

    block = d // per
    third = d // nmp

    def matrix_copies(b):
        inw, outw, up, down = matrices[b]
        return (
            keep(inw, WI.at[b], 4 * b),
            keep(outw, WO.at[b], 4 * b + 1),
            keep(up, M.at[b, pl.ds(0, block)], 4 * b + 2),
            keep(down, M.at[b, pl.ds(block, block)], 4 * b + 3),
        )

    for b in range(2):
        for copy in matrix_copies(b):
            copy.start()
    keep(x_ref, ACC, 8).start()
    keep(ct_ref, GR, 9).start()

    barrier = pltpu.get_barrier_semaphore()
    greeted = [to_peer(key) for key in range(1, nmp * per)]
    if outer > 1:
        greeted += [to_member(flip_by(me, key)) for key in range(1, members)]
    for device in greeted:
        pl.semaphore_signal(barrier, inc=1, device_id=device, device_id_type=MESH)
    SM[...] = jnp.zeros_like(SM)
    narrow = 0
    for i, ref in enumerate(vectors[:12]):
        narrow = ref.shape[1]
        SM[i:i + 1, 0:narrow] = ref[...]
    for i, ref in enumerate(vectors[12:14]):
        SM[12 + 2 * i:14 + 2 * i, 0:narrow] = ref[...]
    for i, ref in enumerate(vectors[14:16]):
        SM[i:i + 1, 32:32 + ref.shape[1]] = ref[...]
    SG[z, y, x, c] = SM[...].astype(BF16)

    def own_shards(b):
        copies = matrix_copies(b)
        copies[0].wait()
        copies[1].wait()
        parts = [WI[b, 0], WI[b, 2], WI[b, 1], WO[b].T]
        W[3 * b, z, y, x, c] = jnp.concatenate(parts, axis=1).astype(BF16)
        copies[2].wait()
        W[3 * b + 1, z, y, x, c] = M[b, 0:block].astype(BF16)
        copies[3].wait()
        W[3 * b + 2, z, y, x, c] = M[b, block:2 * block].astype(BF16)

    own_shards(0)
    pl.semaphore_wait(barrier, len(greeted))

    part_one, part_two = pl.ds(0, half), pl.ds(half, half)
    part_ab = pl.ds(CUT_LOW, CUT_HIGH - CUT_LOW)
    part_a, part_b = pl.ds(CUT_LOW, half - CUT_LOW), pl.ds(half, CUT_HIGH - half)
    part_c, part_d = pl.ds(0, CUT_LOW), pl.ds(CUT_HIGH, d - CUT_HIGH)

    def sides(m, zz):
        return W.at[m, zz, y, :, c, :, part_c], W.at[m, zz, :, x, c, :, part_d]

    def sides_size(m, count):
        return W.at[m, pl.ds(0, count), y, :, c, :, pl.ds(0, CUT_LOW + d - CUT_HIGH)]

    def z_start(m):
        ref = W.at[m, z, y, x, c, :, part_ab]
        for zz in (z1, across):
            send(ref, ref, zs.at[m], zr.at[m, z], to_z(zz))

    def z_pass(m):
        @pl.when(inner)
        def _():
            for zz in (z3, z2):
                ref = W.at[m, zz, y, x, c, :, part_ab]
                got(ref, zr.at[m, zz])
                send(ref, ref, zs.at[m], zr.at[m, zz], to_z(z1))

    def z_rest(m):
        for ref in sides(m, z):
            for zz in (z1, across):
                send(ref, ref, zcs.at[m], zcr.at[m, z], to_z(zz))

    def z_pass_rest(m):
        @pl.when(inner)
        def _():
            for zz in (z3, z2):
                got(sides_size(m, 1), zcr.at[m, zz])
                for ref in sides(m, zz):
                    send(ref, ref, zcs.at[m], zcr.at[m, zz], to_z(z1))

    def arrived(k, ref, sem):
        if k == 1:
            got(ref, sem)
        elif k > 1:
            pl.when(outermost)(lambda: got(ref, sem))

    def g1(m, k):
        zz = flip_by(z, k)
        arrived(k, W.at[m, zz, y, x, c, :, part_ab], zr.at[m, zz])
        t = m * nmp + k
        one = W.at[m, zz, y, x, c, :, part_a if k else part_one]
        two = W.at[m, zz, y, x, c, :, part_b if k else part_two]
        send(one, one, h1s.at[m], h1r.at[t], to_x)
        send(two, two, h1s.at[m], h1r.at[t], to_y)

    def g2(m, k):
        zz = flip_by(z, k)
        t = m * nmp + k
        if k:
            got(W.at[m, zz, oy, ox, c, :, part_ab], h1r.at[t])
        else:
            got(W.at[m, zz, oy, ox, c], h1r.at[t])
        arrived(k, sides_size(m, 1), zcr.at[m, zz])
        one = W.at[m, zz, y, :, c, :, part_one]
        two = W.at[m, zz, :, x, c, :, part_two]
        send(one, one, h2s.at[m], h2r.at[t], to_y)
        send(two, two, h2s.at[m], h2r.at[t], to_x)

    def g3(m, k):
        zz = flip_by(z, k)
        t = m * nmp + k
        got(W.at[m, zz, oy, :, c], h2r.at[t])
        whole = W.at[m, zz, :, :, c]
        send(whole, whole, cs.at[m], cr.at[t], to_c)

    def g4(m, k):
        zz = flip_by(z, k)
        t = m * nmp + k
        got(W.at[m, zz, :, :, oc], cr.at[t])

    def g_done(m):
        for number, which in ((2, outermost), (4, inner)):

            @pl.when(which)
            def _(number=number):
                sent(W.at[m, pl.ds(0, number), y, x, c, :, part_ab], zs.at[m])
                sent(sides_size(m, number), zcs.at[m])

        sent(W.at[m, pl.ds(0, nmp - 1), y, x, c, :, part_ab], h1s.at[m])
        sent(W.at[m, z, y, x, c], h1s.at[m])
        sent(W.at[m, :, y, :, c], h2s.at[m])
        sent(W.at[m, :, :, :, c], cs.at[m])

    total = 6 * nmp

    def advance(t):
        def at(s, stage):
            if 0 <= s < total:
                stage(*ORDER[s])

        at(t - LAG, g2)
        for m in REST_AT.get(t, ()):
            z_rest(m)
        for table, stage in ((Z_AT, z_start), (PASS_AT, z_pass), (PASS_REST_AT, z_pass_rest)):
            for m in table.get(t, ()):
                stage(m)
        at(t, g1)
        at(t - LAG - DEPTH, g3)
        at(t - LAG - DEPTH - 1, g4)

    def here(m, k=None):
        keys = [k] if k is not None else range(nmp)
        return max(ORDER.index((m, key)) for key in keys) + LAG + DEPTH + 1

    back_a, back_b = pl.ds(BACK_LOW, half - BACK_LOW), pl.ds(half, BACK_HIGH - half)
    back_ab = pl.ds(BACK_LOW, BACK_HIGH - BACK_LOW)
    back_c, back_d = pl.ds(0, BACK_LOW), pl.ds(BACK_HIGH, d - BACK_HIGH)

    def release(m):
        g_done(m)
        for device in [to_x, to_y] + [to_z(flip_by(z, key)) for key in range(1, nmp)]:
            pl.semaphore_signal(free.at[m], inc=1, device_id=device, device_id_type=MESH)

    def may_send(m):
        pl.semaphore_wait(free.at[m], nmp + 1)

    def z_first(m, k, ref, dst, s_sem, r_sem):
        @pl.when(jnp.logical_and(k != z, jnp.logical_or(outermost, k == z1)))
        def _():
            slot = jnp.where(k == z1, z, jnp.where(k == z3, k, z1))
            send(ref, dst(slot), s_sem.at[m], r_sem.at[m, slot], to_z(z1))

    def z_second(m, k, ref, dst, s_sem, r_sem):
        @pl.when(jnp.logical_and(inner, jnp.logical_or(k == z2, k == z3)))
        def _():
            slot = jnp.where(k == z2, k, z)
            got(dst(slot), r_sem.at[m, slot])
            add_to(ref, dst(slot))
            send(ref, dst(z), s_sem.at[m], r_sem.at[m, z], to_z(k))

    def chunk_refs(m, k, part):
        return (
            W.at[m, k, y, x, c, :, part],
            lambda slot: W.at[m, slot, oy, ox, oc, :, part],
            zs,
            zr,
        )

    def third_refs(m, k):
        return (
            W.at[m, k, :, x, c, :, back_c],
            lambda slot: W.at[m, slot, :, ox, oc, :, back_c],
            zcs,
            zcr,
        )

    def fourth_refs(m, k):
        return (
            W.at[m, k, y, :, c, :, back_d],
            lambda slot: W.at[m, slot, oy, :, oc, :, back_d],
            zds,
            zdr,
        )

    def r1(m, k):
        t = m * nmp + k
        send(
            W.at[m, k, :, ox, c, :, part_one],
            W.at[m, k, :, ox, oc, :, part_one],
            h2s.at[m],
            h2r.at[t],
            to_x,
        )
        send(
            W.at[m, k, oy, :, c, :, part_two],
            W.at[m, k, oy, :, oc, :, part_two],
            h2s.at[m],
            h2r.at[t],
            to_y,
        )

    def either(m, whole, split):
        if isinstance(m, int):
            (whole if m in NO_THIRD else split)()
            return
        chosen = False
        for one in NO_THIRD:
            chosen = jnp.logical_or(chosen, m == one)
        pl.when(chosen)(whole)
        pl.when(jnp.logical_not(chosen))(split)

    def add_to(dst, src):
        dst[...] = (dst[...].astype(F32) + src[...].astype(F32)).astype(BF16)

    def r2(m, k):
        t = m * nmp + k
        got(W.at[m, k, y, :, oc], h2r.at[t])
        add_to(W.at[m, k, :, x, c, :, part_one], W.at[m, k, :, x, oc, :, part_one])
        add_to(W.at[m, k, y, :, c, :, part_two], W.at[m, k, y, :, oc, :, part_two])

        def second(one, two):
            send(W.at[m, k, oy, x, c, :, one], W.at[m, k, oy, ox, oc, :, one], h1s.at[m], h1r.at[t], to_y)
            send(W.at[m, k, y, ox, c, :, two], W.at[m, k, oy, ox, oc, :, two], h1s.at[m], h1r.at[t], to_x)

        def split():
            second(back_a, back_b)
            z_first(m, k, *third_refs(m, k))
            z_first(m, k, *fourth_refs(m, k))

        either(m, lambda: second(part_one, part_two), split)

    def r3(m, k):
        t = m * nmp + k

        def last(part, one, two):
            got(W.at[m, k, y, x, oc, :, part], h1r.at[t])
            add_to(W.at[m, k, y, x, c, :, one], W.at[m, k, y, ox, oc, :, one])
            add_to(W.at[m, k, y, x, c, :, two], W.at[m, k, oy, x, oc, :, two])
            z_first(m, k, *chunk_refs(m, k, part))

        either(m, lambda: last(pl.ds(0, d), part_one, part_two), lambda: last(back_ab, back_a, back_b))

    def r3_more(m, k):
        def split():
            z_second(m, k, *third_refs(m, k))
            z_second(m, k, *fourth_refs(m, k))
            z_second(m, k, *chunk_refs(m, k, back_ab))

        either(m, lambda: z_second(m, k, *chunk_refs(m, k, pl.ds(0, d))), split)

    def join(m):
        for refs, sem in ((third_refs, zcr), (fourth_refs, zdr)):
            own, slots = refs(m, z)[:2]
            mine = own[...].astype(F32)
            for zz in (z1, across):
                got(slots(zz), sem.at[m, zz])
                mine = mine + slots(zz)[...].astype(F32)
            own[...] = mine.astype(BF16)
        send(W.at[m, z, oy, x, c, :, back_c], XC.at[m, :, pl.ds(0, BACK_LOW)], hcs.at[m], hcr.at[m], to_y)
        send(
            W.at[m, z, y, ox, c, :, back_d],
            XC.at[m, :, pl.ds(BACK_LOW, d - BACK_HIGH)],
            hcs.at[m],
            hcr.at[m],
            to_x,
        )

    def r4(m):
        part = pl.ds(0, d) if m in NO_THIRD else back_ab
        sum_ = W[m, z, y, x, c, :, part].astype(F32)
        for zz in (z1, across):
            src = W.at[m, zz, oy, ox, oc, :, part]
            got(src, zr.at[m, zz])
            sum_ = sum_ + src[...].astype(F32)
        if m not in NO_THIRD:
            got(XC.at[m], hcr.at[m])
            low_part = W[m, z, y, x, c, :, back_c].astype(F32) + XC[m, :, 0:BACK_LOW].astype(F32)
            high_part = W[m, z, y, x, c, :, back_d].astype(F32) + XC[m, :, BACK_LOW:].astype(F32)
            sum_ = jnp.concatenate([low_part, sum_, high_part], axis=1)
        b, j = m // 3, m % 3
        if j == 0:
            WI[b, 0] = sum_[:, 0:third]
            WI[b, 2] = sum_[:, third:2 * third]
            WI[b, 1] = sum_[:, 2 * third:3 * third]
            WO[b] = sum_[:, 3 * third:].T
            result_copy(b, 0).start()
            result_copy(b, 1).start()
        else:
            M[b, (j - 1) * block:j * block] = sum_
            result_copy(b, j + 1).start()

    def result_copy(b, i):
        src = (WI.at[b], WO.at[b], M.at[b, pl.ds(0, block)], M.at[b, pl.ds(block, block)])[i]
        return keep(src, grads_out[b][i], 4 * b + i)

    def r_done(m):
        part = pl.ds(0, d) if m in NO_THIRD else back_ab
        sent(W.at[m, pl.ds(0, nmp - 1), y, x, c, :, part], zs.at[m])
        sent(W.at[m, :, y, x, c, :, part], h1s.at[m])
        sent(W.at[m, :, y, :, c], h2s.at[m])
        if m not in NO_THIRD:
            sent(W.at[m, pl.ds(0, nmp - 1), y, :, c, :, back_c], zcs.at[m])
            sent(W.at[m, pl.ds(0, nmp - 1), y, :, c, :, back_d], zds.at[m])
            sent(XC.at[m], hcs.at[m])

    def chunk(k):
        key, out, weight = nmp - 1 - k, 0, 1
        key = jnp.where(jnp.logical_and(inner, key > 1), 5 - key, key)
        while weight < nmp:
            out = out + weight * ((z // weight + key // weight) % 2)
            weight *= 2
        return out

    def join_any(m, k):
        if isinstance(m, int):
            if m not in NO_THIRD:
                join(m)
        else:
            either(m, lambda: None, lambda: join(m))

    def retreat(u):
        def at(s, stage):
            stage(5 - s // nmp, chunk(s % nmp))

        if isinstance(u, int):
            for v in TAIL_TWO[u]:
                at(v, r2)
            if u < total:
                at(u, r1)
            for v in TAIL_THREE[u]:
                at(v, r3)
            for v in TAIL_FOUR[u]:
                at(v, r3_more)
            for v in TAIL_JOIN[u]:
                at(v, join_any)
            return
        early = u < total - nmp
        pl.when(early)(lambda: at(u, r1))
        pl.when(jnp.logical_and(u >= LAG_TWO, early))(lambda: at(u - LAG_TWO, r2))
        pl.when(jnp.logical_and(u >= LAG_THREE, early))(lambda: at(u - LAG_THREE, r3))
        pl.when(jnp.logical_and(u >= LAG_FOUR, early))(lambda: at(u - LAG_FOUR, r3_more))
        own = (u - LAG_JOIN) % nmp == nmp - 1
        pl.when(jnp.logical_and(jnp.logical_and(u >= LAG_JOIN, own), early))(lambda: at(u - LAG_JOIN, join_any))
        for v in range(total - nmp, total):
            pl.when(u == v)(functools.partial(retreat, v))

    def swap_start(i):
        RB[i, pl.ds(me, 1)] = SB[i, pl.ds(me, 1)]
        for key in range(1, members):
            f = flip_by(me, key)
            send(SB.at[i, f], RB.at[i, me], ts.at[i], tr.at[i], to_member(f))

    def swap_wait(i):
        got(RB.at[i, pl.ds(0, members - 1)], tr.at[i])

    def swap_done(i):
        sent(SB.at[i, pl.ds(0, members - 1)], ts.at[i])

    def rows_of(ref, i):
        return ref[i].reshape(rows, d)

    for key in range(1, nmp):
        ref = SG.at[z, y, x, c]
        send(ref, ref, vs.at[0], vr.at[0], to_z(flip_by(z, key)))
    z_start(0)
    advance(0)
    advance(1)
    own_shards(1)
    got(SG.at[pl.ds(0, nmp - 1), y, x, c], vr.at[0])
    ref = SG.at[:, y, x, c]
    send(ref, ref, vs.at[1], vr.at[1], to_x)
    swap = swap_ref[...]
    keep(x_ref, ACC, 8).wait()
    H[0] = exact(swap.astype(F32), ACC[...], ((1,), (0,)))
    advance(2)
    got(SG.at[:, y, ox, c], vr.at[1])
    ref = SG.at[:, y, :, c]
    send(ref, ref, vs.at[2], vr.at[2], to_y)
    advance(3)
    got(SG.at[:, oy, :, c], vr.at[2])
    ref = SG.at[:, :, :, c]
    send(ref, ref, vs.at[3], vr.at[3], to_c)
    advance(4)
    got(SG.at[:, :, :, oc], vr.at[3])

    lane = lax.broadcasted_iota(jnp.int32, (1, d), 1)
    tall = SG[...].reshape(nmp * per * 16, 128)
    spread = mm(tall, tiles_ref[0]).reshape(nmp * per, 16, d)
    spread = jnp.sum(spread * mask_ref[0:nmp * per].reshape(nmp * per, 1, d), axis=0)
    SV[0, 0:6] = spread[0:6]
    SV[1, 0:6] = spread[6:12]
    is_q = (lane < third).astype(F32)
    is_v = jnp.logical_and(lane >= third, lane < 2 * third).astype(F32)
    spread_in = mm(tall, tiles_ref[1]).reshape(nmp, per, 16, d)
    spread_up = mm(tall, tiles_ref[2]).reshape(nmp, per, 16, d)
    mask_in = mask_ref[nmp * per:nmp * per + per].reshape(per, 1, d)
    mask_up = mask_ref[nmp * per + per:nmp * per + 2 * per].reshape(per, 1, d)
    for k in range(nmp):
        one = jnp.sum(spread_in[k] * mask_in, axis=0)
        two = jnp.sum(spread_up[k] * mask_up, axis=0)
        for b in range(2):
            BI[b, k] = one[12 + 2 * b:13 + 2 * b] * is_q + one[13 + 2 * b:14 + 2 * b] * is_v
            BU[b, k] = two[b:b + 1]
    for t in range(5, here(0) + 1):
        advance(t)

    lane2 = lax.broadcasted_iota(jnp.int32, (1, 256), 1)
    heads = third // HEAD

    def head_mask(lead):
        return jnp.logical_and(lane2 >= lead * HEAD, lane2 < lead * HEAD + HEAD).astype(F32).astype(BF16)

    q_masks = [head_mask(h) for h in range(heads)]
    v_masks = [head_mask(h + 1) for h in range(heads)]
    scale = HEAD ** (-0.5)
    wide = 5 * 128

    def flat(values):
        return values.reshape(d, values.shape[-1])

    def lower(values):
        return values.reshape(half, values.shape[-1])

    def tall_view(values):
        return values.T.astype(BF16).reshape(2, 2, 2, d // per, rows)

    def to_sibling(src, dst, n):
        send(src, dst, ss.at[n], sr.at[n], to_c)

    def early_to_sibling(b):
        to_sibling(HID.at[b], HS, 0)
        to_sibling(NT.at[b, 0, :, :, oc], LS.at[0], 1)
        to_sibling(NT.at[b, 1, :, :, oc], LS.at[1], 2)
        to_sibling(CT.at[b], CS, 3)

    def take_grad(b):
        grad = GR[...]
        SGR[pl.ds(16 * b + 5, 1)] = jnp.sum(grad, axis=0, keepdims=True)
        NB[...] = grad.astype(BF16)
        GT[0] = tall_view(grad)
        to_sibling(GT.at[0, :, :, oc], LS.at[2], 4)

    def shrink(b, k):
        hidden_grad = mm(NB[...], flat(W[3 * b + 2, k]))
        upper_grad = (GP[b, k].astype(F32) * hidden_grad).astype(BF16)
        GP[b, k] = upper_grad
        to_sibling(GP.at[b, k], US.at[k], 6)
        SGR[pl.ds(16 * b + 10 + k, 1)] = jnp.sum(upper_grad.astype(F32), axis=0, keepdims=True)

    def forward(b, _):
        m = 3 * b
        ends = [(here(3 * i), here(3 * i + 1), here(3 * i + 2)) for i in range(2)]
        done = [here(0), here(3)]

        def turn(upto):
            for i in range(2):
                steps_ = range(done[i] + 1, upto[i] + 1)
                done[i] = max(done[i], upto[i])
                if len(steps_):
                    pl.when(b == i)(lambda steps_=steps_: [advance(t) for t in steps_] and None)

        def one_of(i):
            return [min(done[0] + 1, ends[0][i]), min(done[1] + 1, ends[1][i])]

        @pl.when(b == 1)
        def _():
            swap_wait(1)
            H[1] = rows_of(RB, 1).astype(F32)

        h = H[b]
        unit, _s = unit_rows(h)
        normed = unit * SV[b, 0:1] + SV[b, 1:2]
        NB[...] = normed.astype(BF16)
        NT[b, 0] = tall_view(normed)
        ACC[...] = h + SV[b, 2:3]

        def attend(k):
            packed = (mm(NB[...], flat(W[m, k, :, :, :, :, 0:wide])) + BI[b, k, :, 0:wide]).astype(BF16)
            PK[b, k] = packed
            qs = packed[:, 0:256] * BF16(scale)
            vv = packed[:, 128:384]
            kk = packed[:, 384:640]
            mixed = jnp.zeros((rows, 256), F32)
            for h in range(heads):
                scores = mm_t(qs * q_masks[h], kk)
                expo = jnp.exp(scores - jnp.max(scores, axis=-1, keepdims=True))
                probs = (expo * (1.0 / jnp.sum(expo, axis=-1, keepdims=True))).astype(BF16)
                PR[b, k, h] = probs
                mixed += mm(probs, vv * v_masks[h])
            mixed = mixed.astype(BF16)
            CT[b, k] = mixed
            ACC[...] += mm_t(mixed, flat(W[m, k, :, :, :, :, d - 256:d]))

        for k in range(nmp):
            attend(k)
            if k % 2 == 1 and k < 4:
                turn(one_of(1))
        middle = ACC[...]
        M[b] = middle
        unit, _s = unit_rows(middle)
        normed = unit * SV[b, 3:4] + SV[b, 4:5]
        NB[...] = normed.astype(BF16)
        NT[b, 1] = tall_view(normed)
        ACC[...] = middle + SV[b, 5:6]

        @pl.when(b == 0)
        def _():
            keep(ct_ref, GR, 9).wait()
            picked = (swap.astype(F32) * bits_ref[...].astype(F32)).astype(BF16)
            SB[0] = mm(picked, GR[...].astype(BF16)).astype(BF16).reshape(members, rows // members, d)
            swap_start(0)

        turn([ends[0][1], ends[1][1]])

        def expand(k):
            upper = mm(NB[...], flat(W[m + 1, k])) + BU[b, k]
            cdf = 0.5 + 0.5 * lax.erf(upper * (0.5 ** 0.5))
            HID[b, k] = (upper * cdf).astype(BF16)
            density = jnp.exp(-0.5 * upper * upper) * ((2 * np.pi) ** -0.5)
            GP[b, k] = (cdf + upper * density).astype(BF16)

        def contract(k):
            pl.when(b == 1)(lambda: shrink(1, k))
            ACC[...] += mm_t(HID[b, k], flat(W[m + 2, k]))

        for k in range(nmp):
            expand(k)
            if k == 1:
                turn(one_of(2))

        @pl.when(b == 1)
        def _():
            early_to_sibling(1)
            swap_wait(0)
            GR[...] = rows_of(RB, 0).astype(F32)
            take_grad(1)

        contract(z)
        for k in range(1, nmp):
            turn([here(2, k), here(5, k)])
            contract(flip_by(z, k))
        SB[1 + b] = ACC[...].astype(BF16).reshape(members, rows // members, d)
        pl.when(b == 0)(lambda: swap_start(1))
        turn([here(3), done[1]])
        return 0

    lax.fori_loop(0, 2, forward, 0)

    def norm_back(grad, start, gain):
        unit, scale = unit_rows(start)
        lifted = grad * gain
        back = scale * (
            lifted
            - jnp.mean(lifted, axis=-1, keepdims=True)
            - unit * jnp.mean(lifted * unit, axis=-1, keepdims=True)
        )
        return back, jnp.sum(grad * unit, axis=0, keepdims=True), jnp.sum(grad, axis=0, keepdims=True)

    def deal():
        rows_ = []
        for zz in range(nmp):
            own = mask_ref[zz * per:zz * per + per].reshape(per, 1, d)
            plain = jnp.concatenate([SGR[0:6], SGR[16:22]], axis=0).reshape(1, 12, d) * own
            pair = jnp.concatenate([SGR[6 + zz:7 + zz], SGR[22 + zz:23 + zz]], axis=0).reshape(1, 2, d) * mask_in
            up = jnp.concatenate([SGR[10 + zz:11 + zz], SGR[26 + zz:27 + zz]], axis=0).reshape(1, 2, d) * mask_up
            rows_ = jnp.concatenate([plain, pair, up], axis=1).reshape(per * 16, d)
            high = rows_.astype(BF16)
            rest = (rows_ - high.astype(F32)).astype(BF16)
            line = lax.broadcasted_iota(jnp.int32, (per, 16, 128), 1)
            parts = [
                (mm_t(high, tiles_ref[i]) + mm_t(rest, tiles_ref[i])).reshape(per, 16, 128) for i in (0, 3, 2)
            ]
            XS[zz] = jnp.where(line < 12, parts[0], jnp.where(line < 14, parts[1], parts[2]))
        for key in range(1, nmp * per):
            qq, zz = peer(key)
            send(XS.at[zz, qq], XR.at[key], rs.at[0], rr.at[0], to_peer(key))

    def backward(step, _):
        b = 1 - step
        m = 3 * b
        row = 16 * b

        @pl.when(step == 1)
        def _():
            pl.semaphore_wait(free_c, 1)
            early_to_sibling(b)
            take_grad(b)

            def shrink_all(k, _):
                shrink(b, k)
                return 0

            lax.fori_loop(0, nmp, shrink_all, 0)

        release(m + 2)
        got(HS, sr.at[0])
        got(LS.at[2], sr.at[4])
        may_send(m + 2)

        def down_grad(step_k, _):
            k = chunk(step_k)
            own = mm(lower(GT[0, :, :, c]), HID[b, k]) + mm(lower(LS[2]), HS[k])
            W[m + 2, k, :, :, c] = own.astype(BF16).reshape(2, 2, d // per, d)
            retreat(3 * nmp * step + step_k)
            return 0

        lax.fori_loop(0, nmp, down_grad, 0)
        pl.when(step == 1)(lambda: swap_start(2))
        ACC[...] = jnp.zeros_like(ACC)

        def spread_up(k, _):
            ACC[...] += mm_t(GP[b, k], flat(W[m + 1, k]))
            return 0

        lax.fori_loop(0, nmp, spread_up, 0)
        release(m + 1)
        got(US, sr.at[6])
        got(LS.at[1], sr.at[2])
        may_send(m + 1)

        def up_grad(step_k, _):
            k = chunk(step_k)
            own = mm(lower(NT[b, 1, :, :, c]), GP[b, k]) + mm(lower(LS[1]), US[k])
            W[m + 1, k, :, :, c] = own.astype(BF16).reshape(2, 2, d // per, d)
            retreat(3 * nmp * step + nmp + step_k)
            return 0

        lax.fori_loop(0, nmp, up_grad, 0)
        pl.when(step == 1)(lambda: r4(5))
        back, gain_grad, bias_grad = norm_back(ACC[...], M[b], SV[b, 3:4])
        SGR[pl.ds(row + 3, 1)] = gain_grad
        SGR[pl.ds(row + 4, 1)] = bias_grad
        middle_grad = GR[...] + back
        GR[...] = middle_grad
        SGR[pl.ds(row + 2, 1)] = jnp.sum(middle_grad, axis=0, keepdims=True)
        NB[...] = middle_grad.astype(BF16)
        GT[1] = tall_view(middle_grad)
        to_sibling(GT.at[1, :, :, oc], LS.at[3], 5)
        ACC[...] = jnp.zeros_like(ACC)
        def attend_back(k, _):
            mixed_grad = mm(NB[...], flat(W[m, k, :, :, :, :, d - 256:d])).astype(BF16)
            packed = PK[b, k]
            qs = packed[:, 0:256] * BF16(scale)
            vv = packed[:, 128:384]
            kk = packed[:, 384:640]
            q_grad = jnp.zeros((rows, 256), F32)
            k_grad = jnp.zeros((rows, 256), F32)
            v_grad = jnp.zeros((rows, 256), F32)
            for h in range(heads):
                part = mixed_grad * v_masks[h]
                probs_low = PR[b, k, h]
                probs = probs_low.astype(F32)
                weighted = probs * mm_t(part, vv)
                score_grad = (weighted - probs * jnp.sum(weighted, axis=-1, keepdims=True)).astype(BF16)
                q_grad += mm(score_grad, kk * q_masks[h])
                k_grad += t_mm(score_grad, qs * q_masks[h])
                v_grad += t_mm(probs_low, part)
            q_grad = q_grad * scale
            packed_grad = jnp.concatenate(
                [q_grad[:, 0:128], q_grad[:, 128:256] + v_grad[:, 0:128], v_grad[:, 128:256], k_grad], axis=1
            ).astype(BF16)
            PK[b, k] = packed_grad
            to_sibling(PK.at[b, k], PS.at[k], 7)
            SGR[pl.ds(row + 6 + k, 1), 0:wide] = jnp.sum(packed_grad.astype(F32), axis=0, keepdims=True)
            ACC[...] += mm_t(packed_grad, flat(W[m, k, :, :, :, :, 0:wide]))
            return 0

        lax.fori_loop(0, nmp, attend_back, 0)
        release(m)
        back, gain_grad, bias_grad = norm_back(ACC[...], H[b], SV[b, 0:1])
        SGR[pl.ds(row, 1)] = gain_grad
        SGR[pl.ds(row + 1, 1)] = bias_grad
        GR[...] = GR[...] + back

        @pl.when(step == 0)
        def _():
            SB[3] = GR[...].astype(BF16).reshape(members, rows // members, d)
            swap_start(3)

        pl.when(step == 1)(deal)
        got(PS, sr.at[7])
        got(LS.at[0], sr.at[1])
        got(LS.at[3], sr.at[5])
        got(CS, sr.at[3])
        may_send(m)

        def in_grad(step_k, _):
            k = chunk(step_k)
            one = mm(lower(NT[b, 0, :, :, c]), PK[b, k]) + mm(lower(LS[0]), PS[k])
            two = mm(lower(GT[1, :, :, c]), CT[b, k]) + mm(lower(LS[3]), CS[k])
            own = jnp.concatenate(
                [one[:, 0:512], one[:, 512:640] + two[:, 0:128], two[:, 128:256]], axis=1
            ).astype(BF16)
            W[m, k, :, :, c] = own.reshape(2, 2, d // per, d)
            retreat(3 * nmp * step + 2 * nmp + step_k)
            return 0

        lax.fori_loop(0, nmp, in_grad, 0)

        sent(HID.at[b], ss.at[0])
        sent(NT.at[b, 0, :, :, oc], ss.at[1])
        sent(NT.at[b, 1, :, :, oc], ss.at[2])
        sent(CT.at[b], ss.at[3])
        sent(GT.at[0, :, :, oc], ss.at[4])
        sent(GT.at[1, :, :, oc], ss.at[5])
        sent(GP.at[b], ss.at[6])
        sent(PK.at[b], ss.at[7])

        @pl.when(step == 0)
        def _():
            pl.semaphore_signal(free_c, inc=1, device_id=to_c, device_id_type=MESH)

        pl.when(step == 1)(lambda: r4(4))

        @pl.when(step == 0)
        def _():
            swap_wait(3)
            GR[...] = rows_of(RB, 3).astype(F32)
        return 0

    lax.fori_loop(0, 2, backward, 0)

    ACC[...] = exact(swap.astype(F32), GR[...], ((1,), (0,)))
    keep(ACC, ig_ref, 9).start()
    swap_wait(2)
    H[1] = mm(swap, rows_of(RB, 2))
    keep(H.at[1], out_ref, 8).start()
    for u in sorted(TAIL_TWO):
        if u >= total:
            retreat(u)
    r4(3)
    r4(2)
    got(XR.at[pl.ds(1, nmp * per - 1)], rr.at[0])
    sg_ref[...] = XS[z, q] + jnp.sum(XR[1:nmp * per], axis=0)
    r4(1)
    r4(0)
    sent(XR.at[pl.ds(1, nmp * per - 1)], rs.at[0])
    for b in range(2):
        for i in range(4):
            result_copy(b, i).wait()
    keep(H.at[1], out_ref, 8).wait()
    keep(ACC, ig_ref, 9).wait()
    for m in range(6):
        r_done(m)
    for i in range(4):
        swap_done(i)
    sent(SG.at[pl.ds(0, nmp - 1), y, x, c], vs.at[0])
    sent(SG.at[:, y, x, c], vs.at[1])
    sent(SG.at[:, y, :, c], vs.at[2])
    sent(SG.at[:, :, :, c], vs.at[3])


def tables(outer, ndp, nmp, d):
    n = d // (ndp * nmp)
    tiles = np.zeros((4, 128, d), np.float32)
    masks = np.zeros((nmp * INNER + 2 * INNER, d), np.float32)
    for at in range(d):
        i = at % n
        zz = (at // n) % nmp
        pp = at // (n * nmp)
        qq, lo = pp // outer, pp % outer
        tiles[0, lo * n + i, at] = 1
        masks[zz * INNER + qq, at] = 1
    third = d // nmp
    step = third // INNER
    for at in range(2 * third):
        tiles[1, at % step, at] = 1
        tiles[3, at % step + 32 * (at // third), at] = 1
        masks[nmp * INNER + (at % third) // step, at] = 1
    step = d // INNER
    for at in range(d):
        tiles[2, 32 + at % step, at] = 1
        masks[nmp * INNER + INNER + at // step, at] = 1
    return tiles, masks


def turn_table():
    swap = np.zeros((FRAME, FRAME), np.float32)
    across = SIDE // TUBE
    for wr in range(across):
        for i in range(TUBE):
            for wc in range(across):
                for j in range(TUBE):
                    natural = ((wr * TUBE + i) * across + wc) * TUBE + j
                    turned = ((wr * across + wc) * TUBE + i) * TUBE + j
                    swap[turned, natural] = 1
    return swap


def fused(sizes, x, cotangent, bits, matrices, vectors, ndp):
    outer, nmp, d, rows = sizes
    tiles, masks = tables(outer, ndp, nmp, d)
    members = CLIP // FRAME
    vmem = pltpu.VMEM
    dma = pltpu.SemaphoreType.DMA
    regular = pltpu.SemaphoreType.REGULAR
    block = d // INNER
    steps = 6 * nmp
    scratch = [
        vmem((6, nmp, 2, 2, 2, block, d), BF16),
        vmem((nmp, 2, 2, 2, 16, 128), BF16),
        vmem((2, 8, d), F32),
        vmem((2, nmp, 1, d), F32),
        vmem((2, nmp, 1, d), F32),
        vmem((2, rows, d), F32),
        vmem((2, rows, d), F32),
        vmem((rows, d), BF16),
        vmem((2, 2, 2, 2, 2, block, rows), BF16),
        vmem((2, 2, 2, 2, block, rows), BF16),
        vmem((2, nmp, rows, 640), BF16),
        vmem((2, nmp, rows, 256), BF16),
        vmem((2, nmp, rows, d), BF16),
        vmem((2, nmp, rows, d), BF16),
        vmem((2, nmp, d // nmp // HEAD, rows, rows), BF16),
        vmem((rows, d), F32),
        vmem((rows, d), F32),
        vmem((32, d), F32),
        vmem((nmp, INNER, 16, 128), F32),
        vmem((nmp * INNER, 16, 128), F32),
        vmem((4, members, rows // members, d), BF16),
        vmem((4, members, rows // members, d), BF16),
        vmem((nmp, rows, d), BF16),
        vmem((nmp, rows, 256), BF16),
        vmem((nmp, rows, d), BF16),
        vmem((nmp, rows, 640), BF16),
        vmem((4, 2, 2, block, rows), BF16),
        dma((6,)),
        dma((6, nmp)),
        dma((6,)),
        dma((6, nmp)),
        dma((6,)),
        dma((6, nmp)),
        dma((6,)),
        dma((6,)),
        dma((6,)),
        dma((steps,)),
        dma((6,)),
        dma((steps,)),
        dma((6,)),
        dma((steps,)),
        dma((4,)),
        dma((4,)),
        dma((4,)),
        dma((4,)),
        dma((8,)),
        dma((8,)),
        dma((1,)),
        dma((1,)),
        regular((6,)),
        regular,
        vmem((2, 3, block, d // nmp), F32),
        vmem((2, d // nmp, block), F32),
        vmem((16, 128), F32),
        vmem((6, block, d - BACK_HIGH + BACK_LOW), BF16),
        dma((10,)),
    ]
    grads = [
        jax.ShapeDtypeStruct((3, block, d // nmp), F32),
        jax.ShapeDtypeStruct((d // nmp, block), F32),
        jax.ShapeDtypeStruct((block, d), F32),
        jax.ShapeDtypeStruct((block, d), F32),
    ]
    whole = jax.ShapeDtypeStruct((rows, d), F32)
    anywhere = pl.BlockSpec(memory_space=pl.ANY)
    inside = pl.BlockSpec(memory_space=vmem)
    return pl.pallas_call(
        functools.partial(kernel, sizes, len(vectors)),
        out_shape=[whole, whole] + grads + grads + [jax.ShapeDtypeStruct((16, 128), F32)],
        in_specs=[anywhere] * 2 + [inside] + [anywhere] * 8 + [inside] * (len(vectors) + 3),
        out_specs=[anywhere] * 10 + [inside],
        scratch_shapes=scratch,
        compiler_params=pltpu.CompilerParams(
            collective_id=0, has_side_effects=True, vmem_limit_bytes=64 << 20
        ),
        name="two_blocks",
    )(
        x,
        cotangent,
        bits,
        *matrices,
        *vectors,
        jnp.asarray(turn_table(), BF16),
        jnp.asarray(tiles, BF16),
        jnp.asarray(masks, F32),
    )


def settle_kernel(wide, *refs):
    big, sg_in, outs = refs[:10], refs[10], refs[11:37]
    held, sg_ref, sems = refs[37:47], refs[47], refs[48]
    small_copy = pltpu.make_async_copy(sg_in, sg_ref, sems.at[0, 10])
    small_copy.start()
    copies = []
    for i in range(10):
        copies.append(
            (
                pltpu.make_async_copy(big[i], held[i], sems.at[0, i]),
                pltpu.make_async_copy(held[i], outs[i], sems.at[1, i]),
            )
        )
        copies[i][0].start()
    small_copy.wait()
    for b in range(2):
        small = outs[10 + 8 * b:18 + 8 * b]
        for i in range(6):
            small[i][...] = sg_ref[6 * b + i:6 * b + i + 1, 0:wide]
        small[6][0:1] = sg_ref[12 + b:13 + b, 0:wide]
        small[6][1:2] = sg_ref[12 + b:13 + b, 32:32 + wide]
        small[7][...] = sg_ref[14 + b:15 + b, 32:32 + 4 * wide]
    for arrive, leave in copies:
        arrive.wait()
        leave.start()
    for _, leave in copies:
        leave.wait()


def settle(big, sg, wide, ups):
    anywhere = pl.BlockSpec(memory_space=pl.ANY)
    inside = pl.BlockSpec(memory_space=pltpu.VMEM)
    row = jax.ShapeDtypeStruct((1, wide), F32)
    small = [row] * 6 + [jax.ShapeDtypeStruct((2, wide), F32), jax.ShapeDtypeStruct((1, ups), F32)]
    outs = pl.pallas_call(
        functools.partial(settle_kernel, wide),
        out_shape=[jax.ShapeDtypeStruct(v.shape, v.dtype) for v in big] + small + small,
        in_specs=[anywhere] * 11,
        out_specs=[anywhere] * 10 + [inside] * 16,
        scratch_shapes=[pltpu.VMEM(v.shape, v.dtype) for v in (*big, sg)]
        + [pltpu.SemaphoreType.DMA((2, 11))],
        name="settle",
    )(*big, sg)
    return outs[:10], (outs[10:18], outs[18:26])


def shards_of(ndp, nmp, inputs, cotangent, mask_bits, *params):
    frame, tube = params[:12], params[12:]
    d = inputs.shape[1]
    rows = inputs.shape[0]
    outer = ndp // INNER
    groups = [[qq * outer + lo for lo in range(outer)] for qq in range(INNER)]

    def joined(values, axis):
        if outer == 1:
            return values
        return lax.all_gather(values, "dp", axis=axis, tiled=True, axis_index_groups=groups)

    matrices = []
    vectors = []
    for block in (frame, tube):
        matrices += [
            joined(block[2].transpose(1, 0, 2), 1),
            joined(block[4], 1),
            joined(block[8], 0),
            joined(block[10].T, 0),
        ]
        vectors += [joined(block[i][None], 1) for i in (0, 1, 5, 6, 7, 11)]
    vectors += [joined(block[3], 1) for block in (frame, tube)]
    vectors += [joined(block[9][None], 1) for block in (frame, tube)]
    wide, ups = vectors[0].shape[1], vectors[-1].shape[1]
    outs = fused((outer, nmp, d, rows), inputs, cotangent, mask_bits[None], matrices, vectors, ndp)
    big, sg = list(outs[:10]), outs[10]
    if outer == 1:
        big, small = settle(big, sg, wide, ups)
    else:
        low = lax.axis_index("dp") % outer
        sg = lax.psum(sg, "dp", axis_index_groups=groups)

        def piece(values, start, size):
            size = size // outer
            return lax.dynamic_slice_in_dim(values, start + low * size, size, 1)

        small = []
        for b in range(2):
            parts = [piece(sg[6 * b + i:6 * b + i + 1], 0, wide) for i in range(6)]
            pair = sg[12 + b, 0:64].reshape(2, 32)
            small.append(parts + [piece(pair, 0, wide), piece(sg[14 + b:15 + b], 32, ups)])
            for i, axis in enumerate((1, 1, 0, 0)):
                at = 2 + 4 * b + i
                big[at] = lax.psum_scatter(
                    big[at], "dp", scatter_dimension=axis, tiled=True, axis_index_groups=groups
                )
    results = []
    for b in range(2):
        inw, outw, up, down = big[2 + 4 * b:6 + 4 * b]
        rows_ = small[b]
        results += [
            rows_[0].reshape(-1),
            rows_[1].reshape(-1),
            inw.transpose(1, 0, 2),
            rows_[6],
            outw,
            rows_[2].reshape(-1),
            rows_[3].reshape(-1),
            rows_[4].reshape(-1),
            up,
            rows_[7].reshape(-1),
            down.T,
            rows_[5].reshape(-1),
        ]
    return (big[0], big[1]) + tuple(results)


def solution(mesh):
    rows = P(("dp", "mp"), None)
    small = P(("dp", "mp"))
    block = (
        small,
        small,
        P("dp", None, "mp"),
        P(None, ("mp", "dp")),
        P("mp", "dp"),
        small,
        small,
        small,
        P("dp", "mp"),
        P(("mp", "dp")),
        P("mp", "dp"),
        small,
    )
    return jax.shard_map(
        functools.partial(shards_of, mesh.shape["dp"], mesh.shape["mp"]),
        mesh=mesh,
        in_specs=(rows, rows, small) + block + block,
        out_specs=(rows, rows) + block + block,
        check_vma=False,
    )
```

```python
import functools

import jax
import jax.numpy as jnp
import numpy as np
from jax import lax
from jax.experimental import pallas as pl
from jax.experimental.pallas import tpu as pltpu
from jax.sharding import PartitionSpec as P

MESH = pl.DeviceIdType.MESH
HEAD = 64
SIDE = 16
TUBE = 4
FRAME = SIDE * SIDE
CLIP = 4096
EPS = 1e-06
INNER = 8
CUT_LOW = 256
CUT_HIGH = 640
BACK_LOW = 128
BACK_HIGH = 512
LAG = 2
DEPTH = 3
ORDER = (
    [(0, 0), (1, 0), (2, 0), (3, 0)]
    + [(m, k) for m in (0, 1) for k in (1, 2, 3)]
    + [(4, 0), (2, 1), (2, 2), (2, 3), (3, 1), (3, 2), (3, 3), (5, 0)]
    + [(m, k) for m in (4, 5) for k in (1, 2, 3)]
)
Z_AT = {2: (1,), 5: (2,), 8: (3,), 12: (4,), 16: (5,)}
REST_AT = {2: (0,), 3: (1,), 5: (2,), 10: (3,), 13: (4,), 19: (5,)}
PASS_AT = {2: (0,), 6: (1,), 10: (2,), 13: (3,), 17: (4,), 20: (5,)}
PASS_REST_AT = {5: (0,), 8: (1,), 12: (2,), 15: (3,), 19: (4,), 22: (5,)}
NO_THIRD = (0, 1)
LAG_TWO = 4
LAG_THREE = 7
LAG_FOUR = 9
LAG_JOIN = 12
TAIL_TWO = {20: (16, 17), 21: (18, 19), 22: (20,), 23: (21,), 24: (22,), 25: (23,), 26: ()}
TAIL_THREE = {20: (13, 14), 21: (15, 16), 22: (17, 18), 23: (19, 20), 24: (21,), 25: (22,), 26: (23,)}
TAIL_FOUR = {20: (11, 12), 21: (13, 14), 22: (15, 16), 23: (17, 18), 24: (19, 20), 25: (21,), 26: (22, 23)}
TAIL_JOIN = {20: (), 21: (11,), 22: (), 23: (15,), 24: (), 25: (), 26: ()}
F32 = jnp.float32
BF16 = jnp.bfloat16


def mm(left, right):
    return lax.dot_general(left, right, (((1,), (0,)), ((), ())), preferred_element_type=F32)


def mm_t(left, right):
    return lax.dot_general(left, right, (((1,), (1,)), ((), ())), preferred_element_type=F32)


def t_mm(left, right):
    return lax.dot_general(left, right, (((0,), (0,)), ((), ())), preferred_element_type=F32)


def exact(left, right, dims):
    return lax.dot_general(
        left, right, (dims, ((), ())), precision=lax.Precision.HIGHEST, preferred_element_type=F32
    )


def flip(value, weight):
    bit = (value // weight) % 2
    return value + weight * (1 - 2 * bit)


def flip_by(value, key):
    weight = 1
    while key:
        if key & 1:
            value = flip(value, weight)
        key >>= 1
        weight *= 2
    return value


def unit_rows(values):
    center = values - jnp.mean(values, axis=-1, keepdims=True)
    spread = jnp.mean(center * center, axis=-1, keepdims=True)
    scale = lax.rsqrt(spread + EPS)
    return center * scale, scale


def kernel(
    sizes,
    count,
    *refs,
):
    x_ref, ct_ref = refs[:2]
    matrices = (refs[3:7], refs[7:11])
    out_ref, ig_ref = refs[14 + count:16 + count]
    grads_out = (refs[16 + count:20 + count], refs[20 + count:24 + count])
    sg_ref = refs[24 + count]
    sources = (refs[2], *refs[11:14 + count])
    held = refs[-len(sources) - 1:-1]
    bits_ref, vectors, (swap_ref, tiles_ref, mask_ref) = held[0], held[1:1 + count], held[1 + count:]
    sems = refs[-1]
    loads = [pltpu.make_async_copy(src, dst, sems.at[i]) for i, (src, dst) in enumerate(zip(sources, held))]
    body(
        sizes, x_ref, ct_ref, bits_ref, matrices, vectors, swap_ref, tiles_ref, mask_ref, out_ref, ig_ref,
        grads_out, sg_ref, loads, *refs[25 + count:-len(sources) - 1]
    )


def body(
    sizes,
    x_ref,
    ct_ref,
    bits_ref,
    matrices,
    vectors,
    swap_ref,
    tiles_ref,
    mask_ref,
    out_ref,
    ig_ref,
    grads_out,
    sg_ref,
    loads,
    W,
    SG,
    SV,
    BI,
    BU,
    H,
    M,
    NB,
    NT,
    GT,
    PK,
    CT,
    HID,
    GP,
    PR,
    ACC,
    GR,
    SGR,
    XS,
    XR,
    SB,
    RB,
    HS,
    CS,
    US,
    PS,
    LS,
    zs,
    zr,
    zcs,
    zcr,
    zds,
    zdr,
    hcs,
    hcr,
    h1s,
    h1r,
    h2s,
    h2r,
    cs,
    cr,
    vs,
    vr,
    ts,
    tr,
    ss,
    sr,
    rs,
    rr,
    free,
    free_c,
    WI,
    WO,
    SM,
    XC,
    ls,
):
    outer, nmp, d, rows = sizes
    per = INNER
    half = d // 2
    dp = lax.axis_index("dp")
    z = lax.axis_index("mp")
    low = dp % outer
    q = dp // outer
    c = q % 2
    x = (q // 2) % 2
    y = q // 4
    oc, ox, oy = 1 - c, 1 - x, 1 - y
    members = CLIP // FRAME
    dpc = members // nmp
    me = (dp % dpc) * nmp + z

    def place(cc, xx, yy):
        return (yy * 4 + xx * 2 + cc) * outer + low

    assert nmp == 4
    z1, z2, z3 = flip_by(z, 1), flip_by(z, 2), flip_by(z, 3)
    across = 2 - z // 2
    inner = jnp.logical_or(z == 1, z == 2)
    outermost = jnp.logical_not(inner)

    to_c = (place(oc, x, y), z)
    to_x = (place(c, ox, y), z)
    to_y = (place(c, x, oy), z)

    def to_z(zz):
        return (dp, zz)

    def peer(key):
        return flip_by(q, key // nmp), flip_by(z, key % nmp)

    def to_peer(key):
        qq, zz = peer(key)
        return (qq * outer + low, zz)

    def to_member(f):
        return ((dp // dpc) * dpc + f // nmp, f % nmp)

    def send(src, dst, s_sem, r_sem, device):
        pltpu.make_async_remote_copy(
            src_ref=src, dst_ref=dst, send_sem=s_sem, recv_sem=r_sem, device_id=device, device_id_type=MESH
        ).start()

    def sent(src, s_sem):
        pltpu.make_async_remote_copy(
            src_ref=src, dst_ref=src, send_sem=s_sem, recv_sem=s_sem, device_id=to_c, device_id_type=MESH
        ).wait_send()

    def got(dst, r_sem):
        pltpu.make_async_remote_copy(
            src_ref=dst, dst_ref=dst, send_sem=r_sem, recv_sem=r_sem, device_id=to_c, device_id_type=MESH
        ).wait_recv()

    def keep(src, dst, n):
        return pltpu.make_async_copy(src, dst, ls.at[n])

    block = d // per
    third = d // nmp

    def matrix_copies(b):
        inw, outw, up, down = matrices[b]
        return (
            keep(inw, WI.at[b], 4 * b),
            keep(outw, WO.at[b], 4 * b + 1),
            keep(up, M.at[b, pl.ds(0, block)], 4 * b + 2),
            keep(down, M.at[b, pl.ds(block, block)], 4 * b + 3),
        )

    barrier = pltpu.get_barrier_semaphore()
    greeted = [to_peer(key) for key in range(1, nmp * per)]
    if outer > 1:
        greeted += [to_member(flip_by(me, key)) for key in range(1, members)]
    for device in greeted:
        pl.semaphore_signal(barrier, inc=1, device_id=device, device_id_type=MESH)
    for copy in loads[1:-3]:
        copy.start()
    for b in range(2):
        for copy in matrix_copies(b):
            copy.start()
    keep(x_ref, ACC, 8).start()
    keep(ct_ref, GR, 9).start()
    for copy in [*loads[-3:], loads[0]]:
        copy.start()
    SM[...] = jnp.zeros_like(SM)
    for copy in loads[1:-3]:
        copy.wait()
    narrow = 0
    for i, ref in enumerate(vectors[:12]):
        narrow = ref.shape[1]
        SM[i:i + 1, 0:narrow] = ref[...]
    for i, ref in enumerate(vectors[12:14]):
        SM[12 + 2 * i:14 + 2 * i, 0:narrow] = ref[...]
    for i, ref in enumerate(vectors[14:16]):
        SM[i:i + 1, 32:32 + ref.shape[1]] = ref[...]
    SG[z, y, x, c] = SM[...].astype(BF16)

    def own_shards(b):
        copies = matrix_copies(b)
        copies[0].wait()
        copies[1].wait()
        parts = [WI[b, 0], WI[b, 2], WI[b, 1], WO[b].T]
        W[3 * b, z, y, x, c] = jnp.concatenate(parts, axis=1).astype(BF16)
        copies[2].wait()
        W[3 * b + 1, z, y, x, c] = M[b, 0:block].astype(BF16)
        copies[3].wait()
        W[3 * b + 2, z, y, x, c] = M[b, block:2 * block].astype(BF16)

    own_shards(0)
    pl.semaphore_wait(barrier, len(greeted))

    part_one, part_two = pl.ds(0, half), pl.ds(half, half)
    part_ab = pl.ds(CUT_LOW, CUT_HIGH - CUT_LOW)
    part_a, part_b = pl.ds(CUT_LOW, half - CUT_LOW), pl.ds(half, CUT_HIGH - half)
    part_c, part_d = pl.ds(0, CUT_LOW), pl.ds(CUT_HIGH, d - CUT_HIGH)

    def sides(m, zz):
        return W.at[m, zz, y, :, c, :, part_c], W.at[m, zz, :, x, c, :, part_d]

    def sides_size(m, count):
        return W.at[m, pl.ds(0, count), y, :, c, :, pl.ds(0, CUT_LOW + d - CUT_HIGH)]

    def z_start(m):
        ref = W.at[m, z, y, x, c, :, part_ab]
        for zz in (z1, across):
            send(ref, ref, zs.at[m], zr.at[m, z], to_z(zz))

    def z_pass(m):
        @pl.when(inner)
        def _():
            for zz in (z3, z2):
                ref = W.at[m, zz, y, x, c, :, part_ab]
                got(ref, zr.at[m, zz])
                send(ref, ref, zs.at[m], zr.at[m, zz], to_z(z1))

    def z_rest(m):
        for ref in sides(m, z):
            for zz in (z1, across):
                send(ref, ref, zcs.at[m], zcr.at[m, z], to_z(zz))

    def z_pass_rest(m):
        @pl.when(inner)
        def _():
            for zz in (z3, z2):
                got(sides_size(m, 1), zcr.at[m, zz])
                for ref in sides(m, zz):
                    send(ref, ref, zcs.at[m], zcr.at[m, zz], to_z(z1))

    def arrived(k, ref, sem):
        if k == 1:
            got(ref, sem)
        elif k > 1:
            pl.when(outermost)(lambda: got(ref, sem))

    def g1(m, k):
        zz = flip_by(z, k)
        arrived(k, W.at[m, zz, y, x, c, :, part_ab], zr.at[m, zz])
        t = m * nmp + k
        one = W.at[m, zz, y, x, c, :, part_a if k else part_one]
        two = W.at[m, zz, y, x, c, :, part_b if k else part_two]
        send(one, one, h1s.at[m], h1r.at[t], to_x)
        send(two, two, h1s.at[m], h1r.at[t], to_y)

    def g2(m, k):
        zz = flip_by(z, k)
        t = m * nmp + k
        if k:
            got(W.at[m, zz, oy, ox, c, :, part_ab], h1r.at[t])
        else:
            got(W.at[m, zz, oy, ox, c], h1r.at[t])
        arrived(k, sides_size(m, 1), zcr.at[m, zz])
        one = W.at[m, zz, y, :, c, :, part_one]
        two = W.at[m, zz, :, x, c, :, part_two]
        send(one, one, h2s.at[m], h2r.at[t], to_y)
        send(two, two, h2s.at[m], h2r.at[t], to_x)

    def g3(m, k):
        zz = flip_by(z, k)
        t = m * nmp + k
        got(W.at[m, zz, oy, :, c], h2r.at[t])
        whole = W.at[m, zz, :, :, c]
        send(whole, whole, cs.at[m], cr.at[t], to_c)

    def g4(m, k):
        zz = flip_by(z, k)
        t = m * nmp + k
        got(W.at[m, zz, :, :, oc], cr.at[t])

    def g_done(m):
        for number, which in ((2, outermost), (4, inner)):

            @pl.when(which)
            def _(number=number):
                sent(W.at[m, pl.ds(0, number), y, x, c, :, part_ab], zs.at[m])
                sent(sides_size(m, number), zcs.at[m])

        sent(W.at[m, pl.ds(0, nmp - 1), y, x, c, :, part_ab], h1s.at[m])
        sent(W.at[m, z, y, x, c], h1s.at[m])
        sent(W.at[m, :, y, :, c], h2s.at[m])
        sent(W.at[m, :, :, :, c], cs.at[m])

    total = 6 * nmp

    def advance(t):
        def at(s, stage):
            if 0 <= s < total:
                stage(*ORDER[s])

        at(t - LAG, g2)
        for m in REST_AT.get(t, ()):
            z_rest(m)
        for table, stage in ((Z_AT, z_start), (PASS_AT, z_pass), (PASS_REST_AT, z_pass_rest)):
            for m in table.get(t, ()):
                stage(m)
        at(t, g1)
        at(t - LAG - DEPTH, g3)
        at(t - LAG - DEPTH - 1, g4)

    def here(m, k=None):
        keys = [k] if k is not None else range(nmp)
        return max(ORDER.index((m, key)) for key in keys) + LAG + DEPTH + 1

    back_a, back_b = pl.ds(BACK_LOW, half - BACK_LOW), pl.ds(half, BACK_HIGH - half)
    back_ab = pl.ds(BACK_LOW, BACK_HIGH - BACK_LOW)
    back_c, back_d = pl.ds(0, BACK_LOW), pl.ds(BACK_HIGH, d - BACK_HIGH)

    def release(m):
        g_done(m)
        for device in [to_x, to_y] + [to_z(flip_by(z, key)) for key in range(1, nmp)]:
            pl.semaphore_signal(free.at[m], inc=1, device_id=device, device_id_type=MESH)

    def may_send(m):
        pl.semaphore_wait(free.at[m], nmp + 1)

    def z_first(m, k, ref, dst, s_sem, r_sem):
        @pl.when(jnp.logical_and(k != z, jnp.logical_or(outermost, k == z1)))
        def _():
            slot = jnp.where(k == z1, z, jnp.where(k == z3, k, z1))
            send(ref, dst(slot), s_sem.at[m], r_sem.at[m, slot], to_z(z1))

    def z_second(m, k, ref, dst, s_sem, r_sem):
        @pl.when(jnp.logical_and(inner, jnp.logical_or(k == z2, k == z3)))
        def _():
            slot = jnp.where(k == z2, k, z)
            got(dst(slot), r_sem.at[m, slot])
            add_to(ref, dst(slot))
            send(ref, dst(z), s_sem.at[m], r_sem.at[m, z], to_z(k))

    def chunk_refs(m, k, part):
        return (
            W.at[m, k, y, x, c, :, part],
            lambda slot: W.at[m, slot, oy, ox, oc, :, part],
            zs,
            zr,
        )

    def third_refs(m, k):
        return (
            W.at[m, k, :, x, c, :, back_c],
            lambda slot: W.at[m, slot, :, ox, oc, :, back_c],
            zcs,
            zcr,
        )

    def fourth_refs(m, k):
        return (
            W.at[m, k, y, :, c, :, back_d],
            lambda slot: W.at[m, slot, oy, :, oc, :, back_d],
            zds,
            zdr,
        )

    def r1(m, k):
        t = m * nmp + k
        send(
            W.at[m, k, :, ox, c, :, part_one],
            W.at[m, k, :, ox, oc, :, part_one],
            h2s.at[m],
            h2r.at[t],
            to_x,
        )
        send(
            W.at[m, k, oy, :, c, :, part_two],
            W.at[m, k, oy, :, oc, :, part_two],
            h2s.at[m],
            h2r.at[t],
            to_y,
        )

    def either(m, whole, split):
        if isinstance(m, int):
            (whole if m in NO_THIRD else split)()
            return
        chosen = False
        for one in NO_THIRD:
            chosen = jnp.logical_or(chosen, m == one)
        pl.when(chosen)(whole)
        pl.when(jnp.logical_not(chosen))(split)

    def add_to(dst, src):
        dst[...] = (dst[...].astype(F32) + src[...].astype(F32)).astype(BF16)

    def r2(m, k):
        t = m * nmp + k
        got(W.at[m, k, y, :, oc], h2r.at[t])
        add_to(W.at[m, k, :, x, c, :, part_one], W.at[m, k, :, x, oc, :, part_one])
        add_to(W.at[m, k, y, :, c, :, part_two], W.at[m, k, y, :, oc, :, part_two])

        def second(one, two):
            send(W.at[m, k, oy, x, c, :, one], W.at[m, k, oy, ox, oc, :, one], h1s.at[m], h1r.at[t], to_y)
            send(W.at[m, k, y, ox, c, :, two], W.at[m, k, oy, ox, oc, :, two], h1s.at[m], h1r.at[t], to_x)

        def split():
            second(back_a, back_b)
            z_first(m, k, *third_refs(m, k))
            z_first(m, k, *fourth_refs(m, k))

        either(m, lambda: second(part_one, part_two), split)

    def r3(m, k):
        t = m * nmp + k

        def last(part, one, two):
            got(W.at[m, k, y, x, oc, :, part], h1r.at[t])
            add_to(W.at[m, k, y, x, c, :, one], W.at[m, k, y, ox, oc, :, one])
            add_to(W.at[m, k, y, x, c, :, two], W.at[m, k, oy, x, oc, :, two])
            z_first(m, k, *chunk_refs(m, k, part))

        either(m, lambda: last(pl.ds(0, d), part_one, part_two), lambda: last(back_ab, back_a, back_b))

    def r3_more(m, k):
        def split():
            z_second(m, k, *third_refs(m, k))
            z_second(m, k, *fourth_refs(m, k))
            z_second(m, k, *chunk_refs(m, k, back_ab))

        either(m, lambda: z_second(m, k, *chunk_refs(m, k, pl.ds(0, d))), split)

    def join(m):
        for refs, sem in ((third_refs, zcr), (fourth_refs, zdr)):
            own, slots = refs(m, z)[:2]
            mine = own[...].astype(F32)
            for zz in (z1, across):
                got(slots(zz), sem.at[m, zz])
                mine = mine + slots(zz)[...].astype(F32)
            own[...] = mine.astype(BF16)
        send(W.at[m, z, oy, x, c, :, back_c], XC.at[m, :, pl.ds(0, BACK_LOW)], hcs.at[m], hcr.at[m], to_y)
        send(
            W.at[m, z, y, ox, c, :, back_d],
            XC.at[m, :, pl.ds(BACK_LOW, d - BACK_HIGH)],
            hcs.at[m],
            hcr.at[m],
            to_x,
        )

    def r4(m):
        part = pl.ds(0, d) if m in NO_THIRD else back_ab
        sum_ = W[m, z, y, x, c, :, part].astype(F32)
        for zz in (z1, across):
            src = W.at[m, zz, oy, ox, oc, :, part]
            got(src, zr.at[m, zz])
            sum_ = sum_ + src[...].astype(F32)
        if m not in NO_THIRD:
            got(XC.at[m], hcr.at[m])
            low_part = W[m, z, y, x, c, :, back_c].astype(F32) + XC[m, :, 0:BACK_LOW].astype(F32)
            high_part = W[m, z, y, x, c, :, back_d].astype(F32) + XC[m, :, BACK_LOW:].astype(F32)
            sum_ = jnp.concatenate([low_part, sum_, high_part], axis=1)
        b, j = m // 3, m % 3
        if j == 0:
            WI[b, 0] = sum_[:, 0:third]
            WI[b, 2] = sum_[:, third:2 * third]
            WI[b, 1] = sum_[:, 2 * third:3 * third]
            WO[b] = sum_[:, 3 * third:].T
            result_copy(b, 0).start()
            result_copy(b, 1).start()
        else:
            M[b, (j - 1) * block:j * block] = sum_
            result_copy(b, j + 1).start()

    def result_copy(b, i):
        src = (WI.at[b], WO.at[b], M.at[b, pl.ds(0, block)], M.at[b, pl.ds(block, block)])[i]
        return keep(src, grads_out[b][i], 4 * b + i)

    def r_done(m):
        part = pl.ds(0, d) if m in NO_THIRD else back_ab
        sent(W.at[m, pl.ds(0, nmp - 1), y, x, c, :, part], zs.at[m])
        sent(W.at[m, :, y, x, c, :, part], h1s.at[m])
        sent(W.at[m, :, y, :, c], h2s.at[m])
        if m not in NO_THIRD:
            sent(W.at[m, pl.ds(0, nmp - 1), y, :, c, :, back_c], zcs.at[m])
            sent(W.at[m, pl.ds(0, nmp - 1), y, :, c, :, back_d], zds.at[m])
            sent(XC.at[m], hcs.at[m])

    def chunk(k):
        key, out, weight = nmp - 1 - k, 0, 1
        key = jnp.where(jnp.logical_and(inner, key > 1), 5 - key, key)
        while weight < nmp:
            out = out + weight * ((z // weight + key // weight) % 2)
            weight *= 2
        return out

    def join_any(m, k):
        if isinstance(m, int):
            if m not in NO_THIRD:
                join(m)
        else:
            either(m, lambda: None, lambda: join(m))

    def retreat(u):
        def at(s, stage):
            stage(5 - s // nmp, chunk(s % nmp))

        if isinstance(u, int):
            for v in TAIL_TWO[u]:
                at(v, r2)
            if u < total:
                at(u, r1)
            for v in TAIL_THREE[u]:
                at(v, r3)
            for v in TAIL_FOUR[u]:
                at(v, r3_more)
            for v in TAIL_JOIN[u]:
                at(v, join_any)
            return
        early = u < total - nmp
        pl.when(early)(lambda: at(u, r1))
        pl.when(jnp.logical_and(u >= LAG_TWO, early))(lambda: at(u - LAG_TWO, r2))
        pl.when(jnp.logical_and(u >= LAG_THREE, early))(lambda: at(u - LAG_THREE, r3))
        pl.when(jnp.logical_and(u >= LAG_FOUR, early))(lambda: at(u - LAG_FOUR, r3_more))
        own = (u - LAG_JOIN) % nmp == nmp - 1
        pl.when(jnp.logical_and(jnp.logical_and(u >= LAG_JOIN, own), early))(lambda: at(u - LAG_JOIN, join_any))
        for v in range(total - nmp, total):
            pl.when(u == v)(functools.partial(retreat, v))

    def swap_start(i):
        RB[i, pl.ds(me, 1)] = SB[i, pl.ds(me, 1)]
        for key in range(1, members):
            f = flip_by(me, key)
            send(SB.at[i, f], RB.at[i, me], ts.at[i], tr.at[i], to_member(f))

    def swap_wait(i):
        got(RB.at[i, pl.ds(0, members - 1)], tr.at[i])

    def swap_done(i):
        sent(SB.at[i, pl.ds(0, members - 1)], ts.at[i])

    def rows_of(ref, i):
        return ref[i].reshape(rows, d)

    for key in range(1, nmp):
        ref = SG.at[z, y, x, c]
        send(ref, ref, vs.at[0], vr.at[0], to_z(flip_by(z, key)))
    z_start(0)
    advance(0)
    advance(1)
    own_shards(1)
    got(SG.at[pl.ds(0, nmp - 1), y, x, c], vr.at[0])
    ref = SG.at[:, y, x, c]
    send(ref, ref, vs.at[1], vr.at[1], to_x)
    for copy in [*loads[-3:], loads[0]]:
        copy.wait()
    swap = swap_ref[...]
    keep(x_ref, ACC, 8).wait()
    H[0] = exact(swap.astype(F32), ACC[...], ((1,), (0,)))
    advance(2)
    got(SG.at[:, y, ox, c], vr.at[1])
    ref = SG.at[:, y, :, c]
    send(ref, ref, vs.at[2], vr.at[2], to_y)
    advance(3)
    got(SG.at[:, oy, :, c], vr.at[2])
    ref = SG.at[:, :, :, c]
    send(ref, ref, vs.at[3], vr.at[3], to_c)
    advance(4)
    got(SG.at[:, :, :, oc], vr.at[3])

    lane = lax.broadcasted_iota(jnp.int32, (1, d), 1)
    tall = SG[...].reshape(nmp * per * 16, 128)
    spread = mm(tall, tiles_ref[0]).reshape(nmp * per, 16, d)
    spread = jnp.sum(spread * mask_ref[0:nmp * per].reshape(nmp * per, 1, d), axis=0)
    SV[0, 0:6] = spread[0:6]
    SV[1, 0:6] = spread[6:12]
    is_q = (lane < third).astype(F32)
    is_v = jnp.logical_and(lane >= third, lane < 2 * third).astype(F32)
    spread_in = mm(tall, tiles_ref[1]).reshape(nmp, per, 16, d)
    spread_up = mm(tall, tiles_ref[2]).reshape(nmp, per, 16, d)
    mask_in = mask_ref[nmp * per:nmp * per + per].reshape(per, 1, d)
    mask_up = mask_ref[nmp * per + per:nmp * per + 2 * per].reshape(per, 1, d)
    for k in range(nmp):
        one = jnp.sum(spread_in[k] * mask_in, axis=0)
        two = jnp.sum(spread_up[k] * mask_up, axis=0)
        for b in range(2):
            BI[b, k] = one[12 + 2 * b:13 + 2 * b] * is_q + one[13 + 2 * b:14 + 2 * b] * is_v
            BU[b, k] = two[b:b + 1]
    for t in range(5, here(0) + 1):
        advance(t)

    lane2 = lax.broadcasted_iota(jnp.int32, (1, 256), 1)
    heads = third // HEAD

    def head_mask(lead):
        return jnp.logical_and(lane2 >= lead * HEAD, lane2 < lead * HEAD + HEAD).astype(F32).astype(BF16)

    q_masks = [head_mask(h) for h in range(heads)]
    v_masks = [head_mask(h + 1) for h in range(heads)]
    scale = HEAD ** (-0.5)
    wide = 5 * 128

    def flat(values):
        return values.reshape(d, values.shape[-1])

    def lower(values):
        return values.reshape(half, values.shape[-1])

    def tall_view(values):
        return values.T.astype(BF16).reshape(2, 2, 2, d // per, rows)

    def to_sibling(src, dst, n):
        send(src, dst, ss.at[n], sr.at[n], to_c)

    def norm_to_sibling(b, i):
        to_sibling(NT.at[b, i, :, :, oc], LS.at[i], 1 + i)

    def early_to_sibling(b):
        to_sibling(HID.at[b], HS, 0)
        for i in range(2):
            norm_to_sibling(b, i)
        to_sibling(CT.at[b], CS, 3)

    def take_grad(b):
        grad = GR[...]
        SGR[pl.ds(16 * b + 5, 1)] = jnp.sum(grad, axis=0, keepdims=True)
        NB[...] = grad.astype(BF16)
        GT[0] = tall_view(grad)
        to_sibling(GT.at[0, :, :, oc], LS.at[2], 4)

    def shrink(b, k):
        hidden_grad = mm(NB[...], flat(W[3 * b + 2, k]))
        upper_grad = (GP[b, k].astype(F32) * hidden_grad).astype(BF16)
        GP[b, k] = upper_grad
        to_sibling(GP.at[b, k], US.at[k], 6)
        SGR[pl.ds(16 * b + 10 + k, 1)] = jnp.sum(upper_grad.astype(F32), axis=0, keepdims=True)

    def forward(b, _):
        m = 3 * b
        ends = [(here(3 * i), here(3 * i + 1), here(3 * i + 2)) for i in range(2)]
        done = [here(0), here(3)]

        def turn(upto):
            for i in range(2):
                steps_ = range(done[i] + 1, upto[i] + 1)
                done[i] = max(done[i], upto[i])
                if len(steps_):
                    pl.when(b == i)(lambda steps_=steps_: [advance(t) for t in steps_] and None)

        def one_of(i):
            return [min(done[0] + 1, ends[0][i]), min(done[1] + 1, ends[1][i])]

        @pl.when(b == 1)
        def _():
            swap_wait(1)
            H[1] = rows_of(RB, 1).astype(F32)

        h = H[b]
        unit, _s = unit_rows(h)
        normed = unit * SV[b, 0:1] + SV[b, 1:2]
        NB[...] = normed.astype(BF16)
        NT[b, 0] = tall_view(normed)
        pl.when(b == 1)(lambda: norm_to_sibling(1, 0))
        ACC[...] = h + SV[b, 2:3]

        def attend(k):
            packed = (mm(NB[...], flat(W[m, k, :, :, :, :, 0:wide])) + BI[b, k, :, 0:wide]).astype(BF16)
            PK[b, k] = packed
            qs = packed[:, 0:256] * BF16(scale)
            vv = packed[:, 128:384]
            kk = packed[:, 384:640]
            mixed = jnp.zeros((rows, 256), F32)
            for h in range(heads):
                scores = mm_t(qs * q_masks[h], kk)
                expo = jnp.exp(scores - jnp.max(scores, axis=-1, keepdims=True))
                probs = (expo * (1.0 / jnp.sum(expo, axis=-1, keepdims=True))).astype(BF16)
                PR[b, k, h] = probs
                mixed += mm(probs, vv * v_masks[h])
            mixed = mixed.astype(BF16)
            CT[b, k] = mixed
            pl.when(b == 1)(lambda: to_sibling(CT.at[1, k], CS.at[k], 3))
            ACC[...] += mm_t(mixed, flat(W[m, k, :, :, :, :, d - 256:d]))

        for k in range(nmp):
            attend(k)
            if k % 2 == 1 and k < 4:
                turn(one_of(1))
        middle = ACC[...]
        M[b] = middle
        unit, _s = unit_rows(middle)
        normed = unit * SV[b, 3:4] + SV[b, 4:5]
        NB[...] = normed.astype(BF16)
        NT[b, 1] = tall_view(normed)
        pl.when(b == 1)(lambda: norm_to_sibling(1, 1))
        ACC[...] = middle + SV[b, 5:6]

        @pl.when(b == 0)
        def _():
            keep(ct_ref, GR, 9).wait()
            picked = (swap.astype(F32) * bits_ref[...].astype(F32)).astype(BF16)
            SB[0] = mm(picked, GR[...].astype(BF16)).astype(BF16).reshape(members, rows // members, d)
            swap_start(0)

        turn([ends[0][1], ends[1][1]])

        def expand(k):
            upper = mm(NB[...], flat(W[m + 1, k])) + BU[b, k]
            cdf = 0.5 + 0.5 * lax.erf(upper * (0.5 ** 0.5))
            HID[b, k] = (upper * cdf).astype(BF16)
            density = jnp.exp(-0.5 * upper * upper) * ((2 * np.pi) ** -0.5)
            GP[b, k] = (cdf + upper * density).astype(BF16)
            pl.when(b == 1)(lambda: to_sibling(HID.at[1, k], HS.at[k], 0))

        def contract(k):
            pl.when(b == 1)(lambda: shrink(1, k))
            ACC[...] += mm_t(HID[b, k], flat(W[m + 2, k]))

        for k in range(nmp):
            expand(k)
            if k == 1:
                turn(one_of(2))

        @pl.when(b == 1)
        def _():
            swap_wait(0)
            GR[...] = rows_of(RB, 0).astype(F32)
            take_grad(1)

        contract(z)
        for k in range(1, nmp):
            turn([here(2, k), here(5, k)])
            contract(flip_by(z, k))
        SB[1 + b] = ACC[...].astype(BF16).reshape(members, rows // members, d)
        pl.when(b == 0)(lambda: swap_start(1))
        turn([here(3), done[1]])
        return 0

    lax.fori_loop(0, 2, forward, 0)

    def norm_back(grad, start, gain):
        unit, scale = unit_rows(start)
        lifted = grad * gain
        back = scale * (
            lifted
            - jnp.mean(lifted, axis=-1, keepdims=True)
            - unit * jnp.mean(lifted * unit, axis=-1, keepdims=True)
        )
        return back, jnp.sum(grad * unit, axis=0, keepdims=True), jnp.sum(grad, axis=0, keepdims=True)

    def deal():
        rows_ = []
        for zz in range(nmp):
            own = mask_ref[zz * per:zz * per + per].reshape(per, 1, d)
            plain = jnp.concatenate([SGR[0:6], SGR[16:22]], axis=0).reshape(1, 12, d) * own
            pair = jnp.concatenate([SGR[6 + zz:7 + zz], SGR[22 + zz:23 + zz]], axis=0).reshape(1, 2, d) * mask_in
            up = jnp.concatenate([SGR[10 + zz:11 + zz], SGR[26 + zz:27 + zz]], axis=0).reshape(1, 2, d) * mask_up
            rows_ = jnp.concatenate([plain, pair, up], axis=1).reshape(per * 16, d)
            high = rows_.astype(BF16)
            rest = (rows_ - high.astype(F32)).astype(BF16)
            line = lax.broadcasted_iota(jnp.int32, (per, 16, 128), 1)
            parts = [
                (mm_t(high, tiles_ref[i]) + mm_t(rest, tiles_ref[i])).reshape(per, 16, 128) for i in (0, 3, 2)
            ]
            XS[zz] = jnp.where(line < 12, parts[0], jnp.where(line < 14, parts[1], parts[2]))
        for key in range(1, nmp * per):
            qq, zz = peer(key)
            send(XS.at[zz, qq], XR.at[key], rs.at[0], rr.at[0], to_peer(key))

    def backward(step, _):
        b = 1 - step
        m = 3 * b
        row = 16 * b

        @pl.when(step == 1)
        def _():
            pl.semaphore_wait(free_c, 1)
            early_to_sibling(b)
            take_grad(b)

            def shrink_all(k, _):
                shrink(b, k)
                return 0

            lax.fori_loop(0, nmp, shrink_all, 0)

        release(m + 2)
        got(HS, sr.at[0])
        got(LS.at[2], sr.at[4])
        may_send(m + 2)

        def down_grad(step_k, _):
            k = chunk(step_k)
            own = mm(lower(GT[0, :, :, c]), HID[b, k]) + mm(lower(LS[2]), HS[k])
            W[m + 2, k, :, :, c] = own.astype(BF16).reshape(2, 2, d // per, d)
            retreat(3 * nmp * step + step_k)
            return 0

        lax.fori_loop(0, nmp, down_grad, 0)
        pl.when(step == 1)(lambda: swap_start(2))
        ACC[...] = jnp.zeros_like(ACC)

        def spread_up(k, _):
            ACC[...] += mm_t(GP[b, k], flat(W[m + 1, k]))
            return 0

        lax.fori_loop(0, nmp, spread_up, 0)
        release(m + 1)
        got(US, sr.at[6])
        got(LS.at[1], sr.at[2])
        may_send(m + 1)

        def up_grad(step_k, _):
            k = chunk(step_k)
            own = mm(lower(NT[b, 1, :, :, c]), GP[b, k]) + mm(lower(LS[1]), US[k])
            W[m + 1, k, :, :, c] = own.astype(BF16).reshape(2, 2, d // per, d)
            retreat(3 * nmp * step + nmp + step_k)
            return 0

        lax.fori_loop(0, nmp, up_grad, 0)
        pl.when(step == 1)(lambda: r4(5))
        back, gain_grad, bias_grad = norm_back(ACC[...], M[b], SV[b, 3:4])
        SGR[pl.ds(row + 3, 1)] = gain_grad
        SGR[pl.ds(row + 4, 1)] = bias_grad
        middle_grad = GR[...] + back
        GR[...] = middle_grad
        SGR[pl.ds(row + 2, 1)] = jnp.sum(middle_grad, axis=0, keepdims=True)
        NB[...] = middle_grad.astype(BF16)
        GT[1] = tall_view(middle_grad)
        to_sibling(GT.at[1, :, :, oc], LS.at[3], 5)
        ACC[...] = jnp.zeros_like(ACC)
        def attend_back(k, _):
            mixed_grad = mm(NB[...], flat(W[m, k, :, :, :, :, d - 256:d])).astype(BF16)
            packed = PK[b, k]
            qs = packed[:, 0:256] * BF16(scale)
            vv = packed[:, 128:384]
            kk = packed[:, 384:640]
            q_grad = jnp.zeros((rows, 256), F32)
            k_grad = jnp.zeros((rows, 256), F32)
            v_grad = jnp.zeros((rows, 256), F32)
            for h in range(heads):
                part = mixed_grad * v_masks[h]
                probs_low = PR[b, k, h]
                probs = probs_low.astype(F32)
                weighted = probs * mm_t(part, vv)
                score_grad = (weighted - probs * jnp.sum(weighted, axis=-1, keepdims=True)).astype(BF16)
                q_grad += mm(score_grad, kk * q_masks[h])
                k_grad += t_mm(score_grad, qs * q_masks[h])
                v_grad += t_mm(probs_low, part)
            q_grad = q_grad * scale
            packed_grad = jnp.concatenate(
                [q_grad[:, 0:128], q_grad[:, 128:256] + v_grad[:, 0:128], v_grad[:, 128:256], k_grad], axis=1
            ).astype(BF16)
            PK[b, k] = packed_grad
            to_sibling(PK.at[b, k], PS.at[k], 7)
            SGR[pl.ds(row + 6 + k, 1), 0:wide] = jnp.sum(packed_grad.astype(F32), axis=0, keepdims=True)
            ACC[...] += mm_t(packed_grad, flat(W[m, k, :, :, :, :, 0:wide]))
            return 0

        lax.fori_loop(0, nmp, attend_back, 0)
        release(m)
        back, gain_grad, bias_grad = norm_back(ACC[...], H[b], SV[b, 0:1])
        SGR[pl.ds(row, 1)] = gain_grad
        SGR[pl.ds(row + 1, 1)] = bias_grad
        GR[...] = GR[...] + back

        @pl.when(step == 0)
        def _():
            SB[3] = GR[...].astype(BF16).reshape(members, rows // members, d)
            swap_start(3)

        pl.when(step == 1)(deal)
        got(PS, sr.at[7])
        got(LS.at[0], sr.at[1])
        got(LS.at[3], sr.at[5])
        got(CS, sr.at[3])
        may_send(m)

        def in_grad(step_k, _):
            k = chunk(step_k)
            one = mm(lower(NT[b, 0, :, :, c]), PK[b, k]) + mm(lower(LS[0]), PS[k])
            two = mm(lower(GT[1, :, :, c]), CT[b, k]) + mm(lower(LS[3]), CS[k])
            own = jnp.concatenate(
                [one[:, 0:512], one[:, 512:640] + two[:, 0:128], two[:, 128:256]], axis=1
            ).astype(BF16)
            W[m, k, :, :, c] = own.reshape(2, 2, d // per, d)
            retreat(3 * nmp * step + 2 * nmp + step_k)
            return 0

        lax.fori_loop(0, nmp, in_grad, 0)

        sent(HID.at[b], ss.at[0])
        sent(NT.at[b, 0, :, :, oc], ss.at[1])
        sent(NT.at[b, 1, :, :, oc], ss.at[2])
        sent(CT.at[b], ss.at[3])
        sent(GT.at[0, :, :, oc], ss.at[4])
        sent(GT.at[1, :, :, oc], ss.at[5])
        sent(GP.at[b], ss.at[6])
        sent(PK.at[b], ss.at[7])

        @pl.when(step == 0)
        def _():
            pl.semaphore_signal(free_c, inc=1, device_id=to_c, device_id_type=MESH)

        pl.when(step == 1)(lambda: r4(4))

        @pl.when(step == 0)
        def _():
            swap_wait(3)
            GR[...] = rows_of(RB, 3).astype(F32)
        return 0

    lax.fori_loop(0, 2, backward, 0)

    ACC[...] = exact(swap.astype(F32), GR[...], ((1,), (0,)))
    keep(ACC, ig_ref, 9).start()
    swap_wait(2)
    H[1] = mm(swap, rows_of(RB, 2))
    keep(H.at[1], out_ref, 8).start()
    for u in sorted(TAIL_TWO):
        if u >= total:
            retreat(u)
    r4(3)
    r4(2)
    got(XR.at[pl.ds(1, nmp * per - 1)], rr.at[0])
    sg_ref[...] = XS[z, q] + jnp.sum(XR[1:nmp * per], axis=0)
    r4(1)
    r4(0)
    sent(XR.at[pl.ds(1, nmp * per - 1)], rs.at[0])
    for b in range(2):
        for i in range(4):
            result_copy(b, i).wait()
    keep(H.at[1], out_ref, 8).wait()
    keep(ACC, ig_ref, 9).wait()
    for m in range(6):
        r_done(m)
    for i in range(4):
        swap_done(i)
    sent(SG.at[pl.ds(0, nmp - 1), y, x, c], vs.at[0])
    sent(SG.at[:, y, x, c], vs.at[1])
    sent(SG.at[:, y, :, c], vs.at[2])
    sent(SG.at[:, :, :, c], vs.at[3])


def tables(outer, ndp, nmp, d):
    n = d // (ndp * nmp)
    tiles = np.zeros((4, 128, d), np.float32)
    masks = np.zeros((nmp * INNER + 2 * INNER, d), np.float32)
    for at in range(d):
        i = at % n
        zz = (at // n) % nmp
        pp = at // (n * nmp)
        qq, lo = pp // outer, pp % outer
        tiles[0, lo * n + i, at] = 1
        masks[zz * INNER + qq, at] = 1
    third = d // nmp
    step = third // INNER
    for at in range(2 * third):
        tiles[1, at % step, at] = 1
        tiles[3, at % step + 32 * (at // third), at] = 1
        masks[nmp * INNER + (at % third) // step, at] = 1
    step = d // INNER
    for at in range(d):
        tiles[2, 32 + at % step, at] = 1
        masks[nmp * INNER + INNER + at // step, at] = 1
    return tiles, masks


def turn_table():
    swap = np.zeros((FRAME, FRAME), np.float32)
    across = SIDE // TUBE
    for wr in range(across):
        for i in range(TUBE):
            for wc in range(across):
                for j in range(TUBE):
                    natural = ((wr * TUBE + i) * across + wc) * TUBE + j
                    turned = ((wr * across + wc) * TUBE + i) * TUBE + j
                    swap[turned, natural] = 1
    return swap


def fused(sizes, x, cotangent, bits, matrices, vectors, ndp):
    outer, nmp, d, rows = sizes
    tiles, masks = tables(outer, ndp, nmp, d)
    members = CLIP // FRAME
    vmem = pltpu.VMEM
    dma = pltpu.SemaphoreType.DMA
    regular = pltpu.SemaphoreType.REGULAR
    block = d // INNER
    steps = 6 * nmp
    scratch = [
        vmem((6, nmp, 2, 2, 2, block, d), BF16),
        vmem((nmp, 2, 2, 2, 16, 128), BF16),
        vmem((2, 8, d), F32),
        vmem((2, nmp, 1, d), F32),
        vmem((2, nmp, 1, d), F32),
        vmem((2, rows, d), F32),
        vmem((2, rows, d), F32),
        vmem((rows, d), BF16),
        vmem((2, 2, 2, 2, 2, block, rows), BF16),
        vmem((2, 2, 2, 2, block, rows), BF16),
        vmem((2, nmp, rows, 640), BF16),
        vmem((2, nmp, rows, 256), BF16),
        vmem((2, nmp, rows, d), BF16),
        vmem((2, nmp, rows, d), BF16),
        vmem((2, nmp, d // nmp // HEAD, rows, rows), BF16),
        vmem((rows, d), F32),
        vmem((rows, d), F32),
        vmem((32, d), F32),
        vmem((nmp, INNER, 16, 128), F32),
        vmem((nmp * INNER, 16, 128), F32),
        vmem((4, members, rows // members, d), BF16),
        vmem((4, members, rows // members, d), BF16),
        vmem((nmp, rows, d), BF16),
        vmem((nmp, rows, 256), BF16),
        vmem((nmp, rows, d), BF16),
        vmem((nmp, rows, 640), BF16),
        vmem((4, 2, 2, block, rows), BF16),
        dma((6,)),
        dma((6, nmp)),
        dma((6,)),
        dma((6, nmp)),
        dma((6,)),
        dma((6, nmp)),
        dma((6,)),
        dma((6,)),
        dma((6,)),
        dma((steps,)),
        dma((6,)),
        dma((steps,)),
        dma((6,)),
        dma((steps,)),
        dma((4,)),
        dma((4,)),
        dma((4,)),
        dma((4,)),
        dma((8,)),
        dma((8,)),
        dma((1,)),
        dma((1,)),
        regular((6,)),
        regular,
        vmem((2, 3, block, d // nmp), F32),
        vmem((2, d // nmp, block), F32),
        vmem((16, 128), F32),
        vmem((6, block, d - BACK_HIGH + BACK_LOW), BF16),
        dma((10,)),
        vmem(bits.shape, bits.dtype),
        *(vmem(v.shape, v.dtype) for v in vectors),
        vmem((FRAME, FRAME), BF16),
        vmem(tiles.shape, BF16),
        vmem(masks.shape, F32),
        dma((4 + len(vectors),)),
    ]
    grads = [
        jax.ShapeDtypeStruct((3, block, d // nmp), F32),
        jax.ShapeDtypeStruct((d // nmp, block), F32),
        jax.ShapeDtypeStruct((block, d), F32),
        jax.ShapeDtypeStruct((block, d), F32),
    ]
    whole = jax.ShapeDtypeStruct((rows, d), F32)
    anywhere = pl.BlockSpec(memory_space=pl.ANY)
    inside = pl.BlockSpec(memory_space=vmem)
    return pl.pallas_call(
        functools.partial(kernel, sizes, len(vectors)),
        out_shape=[whole, whole] + grads + grads + [jax.ShapeDtypeStruct((16, 128), F32)],
        in_specs=[anywhere] * (14 + len(vectors)),
        out_specs=[anywhere] * 10 + [inside],
        scratch_shapes=scratch,
        compiler_params=pltpu.CompilerParams(
            collective_id=0, has_side_effects=True, vmem_limit_bytes=64 << 20
        ),
        name="two_blocks",
    )(
        x,
        cotangent,
        bits,
        *matrices,
        *vectors,
        jnp.asarray(turn_table(), BF16),
        jnp.asarray(tiles, BF16),
        jnp.asarray(masks, F32),
    )


def settle_kernel(wide, *refs):
    big, sg_in, outs = refs[:10], refs[10], refs[11:37]
    held, sg_ref, sems = refs[37:47], refs[47], refs[48]
    small_copy = pltpu.make_async_copy(sg_in, sg_ref, sems.at[0, 10])
    small_copy.start()
    copies = []
    for i in range(10):
        copies.append(
            (
                pltpu.make_async_copy(big[i], held[i], sems.at[0, i]),
                pltpu.make_async_copy(held[i], outs[i], sems.at[1, i]),
            )
        )
        copies[i][0].start()
    small_copy.wait()
    for b in range(2):
        small = outs[10 + 8 * b:18 + 8 * b]
        for i in range(6):
            small[i][...] = sg_ref[6 * b + i:6 * b + i + 1, 0:wide]
        small[6][0:1] = sg_ref[12 + b:13 + b, 0:wide]
        small[6][1:2] = sg_ref[12 + b:13 + b, 32:32 + wide]
        small[7][...] = sg_ref[14 + b:15 + b, 32:32 + 4 * wide]
    for arrive, leave in copies:
        arrive.wait()
        leave.start()
    for _, leave in copies:
        leave.wait()


def settle(big, sg, wide, ups):
    anywhere = pl.BlockSpec(memory_space=pl.ANY)
    inside = pl.BlockSpec(memory_space=pltpu.VMEM)
    row = jax.ShapeDtypeStruct((1, wide), F32)
    small = [row] * 6 + [jax.ShapeDtypeStruct((2, wide), F32), jax.ShapeDtypeStruct((1, ups), F32)]
    outs = pl.pallas_call(
        functools.partial(settle_kernel, wide),
        out_shape=[jax.ShapeDtypeStruct(v.shape, v.dtype) for v in big] + small + small,
        in_specs=[anywhere] * 11,
        out_specs=[anywhere] * 10 + [inside] * 16,
        scratch_shapes=[pltpu.VMEM(v.shape, v.dtype) for v in (*big, sg)]
        + [pltpu.SemaphoreType.DMA((2, 11))],
        name="settle",
    )(*big, sg)
    return outs[:10], (outs[10:18], outs[18:26])


def shards_of(ndp, nmp, inputs, cotangent, mask_bits, *params):
    frame, tube = params[:12], params[12:]
    d = inputs.shape[1]
    rows = inputs.shape[0]
    outer = ndp // INNER
    groups = [[qq * outer + lo for lo in range(outer)] for qq in range(INNER)]

    def joined(values, axis):
        if outer == 1:
            return values
        return lax.all_gather(values, "dp", axis=axis, tiled=True, axis_index_groups=groups)

    matrices = []
    vectors = []
    for block in (frame, tube):
        matrices += [
            joined(block[2].transpose(1, 0, 2), 1),
            joined(block[4], 1),
            joined(block[8], 0),
            joined(block[10].T, 0),
        ]
        vectors += [joined(block[i][None], 1) for i in (0, 1, 5, 6, 7, 11)]
    vectors += [joined(block[3], 1) for block in (frame, tube)]
    vectors += [joined(block[9][None], 1) for block in (frame, tube)]
    wide, ups = vectors[0].shape[1], vectors[-1].shape[1]
    outs = fused((outer, nmp, d, rows), inputs, cotangent, mask_bits[None], matrices, vectors, ndp)
    big, sg = list(outs[:10]), outs[10]
    if outer == 1:
        big, small = settle(big, sg, wide, ups)
    else:
        low = lax.axis_index("dp") % outer
        sg = lax.psum(sg, "dp", axis_index_groups=groups)

        def piece(values, start, size):
            size = size // outer
            return lax.dynamic_slice_in_dim(values, start + low * size, size, 1)

        small = []
        for b in range(2):
            parts = [piece(sg[6 * b + i:6 * b + i + 1], 0, wide) for i in range(6)]
            pair = sg[12 + b, 0:64].reshape(2, 32)
            small.append(parts + [piece(pair, 0, wide), piece(sg[14 + b:15 + b], 32, ups)])
            for i, axis in enumerate((1, 1, 0, 0)):
                at = 2 + 4 * b + i
                big[at] = lax.psum_scatter(
                    big[at], "dp", scatter_dimension=axis, tiled=True, axis_index_groups=groups
                )
    results = []
    for b in range(2):
        inw, outw, up, down = big[2 + 4 * b:6 + 4 * b]
        rows_ = small[b]
        results += [
            rows_[0].reshape(-1),
            rows_[1].reshape(-1),
            inw.transpose(1, 0, 2),
            rows_[6],
            outw,
            rows_[2].reshape(-1),
            rows_[3].reshape(-1),
            rows_[4].reshape(-1),
            up,
            rows_[7].reshape(-1),
            down.T,
            rows_[5].reshape(-1),
        ]
    return (big[0], big[1]) + tuple(results)


def solution(mesh):
    rows = P(("dp", "mp"), None)
    small = P(("dp", "mp"))
    block = (
        small,
        small,
        P("dp", None, "mp"),
        P(None, ("mp", "dp")),
        P("mp", "dp"),
        small,
        small,
        small,
        P("dp", "mp"),
        P(("mp", "dp")),
        P("mp", "dp"),
        small,
    )
    return jax.shard_map(
        functools.partial(shards_of, mesh.shape["dp"], mesh.shape["mp"]),
        mesh=mesh,
        in_specs=(rows, rows, small) + block + block,
        out_specs=(rows, rows) + block + block,
        check_vma=False,
    )
```

```python
import functools

import jax
import jax.numpy as jnp
import numpy as np
from jax import lax
from jax.experimental import pallas as pl
from jax.experimental.pallas import tpu as pltpu
from jax.sharding import PartitionSpec as P

MESH = pl.DeviceIdType.MESH
HEAD = 64
SIDE = 16
TUBE = 4
FRAME = SIDE * SIDE
CLIP = 4096
EPS = 1e-06
INNER = 8
CUT_LOW = 256
CUT_HIGH = 640
BACK_LOW = 128
BACK_HIGH = 512
LAG = 2
DEPTH = 3
ORDER = (
    [(0, 0), (1, 0), (2, 0), (3, 0)]
    + [(m, k) for m in (0, 1) for k in (1, 2, 3)]
    + [(4, 0), (2, 1), (2, 2), (2, 3), (3, 1), (3, 2), (3, 3), (5, 0)]
    + [(m, k) for m in (4, 5) for k in (1, 2, 3)]
)
Z_AT = {2: (1,), 5: (2,), 8: (3,), 12: (4,), 16: (5,)}
REST_AT = {2: (0,), 3: (1,), 5: (2,), 10: (3,), 13: (4,), 19: (5,)}
PASS_AT = {2: (0,), 6: (1,), 10: (2,), 13: (3,), 17: (4,), 20: (5,)}
PASS_REST_AT = {5: (0,), 8: (1,), 12: (2,), 15: (3,), 19: (4,), 22: (5,)}
NO_THIRD = (0, 1)
LAG_TWO = 4
LAG_THREE = 7
LAG_FOUR = 9
LAG_JOIN = 12
TAIL_TWO = {20: (16, 17), 21: (18, 19), 22: (20,), 23: (21,), 24: (22,), 25: (23,), 26: ()}
TAIL_THREE = {20: (13, 14), 21: (15, 16), 22: (17, 18), 23: (19, 20), 24: (21,), 25: (22,), 26: (23,)}
TAIL_FOUR = {20: (11, 12), 21: (13, 14), 22: (15, 16), 23: (17, 18), 24: (19, 20), 25: (21,), 26: (22, 23)}
TAIL_JOIN = {20: (), 21: (11,), 22: (), 23: (15,), 24: (), 25: (), 26: ()}
F32 = jnp.float32
BF16 = jnp.bfloat16


def mm(left, right):
    return lax.dot_general(left, right, (((1,), (0,)), ((), ())), preferred_element_type=F32)


def mm_t(left, right):
    return lax.dot_general(left, right, (((1,), (1,)), ((), ())), preferred_element_type=F32)


def t_mm(left, right):
    return lax.dot_general(left, right, (((0,), (0,)), ((), ())), preferred_element_type=F32)


def exact(left, right, dims):
    return lax.dot_general(
        left, right, (dims, ((), ())), precision=lax.Precision.HIGHEST, preferred_element_type=F32
    )


def flip(value, weight):
    bit = (value // weight) % 2
    return value + weight * (1 - 2 * bit)


def flip_by(value, key):
    weight = 1
    while key:
        if key & 1:
            value = flip(value, weight)
        key >>= 1
        weight *= 2
    return value


def unit_rows(values):
    center = values - jnp.mean(values, axis=-1, keepdims=True)
    spread = jnp.mean(center * center, axis=-1, keepdims=True)
    scale = lax.rsqrt(spread + EPS)
    return center * scale, scale


def kernel(
    sizes,
    count,
    *refs,
):
    x_ref, ct_ref = refs[:2]
    matrices = (refs[3:7], refs[7:11])
    out_ref, ig_ref = refs[14 + count:16 + count]
    grads_out = (refs[16 + count:20 + count], refs[20 + count:24 + count])
    sg_ref = refs[24 + count]
    sources = (refs[2], *refs[11:14 + count])
    held = refs[-len(sources) - 1:-1]
    bits_ref, vectors, (swap_ref, tiles_ref, mask_ref) = held[0], held[1:1 + count], held[1 + count:]
    sems = refs[-1]
    loads = [pltpu.make_async_copy(src, dst, sems.at[i]) for i, (src, dst) in enumerate(zip(sources, held))]
    body(
        sizes, x_ref, ct_ref, bits_ref, matrices, vectors, swap_ref, tiles_ref, mask_ref, out_ref, ig_ref,
        grads_out, sg_ref, loads, *refs[25 + count:-len(sources) - 1]
    )


def body(
    sizes,
    x_ref,
    ct_ref,
    bits_ref,
    matrices,
    vectors,
    swap_ref,
    tiles_ref,
    mask_ref,
    out_ref,
    ig_ref,
    grads_out,
    sg_ref,
    loads,
    W,
    SG,
    SV,
    BI,
    BU,
    H,
    M,
    NB,
    NT,
    GT,
    PK,
    CT,
    HID,
    GP,
    PR,
    ACC,
    GR,
    SGR,
    XS,
    XR,
    SB,
    RB,
    HS,
    CS,
    US,
    PS,
    LS,
    zs,
    zr,
    zcs,
    zcr,
    zds,
    zdr,
    hcs,
    hcr,
    h1s,
    h1r,
    h2s,
    h2r,
    cs,
    cr,
    vs,
    vr,
    ts,
    tr,
    ss,
    sr,
    rs,
    rr,
    free,
    free_c,
    WI,
    WO,
    SM,
    XC,
    ls,
):
    outer, nmp, d, rows = sizes
    per = INNER
    half = d // 2
    dp = lax.axis_index("dp")
    z = lax.axis_index("mp")
    low = dp % outer
    q = dp // outer
    c = q % 2
    x = (q // 2) % 2
    y = q // 4
    oc, ox, oy = 1 - c, 1 - x, 1 - y
    members = CLIP // FRAME
    dpc = members // nmp
    me = (dp % dpc) * nmp + z

    def place(cc, xx, yy):
        return (yy * 4 + xx * 2 + cc) * outer + low

    assert nmp == 4
    z1, z2, z3 = flip_by(z, 1), flip_by(z, 2), flip_by(z, 3)
    across = 2 - z // 2
    inner = jnp.logical_or(z == 1, z == 2)
    outermost = jnp.logical_not(inner)

    to_c = (place(oc, x, y), z)
    to_x = (place(c, ox, y), z)
    to_y = (place(c, x, oy), z)

    def to_z(zz):
        return (dp, zz)

    def peer(key):
        return flip_by(q, key // nmp), flip_by(z, key % nmp)

    def to_peer(key):
        qq, zz = peer(key)
        return (qq * outer + low, zz)

    def to_member(f):
        return ((dp // dpc) * dpc + f // nmp, f % nmp)

    def send(src, dst, s_sem, r_sem, device):
        pltpu.make_async_remote_copy(
            src_ref=src, dst_ref=dst, send_sem=s_sem, recv_sem=r_sem, device_id=device, device_id_type=MESH
        ).start()

    def sent(src, s_sem):
        pltpu.make_async_remote_copy(
            src_ref=src, dst_ref=src, send_sem=s_sem, recv_sem=s_sem, device_id=to_c, device_id_type=MESH
        ).wait_send()

    def got(dst, r_sem):
        pltpu.make_async_remote_copy(
            src_ref=dst, dst_ref=dst, send_sem=r_sem, recv_sem=r_sem, device_id=to_c, device_id_type=MESH
        ).wait_recv()

    def keep(src, dst, n):
        return pltpu.make_async_copy(src, dst, ls.at[n])

    block = d // per
    third = d // nmp

    def matrix_copies(b):
        inw, outw, up, down = matrices[b]
        return (
            keep(inw, WI.at[b], 4 * b),
            keep(outw, WO.at[b], 4 * b + 1),
            keep(up, M.at[b, pl.ds(0, block)], 4 * b + 2),
            keep(down, M.at[b, pl.ds(block, block)], 4 * b + 3),
        )

    barrier = pltpu.get_barrier_semaphore()
    greeted = [to_peer(key) for key in range(1, nmp * per)]
    if outer > 1:
        greeted += [to_member(flip_by(me, key)) for key in range(1, members)]
    for device in greeted:
        pl.semaphore_signal(barrier, inc=1, device_id=device, device_id_type=MESH)
    for copy in loads[1:-3]:
        copy.start()
    for b in range(2):
        for copy in matrix_copies(b):
            copy.start()
    keep(x_ref, ACC, 8).start()
    keep(ct_ref, GR, 9).start()
    for copy in [*loads[-3:], loads[0]]:
        copy.start()
    SM[...] = jnp.zeros_like(SM)
    for copy in loads[1:-3]:
        copy.wait()
    narrow = 0
    for i, ref in enumerate(vectors[:12]):
        narrow = ref.shape[1]
        SM[i:i + 1, 0:narrow] = ref[...]
    for i, ref in enumerate(vectors[12:14]):
        SM[12 + 2 * i:14 + 2 * i, 0:narrow] = ref[...]
    for i, ref in enumerate(vectors[14:16]):
        SM[i:i + 1, 32:32 + ref.shape[1]] = ref[...]
    SG[z, y, x, c] = SM[...].astype(BF16)

    def own_shards(b):
        copies = matrix_copies(b)
        copies[0].wait()
        copies[1].wait()
        parts = [WI[b, 0], WI[b, 2], WI[b, 1], WO[b].T]
        W[3 * b, z, y, x, c] = jnp.concatenate(parts, axis=1).astype(BF16)
        copies[2].wait()
        W[3 * b + 1, z, y, x, c] = M[b, 0:block].astype(BF16)
        copies[3].wait()
        W[3 * b + 2, z, y, x, c] = M[b, block:2 * block].astype(BF16)

    own_shards(0)
    pl.semaphore_wait(barrier, len(greeted))

    part_one, part_two = pl.ds(0, half), pl.ds(half, half)
    part_ab = pl.ds(CUT_LOW, CUT_HIGH - CUT_LOW)
    part_a, part_b = pl.ds(CUT_LOW, half - CUT_LOW), pl.ds(half, CUT_HIGH - half)
    part_c, part_d = pl.ds(0, CUT_LOW), pl.ds(CUT_HIGH, d - CUT_HIGH)

    def sides(m, zz):
        return W.at[m, zz, y, :, c, :, part_c], W.at[m, zz, :, x, c, :, part_d]

    def sides_size(m, count):
        return W.at[m, pl.ds(0, count), y, :, c, :, pl.ds(0, CUT_LOW + d - CUT_HIGH)]

    def z_start(m):
        ref = W.at[m, z, y, x, c, :, part_ab]
        for zz in (z1, across):
            send(ref, ref, zs.at[m], zr.at[m, z], to_z(zz))

    def z_pass(m):
        @pl.when(inner)
        def _():
            for zz in (z3, z2):
                ref = W.at[m, zz, y, x, c, :, part_ab]
                got(ref, zr.at[m, zz])
                send(ref, ref, zs.at[m], zr.at[m, zz], to_z(z1))

    def z_rest(m):
        for ref in sides(m, z):
            for zz in (z1, across):
                send(ref, ref, zcs.at[m], zcr.at[m, z], to_z(zz))

    def z_pass_rest(m):
        @pl.when(inner)
        def _():
            for zz in (z3, z2):
                got(sides_size(m, 1), zcr.at[m, zz])
                for ref in sides(m, zz):
                    send(ref, ref, zcs.at[m], zcr.at[m, zz], to_z(z1))

    def arrived(k, ref, sem):
        if k == 1:
            got(ref, sem)
        elif k > 1:
            pl.when(outermost)(lambda: got(ref, sem))

    def g1(m, k):
        zz = flip_by(z, k)
        arrived(k, W.at[m, zz, y, x, c, :, part_ab], zr.at[m, zz])
        t = m * nmp + k
        one = W.at[m, zz, y, x, c, :, part_a if k else part_one]
        two = W.at[m, zz, y, x, c, :, part_b if k else part_two]
        send(one, one, h1s.at[m], h1r.at[t], to_x)
        send(two, two, h1s.at[m], h1r.at[t], to_y)

    def g2(m, k):
        zz = flip_by(z, k)
        t = m * nmp + k
        if k:
            got(W.at[m, zz, oy, ox, c, :, part_ab], h1r.at[t])
        else:
            got(W.at[m, zz, oy, ox, c], h1r.at[t])
        arrived(k, sides_size(m, 1), zcr.at[m, zz])
        one = W.at[m, zz, y, :, c, :, part_one]
        two = W.at[m, zz, :, x, c, :, part_two]
        send(one, one, h2s.at[m], h2r.at[t], to_y)
        send(two, two, h2s.at[m], h2r.at[t], to_x)

    def g3(m, k):
        zz = flip_by(z, k)
        t = m * nmp + k
        got(W.at[m, zz, oy, :, c], h2r.at[t])
        whole = W.at[m, zz, :, :, c]
        send(whole, whole, cs.at[m], cr.at[t], to_c)

    def g4(m, k):
        zz = flip_by(z, k)
        t = m * nmp + k
        got(W.at[m, zz, :, :, oc], cr.at[t])

    def g_done(m):
        for number, which in ((2, outermost), (4, inner)):

            @pl.when(which)
            def _(number=number):
                sent(W.at[m, pl.ds(0, number), y, x, c, :, part_ab], zs.at[m])
                sent(sides_size(m, number), zcs.at[m])

        sent(W.at[m, pl.ds(0, nmp - 1), y, x, c, :, part_ab], h1s.at[m])
        sent(W.at[m, z, y, x, c], h1s.at[m])
        sent(W.at[m, :, y, :, c], h2s.at[m])
        sent(W.at[m, :, :, :, c], cs.at[m])

    total = 6 * nmp

    def advance(t):
        def at(s, stage):
            if 0 <= s < total:
                stage(*ORDER[s])

        at(t - LAG, g2)
        for m in REST_AT.get(t, ()):
            z_rest(m)
        for table, stage in ((Z_AT, z_start), (PASS_AT, z_pass), (PASS_REST_AT, z_pass_rest)):
            for m in table.get(t, ()):
                stage(m)
        at(t, g1)
        at(t - LAG - DEPTH, g3)
        at(t - LAG - DEPTH - 1, g4)

    def here(m, k=None):
        keys = [k] if k is not None else range(nmp)
        return max(ORDER.index((m, key)) for key in keys) + LAG + DEPTH + 1

    back_a, back_b = pl.ds(BACK_LOW, half - BACK_LOW), pl.ds(half, BACK_HIGH - half)
    back_ab = pl.ds(BACK_LOW, BACK_HIGH - BACK_LOW)
    back_c, back_d = pl.ds(0, BACK_LOW), pl.ds(BACK_HIGH, d - BACK_HIGH)

    def release(m):
        g_done(m)
        for device in [to_x, to_y] + [to_z(flip_by(z, key)) for key in range(1, nmp)]:
            pl.semaphore_signal(free.at[m], inc=1, device_id=device, device_id_type=MESH)

    def may_send(m):
        pl.semaphore_wait(free.at[m], nmp + 1)

    def z_first(m, k, ref, dst, s_sem, r_sem):
        @pl.when(jnp.logical_and(k != z, jnp.logical_or(outermost, k == z1)))
        def _():
            slot = jnp.where(k == z1, z, jnp.where(k == z3, k, z1))
            send(ref, dst(slot), s_sem.at[m], r_sem.at[m, slot], to_z(z1))

    def z_second(m, k, ref, dst, s_sem, r_sem):
        @pl.when(jnp.logical_and(inner, jnp.logical_or(k == z2, k == z3)))
        def _():
            slot = jnp.where(k == z2, k, z)
            got(dst(slot), r_sem.at[m, slot])
            add_to(ref, dst(slot))
            send(ref, dst(z), s_sem.at[m], r_sem.at[m, z], to_z(k))

    def chunk_refs(m, k, part):
        return (
            W.at[m, k, y, x, c, :, part],
            lambda slot: W.at[m, slot, oy, ox, oc, :, part],
            zs,
            zr,
        )

    def third_refs(m, k):
        return (
            W.at[m, k, :, x, c, :, back_c],
            lambda slot: W.at[m, slot, :, ox, oc, :, back_c],
            zcs,
            zcr,
        )

    def fourth_refs(m, k):
        return (
            W.at[m, k, y, :, c, :, back_d],
            lambda slot: W.at[m, slot, oy, :, oc, :, back_d],
            zds,
            zdr,
        )

    def r1(m, k):
        t = m * nmp + k
        send(
            W.at[m, k, :, ox, c, :, part_one],
            W.at[m, k, :, ox, oc, :, part_one],
            h2s.at[m],
            h2r.at[t],
            to_x,
        )
        send(
            W.at[m, k, oy, :, c, :, part_two],
            W.at[m, k, oy, :, oc, :, part_two],
            h2s.at[m],
            h2r.at[t],
            to_y,
        )

    def either(m, whole, split):
        if isinstance(m, int):
            (whole if m in NO_THIRD else split)()
            return
        chosen = False
        for one in NO_THIRD:
            chosen = jnp.logical_or(chosen, m == one)
        pl.when(chosen)(whole)
        pl.when(jnp.logical_not(chosen))(split)

    def add_to(dst, src):
        dst[...] = (dst[...].astype(F32) + src[...].astype(F32)).astype(BF16)

    def r2(m, k):
        t = m * nmp + k
        got(W.at[m, k, y, :, oc], h2r.at[t])
        add_to(W.at[m, k, :, x, c, :, part_one], W.at[m, k, :, x, oc, :, part_one])
        add_to(W.at[m, k, y, :, c, :, part_two], W.at[m, k, y, :, oc, :, part_two])

        def second(one, two):
            send(W.at[m, k, oy, x, c, :, one], W.at[m, k, oy, ox, oc, :, one], h1s.at[m], h1r.at[t], to_y)
            send(W.at[m, k, y, ox, c, :, two], W.at[m, k, oy, ox, oc, :, two], h1s.at[m], h1r.at[t], to_x)

        def split():
            second(back_a, back_b)
            z_first(m, k, *third_refs(m, k))
            z_first(m, k, *fourth_refs(m, k))

        either(m, lambda: second(part_one, part_two), split)

    def r3(m, k):
        t = m * nmp + k

        def last(part, one, two):
            got(W.at[m, k, y, x, oc, :, part], h1r.at[t])
            add_to(W.at[m, k, y, x, c, :, one], W.at[m, k, y, ox, oc, :, one])
            add_to(W.at[m, k, y, x, c, :, two], W.at[m, k, oy, x, oc, :, two])
            z_first(m, k, *chunk_refs(m, k, part))

        either(m, lambda: last(pl.ds(0, d), part_one, part_two), lambda: last(back_ab, back_a, back_b))

    def r3_more(m, k):
        def split():
            z_second(m, k, *third_refs(m, k))
            z_second(m, k, *fourth_refs(m, k))
            z_second(m, k, *chunk_refs(m, k, back_ab))

        either(m, lambda: z_second(m, k, *chunk_refs(m, k, pl.ds(0, d))), split)

    def join(m):
        for refs, sem in ((third_refs, zcr), (fourth_refs, zdr)):
            own, slots = refs(m, z)[:2]
            mine = own[...].astype(F32)
            for zz in (z1, across):
                got(slots(zz), sem.at[m, zz])
                mine = mine + slots(zz)[...].astype(F32)
            own[...] = mine.astype(BF16)
        send(W.at[m, z, oy, x, c, :, back_c], XC.at[m, :, pl.ds(0, BACK_LOW)], hcs.at[m], hcr.at[m], to_y)
        send(
            W.at[m, z, y, ox, c, :, back_d],
            XC.at[m, :, pl.ds(BACK_LOW, d - BACK_HIGH)],
            hcs.at[m],
            hcr.at[m],
            to_x,
        )

    def r4(m):
        part = pl.ds(0, d) if m in NO_THIRD else back_ab
        sum_ = W[m, z, y, x, c, :, part].astype(F32)
        for zz in (z1, across):
            src = W.at[m, zz, oy, ox, oc, :, part]
            got(src, zr.at[m, zz])
            sum_ = sum_ + src[...].astype(F32)
        if m not in NO_THIRD:
            got(XC.at[m], hcr.at[m])
            low_part = W[m, z, y, x, c, :, back_c].astype(F32) + XC[m, :, 0:BACK_LOW].astype(F32)
            high_part = W[m, z, y, x, c, :, back_d].astype(F32) + XC[m, :, BACK_LOW:].astype(F32)
            sum_ = jnp.concatenate([low_part, sum_, high_part], axis=1)
        b, j = m // 3, m % 3
        if j == 0:
            WI[b, 0] = sum_[:, 0:third]
            WI[b, 2] = sum_[:, third:2 * third]
            WI[b, 1] = sum_[:, 2 * third:3 * third]
            WO[b] = sum_[:, 3 * third:].T
            result_copy(b, 0).start()
            result_copy(b, 1).start()
        else:
            M[b, (j - 1) * block:j * block] = sum_
            result_copy(b, j + 1).start()

    def result_copy(b, i):
        src = (WI.at[b], WO.at[b], M.at[b, pl.ds(0, block)], M.at[b, pl.ds(block, block)])[i]
        return keep(src, grads_out[b][i], 4 * b + i)

    def r_done(m):
        part = pl.ds(0, d) if m in NO_THIRD else back_ab
        sent(W.at[m, pl.ds(0, nmp - 1), y, x, c, :, part], zs.at[m])
        sent(W.at[m, :, y, x, c, :, part], h1s.at[m])
        sent(W.at[m, :, y, :, c], h2s.at[m])
        if m not in NO_THIRD:
            sent(W.at[m, pl.ds(0, nmp - 1), y, :, c, :, back_c], zcs.at[m])
            sent(W.at[m, pl.ds(0, nmp - 1), y, :, c, :, back_d], zds.at[m])
            sent(XC.at[m], hcs.at[m])

    def chunk(k):
        key, out, weight = nmp - 1 - k, 0, 1
        key = jnp.where(jnp.logical_and(inner, key > 1), 5 - key, key)
        while weight < nmp:
            out = out + weight * ((z // weight + key // weight) % 2)
            weight *= 2
        return out

    def join_any(m, k):
        if isinstance(m, int):
            if m not in NO_THIRD:
                join(m)
        else:
            either(m, lambda: None, lambda: join(m))

    def retreat(u):
        def at(s, stage):
            stage(5 - s // nmp, chunk(s % nmp))

        if isinstance(u, int):
            for v in TAIL_TWO[u]:
                at(v, r2)
            if u < total:
                at(u, r1)
            for v in TAIL_THREE[u]:
                at(v, r3)
            for v in TAIL_FOUR[u]:
                at(v, r3_more)
            for v in TAIL_JOIN[u]:
                at(v, join_any)
            return
        early = u < total - nmp
        pl.when(early)(lambda: at(u, r1))
        pl.when(jnp.logical_and(u >= LAG_TWO, early))(lambda: at(u - LAG_TWO, r2))
        pl.when(jnp.logical_and(u >= LAG_THREE, early))(lambda: at(u - LAG_THREE, r3))
        pl.when(jnp.logical_and(u >= LAG_FOUR, early))(lambda: at(u - LAG_FOUR, r3_more))
        own = (u - LAG_JOIN) % nmp == nmp - 1
        pl.when(jnp.logical_and(jnp.logical_and(u >= LAG_JOIN, own), early))(lambda: at(u - LAG_JOIN, join_any))
        for v in range(total - nmp, total):
            pl.when(u == v)(functools.partial(retreat, v))

    def swap_start(i):
        RB[i, pl.ds(me, 1)] = SB[i, pl.ds(me, 1)]
        for key in range(1, members):
            f = flip_by(me, key)
            send(SB.at[i, f], RB.at[i, me], ts.at[i], tr.at[i], to_member(f))

    def swap_wait(i):
        got(RB.at[i, pl.ds(0, members - 1)], tr.at[i])

    def swap_done(i):
        sent(SB.at[i, pl.ds(0, members - 1)], ts.at[i])

    def rows_of(ref, i):
        return ref[i].reshape(rows, d)

    for key in range(1, nmp):
        ref = SG.at[z, y, x, c]
        send(ref, ref, vs.at[0], vr.at[0], to_z(flip_by(z, key)))
    z_start(0)
    advance(0)
    advance(1)
    own_shards(1)
    got(SG.at[pl.ds(0, nmp - 1), y, x, c], vr.at[0])
    ref = SG.at[:, y, x, c]
    send(ref, ref, vs.at[1], vr.at[1], to_x)
    for copy in [*loads[-3:], loads[0]]:
        copy.wait()
    swap = swap_ref[...]
    keep(x_ref, ACC, 8).wait()
    H[0] = exact(swap.astype(F32), ACC[...], ((1,), (0,)))
    advance(2)
    got(SG.at[:, y, ox, c], vr.at[1])
    ref = SG.at[:, y, :, c]
    send(ref, ref, vs.at[2], vr.at[2], to_y)
    advance(3)
    got(SG.at[:, oy, :, c], vr.at[2])
    ref = SG.at[:, :, :, c]
    send(ref, ref, vs.at[3], vr.at[3], to_c)
    advance(4)
    got(SG.at[:, :, :, oc], vr.at[3])

    lane = lax.broadcasted_iota(jnp.int32, (1, d), 1)
    tall = SG[...].reshape(nmp * per * 16, 128)
    spread = mm(tall, tiles_ref[0]).reshape(nmp * per, 16, d)
    spread = jnp.sum(spread * mask_ref[0:nmp * per].reshape(nmp * per, 1, d), axis=0)
    SV[0, 0:6] = spread[0:6]
    SV[1, 0:6] = spread[6:12]
    is_q = (lane < third).astype(F32)
    is_v = jnp.logical_and(lane >= third, lane < 2 * third).astype(F32)
    spread_in = mm(tall, tiles_ref[1]).reshape(nmp, per, 16, d)
    spread_up = mm(tall, tiles_ref[2]).reshape(nmp, per, 16, d)
    mask_in = mask_ref[nmp * per:nmp * per + per].reshape(per, 1, d)
    mask_up = mask_ref[nmp * per + per:nmp * per + 2 * per].reshape(per, 1, d)
    for k in range(nmp):
        one = jnp.sum(spread_in[k] * mask_in, axis=0)
        two = jnp.sum(spread_up[k] * mask_up, axis=0)
        for b in range(2):
            BI[b, k] = one[12 + 2 * b:13 + 2 * b] * is_q + one[13 + 2 * b:14 + 2 * b] * is_v
            BU[b, k] = two[b:b + 1]
    for t in range(5, here(0) + 1):
        advance(t)

    lane2 = lax.broadcasted_iota(jnp.int32, (1, 256), 1)
    heads = third // HEAD

    def head_mask(lead):
        return jnp.logical_and(lane2 >= lead * HEAD, lane2 < lead * HEAD + HEAD).astype(F32).astype(BF16)

    q_masks = [head_mask(h) for h in range(heads)]
    v_masks = [head_mask(h + 1) for h in range(heads)]
    scale = HEAD ** (-0.5)
    wide = 5 * 128

    def flat(values):
        return values.reshape(d, values.shape[-1])

    def lower(values):
        return values.reshape(half, values.shape[-1])

    def tall_view(values):
        return values.T.astype(BF16).reshape(2, 2, 2, d // per, rows)

    def to_sibling(src, dst, n):
        send(src, dst, ss.at[n], sr.at[n], to_c)

    def norm_to_sibling(b, i):
        to_sibling(NT.at[b, i, :, :, oc], LS.at[i], 1 + i)

    def early_to_sibling(b):
        to_sibling(HID.at[b], HS, 0)
        for i in range(2):
            norm_to_sibling(b, i)
        to_sibling(CT.at[b], CS, 3)

    def take_grad(b):
        grad = GR[...]
        SGR[pl.ds(16 * b + 5, 1)] = jnp.sum(grad, axis=0, keepdims=True)
        NB[...] = grad.astype(BF16)
        GT[0] = tall_view(grad)
        to_sibling(GT.at[0, :, :, oc], LS.at[2], 4)

    def shrink(b, k):
        hidden_grad = mm(NB[...], flat(W[3 * b + 2, k]))
        upper_grad = (GP[b, k].astype(F32) * hidden_grad).astype(BF16)
        GP[b, k] = upper_grad
        to_sibling(GP.at[b, k], US.at[k], 6)
        SGR[pl.ds(16 * b + 10 + k, 1)] = jnp.sum(upper_grad.astype(F32), axis=0, keepdims=True)

    def forward(b, _):
        m = 3 * b
        ends = [(here(3 * i), here(3 * i + 1), here(3 * i + 2)) for i in range(2)]
        done = [here(0), here(3)]

        def turn(upto):
            for i in range(2):
                steps_ = range(done[i] + 1, upto[i] + 1)
                done[i] = max(done[i], upto[i])
                if len(steps_):
                    pl.when(b == i)(lambda steps_=steps_: [advance(t) for t in steps_] and None)

        def one_of(i):
            return [min(done[0] + 1, ends[0][i]), min(done[1] + 1, ends[1][i])]

        @pl.when(b == 1)
        def _():
            swap_wait(1)
            H[1] = rows_of(RB, 1).astype(F32)

        @pl.when(b == 0)
        def _():
            keep(ct_ref, GR, 9).wait()
            picked = (swap.astype(F32) * bits_ref[...].astype(F32)).astype(BF16)
            SB[0] = mm(picked, GR[...].astype(BF16)).astype(BF16).reshape(members, rows // members, d)
            swap_start(0)

        h = H[b]
        unit, _s = unit_rows(h)
        normed = unit * SV[b, 0:1] + SV[b, 1:2]
        NB[...] = normed.astype(BF16)
        NT[b, 0] = tall_view(normed)
        pl.when(b == 1)(lambda: norm_to_sibling(1, 0))
        ACC[...] = h + SV[b, 2:3]

        def attend(k):
            packed = (mm(NB[...], flat(W[m, k, :, :, :, :, 0:wide])) + BI[b, k, :, 0:wide]).astype(BF16)
            PK[b, k] = packed
            qs = packed[:, 0:256] * BF16(scale)
            vv = packed[:, 128:384]
            kk = packed[:, 384:640]
            mixed = jnp.zeros((rows, 256), F32)
            for h in range(heads):
                scores = mm_t(qs * q_masks[h], kk)
                expo = jnp.exp(scores - jnp.max(scores, axis=-1, keepdims=True))
                probs = (expo * (1.0 / jnp.sum(expo, axis=-1, keepdims=True))).astype(BF16)
                PR[b, k, h] = probs
                mixed += mm(probs, vv * v_masks[h])
            mixed = mixed.astype(BF16)
            CT[b, k] = mixed
            pl.when(b == 1)(lambda: to_sibling(CT.at[1, k], CS.at[k], 3))
            ACC[...] += mm_t(mixed, flat(W[m, k, :, :, :, :, d - 256:d]))

        for k in range(nmp):
            attend(k)
            if k % 2 == 1 and k < 4:
                turn(one_of(1))
        middle = ACC[...]
        M[b] = middle
        unit, _s = unit_rows(middle)
        normed = unit * SV[b, 3:4] + SV[b, 4:5]
        NB[...] = normed.astype(BF16)
        NT[b, 1] = tall_view(normed)
        pl.when(b == 1)(lambda: norm_to_sibling(1, 1))
        ACC[...] = middle + SV[b, 5:6]

        turn([ends[0][1], ends[1][1]])

        def expand(k):
            upper = mm(NB[...], flat(W[m + 1, k])) + BU[b, k]
            cdf = 0.5 + 0.5 * lax.erf(upper * (0.5 ** 0.5))
            HID[b, k] = (upper * cdf).astype(BF16)
            density = jnp.exp(-0.5 * upper * upper) * ((2 * np.pi) ** -0.5)
            GP[b, k] = (cdf + upper * density).astype(BF16)
            pl.when(b == 1)(lambda: to_sibling(HID.at[1, k], HS.at[k], 0))

        def contract(k):
            pl.when(b == 1)(lambda: shrink(1, k))
            ACC[...] += mm_t(HID[b, k], flat(W[m + 2, k]))

        for k in range(nmp):
            expand(k)
            if k == 1:
                turn(one_of(2))

        @pl.when(b == 1)
        def _():
            swap_wait(0)
            GR[...] = rows_of(RB, 0).astype(F32)
            take_grad(1)

        contract(z)
        for k in range(1, nmp):
            turn([here(2, k), here(5, k)])
            contract(flip_by(z, k))
        SB[1 + b] = ACC[...].astype(BF16).reshape(members, rows // members, d)
        pl.when(b == 0)(lambda: swap_start(1))
        turn([here(3), done[1]])
        return 0

    lax.fori_loop(0, 2, forward, 0)

    def norm_back(grad, start, gain):
        unit, scale = unit_rows(start)
        lifted = grad * gain
        back = scale * (
            lifted
            - jnp.mean(lifted, axis=-1, keepdims=True)
            - unit * jnp.mean(lifted * unit, axis=-1, keepdims=True)
        )
        return back, jnp.sum(grad * unit, axis=0, keepdims=True), jnp.sum(grad, axis=0, keepdims=True)

    def deal():
        rows_ = []
        for zz in range(nmp):
            own = mask_ref[zz * per:zz * per + per].reshape(per, 1, d)
            plain = jnp.concatenate([SGR[0:6], SGR[16:22]], axis=0).reshape(1, 12, d) * own
            pair = jnp.concatenate([SGR[6 + zz:7 + zz], SGR[22 + zz:23 + zz]], axis=0).reshape(1, 2, d) * mask_in
            up = jnp.concatenate([SGR[10 + zz:11 + zz], SGR[26 + zz:27 + zz]], axis=0).reshape(1, 2, d) * mask_up
            rows_ = jnp.concatenate([plain, pair, up], axis=1).reshape(per * 16, d)
            high = rows_.astype(BF16)
            rest = (rows_ - high.astype(F32)).astype(BF16)
            line = lax.broadcasted_iota(jnp.int32, (per, 16, 128), 1)
            parts = [
                (mm_t(high, tiles_ref[i]) + mm_t(rest, tiles_ref[i])).reshape(per, 16, 128) for i in (0, 3, 2)
            ]
            XS[zz] = jnp.where(line < 12, parts[0], jnp.where(line < 14, parts[1], parts[2]))
        for key in range(1, nmp * per):
            qq, zz = peer(key)
            send(XS.at[zz, qq], XR.at[key], rs.at[0], rr.at[0], to_peer(key))

    def backward(step, _):
        b = 1 - step
        m = 3 * b
        row = 16 * b

        @pl.when(step == 1)
        def _():
            pl.semaphore_wait(free_c, 1)
            early_to_sibling(b)
            take_grad(b)

            def shrink_all(k, _):
                shrink(b, k)
                return 0

            lax.fori_loop(0, nmp, shrink_all, 0)

        release(m + 2)
        got(HS, sr.at[0])
        got(LS.at[2], sr.at[4])
        may_send(m + 2)

        def down_grad(step_k, _):
            k = chunk(step_k)
            own = mm(lower(GT[0, :, :, c]), HID[b, k]) + mm(lower(LS[2]), HS[k])
            W[m + 2, k, :, :, c] = own.astype(BF16).reshape(2, 2, d // per, d)
            retreat(3 * nmp * step + step_k)
            return 0

        lax.fori_loop(0, nmp, down_grad, 0)
        pl.when(step == 1)(lambda: swap_start(2))
        ACC[...] = jnp.zeros_like(ACC)

        def spread_up(k, _):
            ACC[...] += mm_t(GP[b, k], flat(W[m + 1, k]))
            return 0

        lax.fori_loop(0, nmp, spread_up, 0)
        release(m + 1)
        got(US, sr.at[6])
        got(LS.at[1], sr.at[2])
        may_send(m + 1)

        def up_grad(step_k, _):
            k = chunk(step_k)
            own = mm(lower(NT[b, 1, :, :, c]), GP[b, k]) + mm(lower(LS[1]), US[k])
            W[m + 1, k, :, :, c] = own.astype(BF16).reshape(2, 2, d // per, d)
            retreat(3 * nmp * step + nmp + step_k)
            return 0

        lax.fori_loop(0, nmp, up_grad, 0)
        pl.when(step == 1)(lambda: r4(5))
        back, gain_grad, bias_grad = norm_back(ACC[...], M[b], SV[b, 3:4])
        SGR[pl.ds(row + 3, 1)] = gain_grad
        SGR[pl.ds(row + 4, 1)] = bias_grad
        middle_grad = GR[...] + back
        GR[...] = middle_grad
        SGR[pl.ds(row + 2, 1)] = jnp.sum(middle_grad, axis=0, keepdims=True)
        NB[...] = middle_grad.astype(BF16)
        GT[1] = tall_view(middle_grad)
        to_sibling(GT.at[1, :, :, oc], LS.at[3], 5)
        ACC[...] = jnp.zeros_like(ACC)
        def attend_back(k, _):
            mixed_grad = mm(NB[...], flat(W[m, k, :, :, :, :, d - 256:d])).astype(BF16)
            packed = PK[b, k]
            qs = packed[:, 0:256] * BF16(scale)
            vv = packed[:, 128:384]
            kk = packed[:, 384:640]
            q_grad = jnp.zeros((rows, 256), F32)
            k_grad = jnp.zeros((rows, 256), F32)
            v_grad = jnp.zeros((rows, 256), F32)
            for h in range(heads):
                part = mixed_grad * v_masks[h]
                probs_low = PR[b, k, h]
                probs = probs_low.astype(F32)
                weighted = probs * mm_t(part, vv)
                score_grad = (weighted - probs * jnp.sum(weighted, axis=-1, keepdims=True)).astype(BF16)
                q_grad += mm(score_grad, kk * q_masks[h])
                k_grad += t_mm(score_grad, qs * q_masks[h])
                v_grad += t_mm(probs_low, part)
            q_grad = q_grad * scale
            packed_grad = jnp.concatenate(
                [q_grad[:, 0:128], q_grad[:, 128:256] + v_grad[:, 0:128], v_grad[:, 128:256], k_grad], axis=1
            ).astype(BF16)
            PK[b, k] = packed_grad
            to_sibling(PK.at[b, k], PS.at[k], 7)
            SGR[pl.ds(row + 6 + k, 1), 0:wide] = jnp.sum(packed_grad.astype(F32), axis=0, keepdims=True)
            ACC[...] += mm_t(packed_grad, flat(W[m, k, :, :, :, :, 0:wide]))
            return 0

        lax.fori_loop(0, nmp, attend_back, 0)
        release(m)
        back, gain_grad, bias_grad = norm_back(ACC[...], H[b], SV[b, 0:1])
        SGR[pl.ds(row, 1)] = gain_grad
        SGR[pl.ds(row + 1, 1)] = bias_grad
        GR[...] = GR[...] + back

        @pl.when(step == 0)
        def _():
            SB[3] = GR[...].astype(BF16).reshape(members, rows // members, d)
            swap_start(3)

        pl.when(step == 1)(deal)
        got(PS, sr.at[7])
        got(LS.at[0], sr.at[1])
        got(LS.at[3], sr.at[5])
        got(CS, sr.at[3])
        may_send(m)

        def in_grad(step_k, _):
            k = chunk(step_k)
            one = mm(lower(NT[b, 0, :, :, c]), PK[b, k]) + mm(lower(LS[0]), PS[k])
            two = mm(lower(GT[1, :, :, c]), CT[b, k]) + mm(lower(LS[3]), CS[k])
            own = jnp.concatenate(
                [one[:, 0:512], one[:, 512:640] + two[:, 0:128], two[:, 128:256]], axis=1
            ).astype(BF16)
            W[m, k, :, :, c] = own.reshape(2, 2, d // per, d)
            retreat(3 * nmp * step + 2 * nmp + step_k)
            return 0

        lax.fori_loop(0, nmp, in_grad, 0)

        sent(HID.at[b], ss.at[0])
        sent(NT.at[b, 0, :, :, oc], ss.at[1])
        sent(NT.at[b, 1, :, :, oc], ss.at[2])
        sent(CT.at[b], ss.at[3])
        sent(GT.at[0, :, :, oc], ss.at[4])
        sent(GT.at[1, :, :, oc], ss.at[5])
        sent(GP.at[b], ss.at[6])
        sent(PK.at[b], ss.at[7])

        @pl.when(step == 0)
        def _():
            pl.semaphore_signal(free_c, inc=1, device_id=to_c, device_id_type=MESH)

        pl.when(step == 1)(lambda: r4(4))

        @pl.when(step == 0)
        def _():
            swap_wait(3)
            GR[...] = rows_of(RB, 3).astype(F32)
        return 0

    lax.fori_loop(0, 2, backward, 0)

    ACC[...] = exact(swap.astype(F32), GR[...], ((1,), (0,)))
    keep(ACC, ig_ref, 9).start()
    swap_wait(2)
    H[1] = mm(swap, rows_of(RB, 2))
    keep(H.at[1], out_ref, 8).start()
    for u in sorted(TAIL_TWO):
        if u >= total:
            retreat(u)
    r4(3)
    r4(2)
    got(XR.at[pl.ds(1, nmp * per - 1)], rr.at[0])
    sg_ref[...] = XS[z, q] + jnp.sum(XR[1:nmp * per], axis=0)
    r4(1)
    r4(0)
    sent(XR.at[pl.ds(1, nmp * per - 1)], rs.at[0])
    for b in range(2):
        for i in range(4):
            result_copy(b, i).wait()
    keep(H.at[1], out_ref, 8).wait()
    keep(ACC, ig_ref, 9).wait()
    for m in range(6):
        r_done(m)
    for i in range(4):
        swap_done(i)
    sent(SG.at[pl.ds(0, nmp - 1), y, x, c], vs.at[0])
    sent(SG.at[:, y, x, c], vs.at[1])
    sent(SG.at[:, y, :, c], vs.at[2])
    sent(SG.at[:, :, :, c], vs.at[3])


def tables(outer, ndp, nmp, d):
    n = d // (ndp * nmp)
    tiles = np.zeros((4, 128, d), np.float32)
    masks = np.zeros((nmp * INNER + 2 * INNER, d), np.float32)
    for at in range(d):
        i = at % n
        zz = (at // n) % nmp
        pp = at // (n * nmp)
        qq, lo = pp // outer, pp % outer
        tiles[0, lo * n + i, at] = 1
        masks[zz * INNER + qq, at] = 1
    third = d // nmp
    step = third // INNER
    for at in range(2 * third):
        tiles[1, at % step, at] = 1
        tiles[3, at % step + 32 * (at // third), at] = 1
        masks[nmp * INNER + (at % third) // step, at] = 1
    step = d // INNER
    for at in range(d):
        tiles[2, 32 + at % step, at] = 1
        masks[nmp * INNER + INNER + at // step, at] = 1
    return tiles, masks


def turn_table():
    swap = np.zeros((FRAME, FRAME), np.float32)
    across = SIDE // TUBE
    for wr in range(across):
        for i in range(TUBE):
            for wc in range(across):
                for j in range(TUBE):
                    natural = ((wr * TUBE + i) * across + wc) * TUBE + j
                    turned = ((wr * across + wc) * TUBE + i) * TUBE + j
                    swap[turned, natural] = 1
    return swap


def fused(sizes, x, cotangent, bits, matrices, vectors, ndp):
    outer, nmp, d, rows = sizes
    tiles, masks = tables(outer, ndp, nmp, d)
    members = CLIP // FRAME
    vmem = pltpu.VMEM
    dma = pltpu.SemaphoreType.DMA
    regular = pltpu.SemaphoreType.REGULAR
    block = d // INNER
    steps = 6 * nmp
    scratch = [
        vmem((6, nmp, 2, 2, 2, block, d), BF16),
        vmem((nmp, 2, 2, 2, 16, 128), BF16),
        vmem((2, 8, d), F32),
        vmem((2, nmp, 1, d), F32),
        vmem((2, nmp, 1, d), F32),
        vmem((2, rows, d), F32),
        vmem((2, rows, d), F32),
        vmem((rows, d), BF16),
        vmem((2, 2, 2, 2, 2, block, rows), BF16),
        vmem((2, 2, 2, 2, block, rows), BF16),
        vmem((2, nmp, rows, 640), BF16),
        vmem((2, nmp, rows, 256), BF16),
        vmem((2, nmp, rows, d), BF16),
        vmem((2, nmp, rows, d), BF16),
        vmem((2, nmp, d // nmp // HEAD, rows, rows), BF16),
        vmem((rows, d), F32),
        vmem((rows, d), F32),
        vmem((32, d), F32),
        vmem((nmp, INNER, 16, 128), F32),
        vmem((nmp * INNER, 16, 128), F32),
        vmem((4, members, rows // members, d), BF16),
        vmem((4, members, rows // members, d), BF16),
        vmem((nmp, rows, d), BF16),
        vmem((nmp, rows, 256), BF16),
        vmem((nmp, rows, d), BF16),
        vmem((nmp, rows, 640), BF16),
        vmem((4, 2, 2, block, rows), BF16),
        dma((6,)),
        dma((6, nmp)),
        dma((6,)),
        dma((6, nmp)),
        dma((6,)),
        dma((6, nmp)),
        dma((6,)),
        dma((6,)),
        dma((6,)),
        dma((steps,)),
        dma((6,)),
        dma((steps,)),
        dma((6,)),
        dma((steps,)),
        dma((4,)),
        dma((4,)),
        dma((4,)),
        dma((4,)),
        dma((8,)),
        dma((8,)),
        dma((1,)),
        dma((1,)),
        regular((6,)),
        regular,
        vmem((2, 3, block, d // nmp), F32),
        vmem((2, d // nmp, block), F32),
        vmem((16, 128), F32),
        vmem((6, block, d - BACK_HIGH + BACK_LOW), BF16),
        dma((10,)),
        vmem(bits.shape, bits.dtype),
        *(vmem(v.shape, v.dtype) for v in vectors),
        vmem((FRAME, FRAME), BF16),
        vmem(tiles.shape, BF16),
        vmem(masks.shape, F32),
        dma((4 + len(vectors),)),
    ]
    grads = [
        jax.ShapeDtypeStruct((3, block, d // nmp), F32),
        jax.ShapeDtypeStruct((d // nmp, block), F32),
        jax.ShapeDtypeStruct((block, d), F32),
        jax.ShapeDtypeStruct((block, d), F32),
    ]
    whole = jax.ShapeDtypeStruct((rows, d), F32)
    anywhere = pl.BlockSpec(memory_space=pl.ANY)
    inside = pl.BlockSpec(memory_space=vmem)
    return pl.pallas_call(
        functools.partial(kernel, sizes, len(vectors)),
        out_shape=[whole, whole] + grads + grads + [jax.ShapeDtypeStruct((16, 128), F32)],
        in_specs=[anywhere] * (14 + len(vectors)),
        out_specs=[anywhere] * 10 + [inside],
        scratch_shapes=scratch,
        compiler_params=pltpu.CompilerParams(
            collective_id=0, has_side_effects=True, vmem_limit_bytes=64 << 20
        ),
        name="two_blocks",
    )(
        x,
        cotangent,
        bits,
        *matrices,
        *vectors,
        jnp.asarray(turn_table(), BF16),
        jnp.asarray(tiles, BF16),
        jnp.asarray(masks, F32),
    )


def settle_kernel(wide, *refs):
    big, sg_in, outs = refs[:10], refs[10], refs[11:37]
    held, sg_ref, sems = refs[37:47], refs[47], refs[48]
    small_copy = pltpu.make_async_copy(sg_in, sg_ref, sems.at[0, 10])
    small_copy.start()
    copies = []
    for i in range(10):
        copies.append(
            (
                pltpu.make_async_copy(big[i], held[i], sems.at[0, i]),
                pltpu.make_async_copy(held[i], outs[i], sems.at[1, i]),
            )
        )
        copies[i][0].start()
    small_copy.wait()
    for b in range(2):
        small = outs[10 + 8 * b:18 + 8 * b]
        for i in range(6):
            small[i][...] = sg_ref[6 * b + i:6 * b + i + 1, 0:wide]
        small[6][0:1] = sg_ref[12 + b:13 + b, 0:wide]
        small[6][1:2] = sg_ref[12 + b:13 + b, 32:32 + wide]
        small[7][...] = sg_ref[14 + b:15 + b, 32:32 + 4 * wide]
    for arrive, leave in copies:
        arrive.wait()
        leave.start()
    for _, leave in copies:
        leave.wait()


def settle(big, sg, wide, ups):
    anywhere = pl.BlockSpec(memory_space=pl.ANY)
    inside = pl.BlockSpec(memory_space=pltpu.VMEM)
    row = jax.ShapeDtypeStruct((1, wide), F32)
    small = [row] * 6 + [jax.ShapeDtypeStruct((2, wide), F32), jax.ShapeDtypeStruct((1, ups), F32)]
    outs = pl.pallas_call(
        functools.partial(settle_kernel, wide),
        out_shape=[jax.ShapeDtypeStruct(v.shape, v.dtype) for v in big] + small + small,
        in_specs=[anywhere] * 11,
        out_specs=[anywhere] * 10 + [inside] * 16,
        scratch_shapes=[pltpu.VMEM(v.shape, v.dtype) for v in (*big, sg)]
        + [pltpu.SemaphoreType.DMA((2, 11))],
        name="settle",
    )(*big, sg)
    return outs[:10], (outs[10:18], outs[18:26])


def shards_of(ndp, nmp, inputs, cotangent, mask_bits, *params):
    frame, tube = params[:12], params[12:]
    d = inputs.shape[1]
    rows = inputs.shape[0]
    outer = ndp // INNER
    groups = [[qq * outer + lo for lo in range(outer)] for qq in range(INNER)]

    def joined(values, axis):
        if outer == 1:
            return values
        return lax.all_gather(values, "dp", axis=axis, tiled=True, axis_index_groups=groups)

    matrices = []
    vectors = []
    for block in (frame, tube):
        matrices += [
            joined(block[2].transpose(1, 0, 2), 1),
            joined(block[4], 1),
            joined(block[8], 0),
            joined(block[10].T, 0),
        ]
        vectors += [joined(block[i][None], 1) for i in (0, 1, 5, 6, 7, 11)]
    vectors += [joined(block[3], 1) for block in (frame, tube)]
    vectors += [joined(block[9][None], 1) for block in (frame, tube)]
    wide, ups = vectors[0].shape[1], vectors[-1].shape[1]
    outs = fused((outer, nmp, d, rows), inputs, cotangent, mask_bits[None], matrices, vectors, ndp)
    big, sg = list(outs[:10]), outs[10]
    if outer == 1:
        big, small = settle(big, sg, wide, ups)
    else:
        low = lax.axis_index("dp") % outer
        sg = lax.psum(sg, "dp", axis_index_groups=groups)

        def piece(values, start, size):
            size = size // outer
            return lax.dynamic_slice_in_dim(values, start + low * size, size, 1)

        small = []
        for b in range(2):
            parts = [piece(sg[6 * b + i:6 * b + i + 1], 0, wide) for i in range(6)]
            pair = sg[12 + b, 0:64].reshape(2, 32)
            small.append(parts + [piece(pair, 0, wide), piece(sg[14 + b:15 + b], 32, ups)])
            for i, axis in enumerate((1, 1, 0, 0)):
                at = 2 + 4 * b + i
                big[at] = lax.psum_scatter(
                    big[at], "dp", scatter_dimension=axis, tiled=True, axis_index_groups=groups
                )
    results = []
    for b in range(2):
        inw, outw, up, down = big[2 + 4 * b:6 + 4 * b]
        rows_ = small[b]
        results += [
            rows_[0].reshape(-1),
            rows_[1].reshape(-1),
            inw.transpose(1, 0, 2),
            rows_[6],
            outw,
            rows_[2].reshape(-1),
            rows_[3].reshape(-1),
            rows_[4].reshape(-1),
            up,
            rows_[7].reshape(-1),
            down.T,
            rows_[5].reshape(-1),
        ]
    return (big[0], big[1]) + tuple(results)


def solution(mesh):
    rows = P(("dp", "mp"), None)
    small = P(("dp", "mp"))
    block = (
        small,
        small,
        P("dp", None, "mp"),
        P(None, ("mp", "dp")),
        P("mp", "dp"),
        small,
        small,
        small,
        P("dp", "mp"),
        P(("mp", "dp")),
        P("mp", "dp"),
        small,
    )
    return jax.shard_map(
        functools.partial(shards_of, mesh.shape["dp"], mesh.shape["mp"]),
        mesh=mesh,
        in_specs=(rows, rows, small) + block + block,
        out_specs=(rows, rows) + block + block,
        check_vma=False,
    )
```
